32 devices in a mesh: dp: 4 (over x, core), seq: 8 (over z, y).
Axes of the slice: x: 2, y: 2, z: 4, core: 2. Of those that a mesh axis runs over, the one named last changes fastest.
Arguments:
- bases: int32 [4, 32768], P('dp', 'seq'), may hold values from 0 to 3
- stem_table: bfloat16 [15, 4, 768], replicated, may hold values from -1.5 to 1.5
- conv_weight: bfloat16 [768, 3840], P('seq'), may hold values from -0.09375 to 0.09375
- query_weight: bfloat16 [768, 128], replicated, may hold values from -0.21875 to 0.21875
- key_weight: bfloat16 [768, 128], replicated, may hold values from -0.21875 to 0.21875
- pair_grad: float32 [4, 16, 16], P('dp', 'seq'), may hold values from -6 to 6
Outputs:
- conv_grad: float32 [768, 3840], P('seq')
- query_grad: float32 [768, 128], P('seq')
- key_grad: float32 [768, 128], P('seq')
The draws below stay inside these ranges and needn't reach their ends.
Inputs may be any that keep to these rules, and one draw needn't show every extreme that they name: `bases`: 0, 1, 2, 3 stand for A, C, G, T.
All inputs are finite; a program needn't handle non-finite values.
Results may differ from the reference program's by a relative error of at most 0.0084.
Values may be sent and summed in bfloat16 or wider, within the bound.
No kernel may reach another device: no remote copies, remote signals or barrier semaphores. Data moves between devices by JAX's collectives and lax.ppermute only.
A program may use at most 128 MiB of HBM per device.

```python
import jax
import jax.numpy as jnp
from jax import lax

C0 = 768
C1 = 768
PC = 128
K0 = 15
K1 = 5
POOL = 8
BIN = 2048
BASE_DEV = 4096
NB = 32768
NPOS = 16
SEQS = 4
N_SEQ = 8


def place_ends(drawn, own_key, least, top_value):
    place = [jax.random.randint(jax.random.fold_in(own_key, axis), (), 0, length) for axis, length in enumerate(drawn.shape)]
    longest = drawn.shape.index(max(drawn.shape))
    next_to = place[:longest] + [(place[longest] + 1) % drawn.shape[longest]] + place[longest + 1:]
    return drawn.at[tuple(place)].set(least).at[tuple(next_to)].set(top_value)


def levels(own_key, shape, pieces, smallest, high):
    factor_of = 1.0
    for dim, blocks in pieces:
        draws = jax.random.uniform(jax.random.fold_in(jax.random.fold_in(own_key, 6), dim), (blocks,), jnp.float32, smallest / len(pieces), high / len(pieces))
        factor_of = factor_of * jnp.repeat(jnp.exp(draws), shape[dim] // blocks).reshape((-1,) + (1,) * (len(shape) - 1 - dim))
    return factor_of


def gaussian(rng, shape, width, most, pieces=(), kind=jnp.bfloat16):
    factor_of = levels(rng, shape, pieces, -0.22, 0.18) if pieces else 1.0
    entries = jax.random.normal(rng, shape, jnp.float32) * width * factor_of
    return jnp.minimum(jnp.maximum(entries, -most), most).astype(kind)


def setup_inputs(seed: int = 0) -> dict:
    streams_of = jax.random.split(jax.random.key(seed), 7)
    bases = place_ends(jax.random.randint(streams_of[0], (SEQS, NB), 0, 4), jax.random.fold_in(streams_of[0], 1), 0, 3).astype(jnp.int32)
    stem_table = gaussian(streams_of[1], (K0, 4, C0), K0 ** -0.5, 1.5)
    conv_weight = gaussian(streams_of[2], (C1, K1 * C0), (K1 * C0) ** -0.5, 0.09375, ((0, 8),))
    query_weight = gaussian(streams_of[3], (C1, PC), C1 ** -0.5, 0.21875)
    key_weight = gaussian(streams_of[4], (C1, PC), C1 ** -0.5, 0.21875)
    pair_grad = gaussian(streams_of[5], (SEQS, NPOS, NPOS), 1.0, 6.0, ((0, 4), (1, 8)), jnp.float32)
    return dict(bases=bases, stem_table=stem_table, conv_weight=conv_weight, query_weight=query_weight, key_weight=key_weight, pair_grad=pair_grad)


root_coeff = 0.7978845608028654


def gelu_slope(value):
    tangent = jnp.tanh(root_coeff * (value + 0.044715 * value * value * value))
    return 0.5 * (1.0 + tangent) + 0.5 * value * (1.0 - tangent * tangent) * root_coeff * (1.0 + 3.0 * 0.044715 * value * value)


def reference(bases, stem_table, conv_weight, query_weight, key_weight, pair_grad):
    scale = PC ** -0.5
    wq_f = query_weight.astype(jnp.float32)
    wk_f = key_weight.astype(jnp.float32)
    high = lax.Precision.HIGHEST

    def one_sequence(carry, inputs):
        acc_conv, acc_query, acc_key = carry
        seq_bases, grad_map = inputs
        length = seq_bases.shape[0]
        padded = jnp.pad(seq_bases + 1, (K0 // 2, K0 // 2))
        taps = jnp.stack([padded[t:t + length] for t in range(K0)], axis=1)
        onehot = (taps[:, :, None] == jnp.arange(1, 5, dtype=jnp.int32)).astype(jnp.bfloat16).reshape(length, K0 * 4)
        stem = jnp.dot(onehot, stem_table.reshape(K0 * 4, C0), preferred_element_type=jnp.float32)
        pooled = jax.nn.gelu(stem).reshape(-1, POOL, C0).max(axis=1).astype(jnp.bfloat16)
        nrows = pooled.shape[0]
        ppad = jnp.pad(pooled, ((K1 // 2, K1 // 2), (0, 0)))
        conv = jnp.zeros((nrows, C1), jnp.float32)
        for t in range(K1):
            conv = conv + jnp.dot(ppad[t:t + nrows], conv_weight[:, t * C0:(t + 1) * C0].T, preferred_element_type=jnp.float32)
        embed = jax.nn.gelu(conv).reshape(-1, BIN // POOL, C1).mean(axis=1).astype(jnp.bfloat16)
        query = jnp.dot(embed, query_weight, preferred_element_type=jnp.float32)
        keys = jnp.dot(embed, key_weight, preferred_element_type=jnp.float32)
        dquery = jnp.dot(grad_map, keys, precision=high) * scale
        dkeys = jnp.dot(grad_map.T, query, precision=high) * scale
        dembed = jnp.dot(dquery, wq_f.T, precision=high) + jnp.dot(dkeys, wk_f.T, precision=high)
        embed_f = embed.astype(jnp.float32)
        acc_query = acc_query + jnp.dot(embed_f.T, dquery, precision=high)
        acc_key = acc_key + jnp.dot(embed_f.T, dkeys, precision=high)
        dconv = (gelu_slope(conv).reshape(-1, BIN // POOL, C1) * dembed[:, None, :] / (BIN // POOL)).reshape(nrows, C1).astype(jnp.bfloat16)
        slab = BASE_DEV // POOL

        def one_slab(total, index):
            first = (index * slab).astype(jnp.int32)
            dslab = lax.dynamic_slice_in_dim(dconv, first, slab, 0)
            blocks = []
            for t in range(K1):
                pslab = lax.dynamic_slice_in_dim(ppad, first + t, slab, 0)
                blocks.append(jnp.dot(dslab.T, pslab, preferred_element_type=jnp.float32))
            return total + jnp.concatenate(blocks, axis=1), None

        acc_conv, unused = lax.scan(one_slab, acc_conv, jnp.arange(N_SEQ, dtype=jnp.int32))
        return (acc_conv, acc_query, acc_key), None

    start = (jnp.zeros((C1, K1 * C0), jnp.float32), jnp.zeros((C1, PC), jnp.float32), jnp.zeros((C1, PC), jnp.float32))
    final, unused = lax.scan(one_sequence, start, (bases, pair_grad))
    return (final[0], final[1], final[2])
```

```python
import functools

import jax
import jax.numpy as jnp
from jax import lax
from jax.experimental import pallas as pl
from jax.experimental.pallas import tpu as pltpu
from jax.sharding import PartitionSpec as P

C0 = 768
C1 = 768
PC = 128
K0 = 15
K1 = 5
POOL = 8
BIN_ROWS = 256
WINDOW = 24
CHUNK = 64
PAD = 128
GRAD_BLOCK = 512

ROOT = 0.7978845608028654
CUBE = 0.044715
HIGH = lax.Precision.HIGHEST
VMEM_LIMIT = 56 * 1024 * 1024


def params():
    return pltpu.CompilerParams(vmem_limit_bytes=VMEM_LIMIT)


def swap(x, axis, bit):
    size = lax.axis_size(axis)
    return lax.ppermute(x, axis, [(i, i ^ bit) for i in range(size)])


def gather_xor(x, axis, dim):
    bit = 1
    while bit < lax.axis_size(axis):
        x = jnp.concatenate([x, swap(x, axis, bit)], axis=dim)
        bit *= 2
    return x


def twice_gelu(v):
    return v + v * jnp.tanh(v * (ROOT + (ROOT * CUBE) * (v * v)))


def stem_kernel(
    n, rows_dev, co, pay_ref, t0_ref, w_ref, p_ref, slope_ref, emb_ref, bases, table, weights, ybuf, sums
):
    step = pl.program_id(0)
    rows = n * rows_dev
    blocks = rows // BIN_ROWS

    @pl.when(step == 0)
    def _():
        me = lax.axis_index("seq")
        bases[...] = jnp.full(bases.shape, -1.0, jnp.float32)
        for slab in range(n):
            slot = jnp.bitwise_xor(me, slab)
            start = pl.multiple_of(slot * rows_dev, 128)
            block = pay_ref[:, pl.ds(start, rows_dev)].astype(jnp.float32)
            bases[:, PAD + slab * rows_dev : PAD + (slab + 1) * rows_dev] = block[:POOL]
        for chunk in range(C0 // CHUNK):
            part = t0_ref[chunk * CHUNK : (chunk + 1) * CHUNK, :]
            for pos in range(POOL):
                shifted = part if pos == 0 else pltpu.roll(part, pos, 1)
                first = (chunk * POOL + pos) * CHUNK
                table[first : first + CHUNK, :] = shifted.astype(jnp.bfloat16)
        for tap in range(K1):
            weights[tap * co : (tap + 1) * co, :] = w_ref[:, tap * C0 : (tap + 1) * C0]
        ybuf[:, :PAD] = jnp.zeros((K1 * co, PAD), jnp.float32)
        ybuf[:, PAD + rows :] = jnp.zeros((K1 * co, PAD), jnp.float32)
        sums[...] = jnp.zeros(sums.shape, jnp.float32)

    @pl.when(step < blocks)
    def _():
        first = pl.multiple_of(step * BIN_ROWS, 128)
        near = bases[:, pl.ds(first, BIN_ROWS + 2 * PAD)]
        window = jnp.concatenate(
            [near[:, PAD + q : PAD + q + BIN_ROWS] for q in (-1, 0, 1)], axis=0
        )
        onehot = jnp.concatenate(
            [(window == b).astype(jnp.float32) for b in range(4)]
            + [jnp.zeros((128 - 4 * WINDOW, BIN_ROWS), jnp.float32)],
            axis=0,
        ).astype(jnp.bfloat16)
        for chunk in range(C0 // CHUNK):
            stem = jnp.dot(
                table[chunk * POOL * CHUNK : (chunk + 1) * POOL * CHUNK, :],
                onehot,
                preferred_element_type=jnp.float32,
            )
            most = least = stem[:CHUNK]
            for pos in range(1, POOL):
                part = stem[pos * CHUNK : (pos + 1) * CHUNK]
                most = jnp.maximum(most, part)
                least = jnp.minimum(least, part)
            pooled = 0.5 * jnp.maximum(twice_gelu(most), twice_gelu(least))
            p_ref[chunk * CHUNK : (chunk + 1) * CHUNK, :] = pooled.astype(jnp.bfloat16)
        ybuf[:, pl.ds(first + PAD, BIN_ROWS)] = jnp.dot(
            weights[...], p_ref[...], preferred_element_type=jnp.float32
        )

    @pl.when(step >= 1)
    def _():
        first = pl.multiple_of((step - 1) * BIN_ROWS, 128)
        conv = None
        for tap in range(K1):
            near = ybuf[tap * co : (tap + 1) * co, pl.ds(first, BIN_ROWS + 2 * PAD)]
            begin = PAD + tap - K1 // 2
            part = near[:, begin : begin + BIN_ROWS]
            conv = part if conv is None else conv + part
        square = conv * conv
        tangent = jnp.tanh(conv * (ROOT + (ROOT * CUBE) * square))
        half = 0.5 * conv
        gelu = half + half * tangent
        slope_ref[...] = (0.5 + 0.5 * tangent) + half * (1.0 - tangent * tangent) * (
            ROOT + (3.0 * ROOT * CUBE) * square
        )
        mean = jnp.sum(gelu, axis=1, keepdims=True) * (1.0 / BIN_ROWS)
        lane = lax.broadcasted_iota(jnp.int32, sums.shape, 1)
        sums[...] = jnp.where(lane == step - 1, mean, sums[...])

    @pl.when(step == blocks)
    def _():
        emb_ref[...] = sums[...].T[: emb_ref.shape[0], :].astype(jnp.bfloat16)


def stem_and_conv(n, payload, first_table, conv_weight):
    co = conv_weight.shape[0]
    rows = payload.shape[1]
    blocks = rows // BIN_ROWS
    return pl.pallas_call(
        functools.partial(stem_kernel, n, rows // n, co),
        grid=(blocks + 1,),
        in_specs=[
            pl.BlockSpec(payload.shape, lambda i: (0, 0)),
            pl.BlockSpec(first_table.shape, lambda i: (0, 0)),
            pl.BlockSpec(conv_weight.shape, lambda i: (0, 0)),
        ],
        out_specs=[
            pl.BlockSpec((C0, BIN_ROWS), lambda i: (0, jnp.minimum(i, blocks - 1))),
            pl.BlockSpec((co, BIN_ROWS), lambda i: (0, jnp.maximum(i - 1, 0))),
            pl.BlockSpec((blocks, co), lambda i: (0, 0)),
        ],
        out_shape=[
            jax.ShapeDtypeStruct((C0, rows), jnp.bfloat16),
            jax.ShapeDtypeStruct((co, rows), jnp.float32),
            jax.ShapeDtypeStruct((blocks, co), jnp.bfloat16),
        ],
        scratch_shapes=[
            pltpu.VMEM((POOL, rows + 2 * PAD), jnp.float32),
            pltpu.VMEM((POOL * C0, 128), jnp.bfloat16),
            pltpu.VMEM((K1 * co, C0), jnp.bfloat16),
            pltpu.VMEM((K1 * co, rows + 2 * PAD), jnp.float32),
            pltpu.VMEM((co, 128), jnp.float32),
        ],
        compiler_params=params(),
        name="stem_and_conv",
    )(payload, first_table, conv_weight)


def grad_kernel(
    n, rows_dev, co, pay_ref, emb_ref, wq_ref, wk_ref, slope_ref, p_ref, keep_ref, send_ref, dpad, acc, qk
):
    step = pl.program_id(0)
    rows = n * rows_dev
    npos = rows // BIN_ROWS
    own_pos = npos // n
    scale = PC**-0.5

    @pl.when(step == 0)
    def _():
        me = lax.axis_index("seq")
        query = jnp.zeros((npos, PC), jnp.float32)
        keys = jnp.zeros((npos, PC), jnp.float32)
        for slot in range(n):
            first = pl.multiple_of(jnp.bitwise_xor(me, slot) * co, 16)
            embed = emb_ref[slot * npos : (slot + 1) * npos, :]
            query = query + jnp.dot(
                embed, wq_ref[pl.ds(first, co), :], preferred_element_type=jnp.float32
            )
            keys = keys + jnp.dot(
                embed, wk_ref[pl.ds(first, co), :], preferred_element_type=jnp.float32
            )
        pieces = []
        for slab in range(n):
            start = pl.multiple_of(jnp.bitwise_xor(me, slab) * rows_dev, 128)
            block = pay_ref[:, pl.ds(start, 128)].astype(jnp.float32)
            for row in range(own_pos):
                at = POOL + 3 * row
                pieces.append(block[at : at + 1] + block[at + 1 : at + 2] + block[at + 2 : at + 3])
        grad = jnp.concatenate(pieces, axis=0)[:, :npos]
        dquery = jnp.dot(grad, keys, precision=HIGH, preferred_element_type=jnp.float32) * scale
        dkeys = (
            lax.dot_general(
                grad, query, (((0,), (0,)), ((), ())), precision=HIGH,
                preferred_element_type=jnp.float32,
            )
            * scale
        )
        first = pl.multiple_of(me * co, 16)
        dembed = None
        for w_ref, cotangent in ((wq_ref, dquery), (wk_ref, dkeys)):
            part = lax.dot_general(
                w_ref[pl.ds(first, co), :].astype(jnp.float32), cotangent,
                (((1,), (1,)), ((), ())), precision=HIGH, preferred_element_type=jnp.float32,
            )
            dembed = part if dembed is None else dembed + part
        dembed = dembed * (1.0 / BIN_ROWS)
        own = emb_ref[:npos, :].astype(jnp.float32)
        for at, cotangent in enumerate((dquery, dkeys)):
            qk[:, at * PC : (at + 1) * PC] = lax.dot_general(
                own, cotangent, (((0,), (0,)), ((), ())), precision=HIGH,
                preferred_element_type=jnp.float32,
            )
        dpad[:, :PAD] = jnp.zeros((co, PAD), jnp.float32)
        dpad[:, PAD + rows :] = jnp.zeros((co, PAD), jnp.float32)
        for pos in range(npos):
            dpad[:, PAD + pos * BIN_ROWS : PAD + (pos + 1) * BIN_ROWS] = (
                slope_ref[:, pos * BIN_ROWS : (pos + 1) * BIN_ROWS] * dembed[:, pos : pos + 1]
            )
        acc[...] = jnp.zeros(acc.shape, jnp.float32)

    first = pl.multiple_of(step * GRAD_BLOCK, 128)
    near = dpad[:, pl.ds(first, GRAD_BLOCK + 2 * PAD)]
    shifted = jnp.concatenate(
        [
            near[:, PAD - tap + K1 // 2 : PAD - tap + K1 // 2 + GRAD_BLOCK].astype(jnp.bfloat16)
            for tap in range(K1)
        ],
        axis=0,
    )
    acc[...] += lax.dot_general(
        shifted, p_ref[...], (((1,), (1,)), ((), ())), preferred_element_type=jnp.float32
    )

    @pl.when(step == rows // GRAD_BLOCK - 1)
    def _():
        core = lax.axis_index("dp") % 2

        def write(low, high, kind_low, kind_high):
            taps = [acc[tap * co : (tap + 1) * co, :] for tap in range(K1)]
            low[:, : 2 * C0] = jnp.concatenate(taps[:2], axis=1).astype(kind_low)
            low[:, 2 * C0 :] = taps[2][:, : 2 * C0 // 3].astype(kind_low)
            high[:, : C0 // 3] = taps[2][:, 2 * C0 // 3 :].astype(kind_high)
            high[:, C0 // 3 : C0 // 3 + 2 * C0] = jnp.concatenate(taps[3:], axis=1).astype(kind_high)
            high[:, C0 // 3 + 2 * C0 :] = qk[...].astype(kind_high)

        @pl.when(core == 0)
        def _():
            write(keep_ref, send_ref, jnp.float32, jnp.bfloat16)

        @pl.when(core == 1)
        def _():
            write(send_ref, keep_ref, jnp.bfloat16, jnp.float32)


def gradients(n, payload, embed, query_weight, key_weight, slope, pooled):
    co, rows = slope.shape
    half = (K1 * C0 + 2 * PC) // 2
    whole = lambda i: (0, 0)
    return pl.pallas_call(
        functools.partial(grad_kernel, n, rows // n, co),
        grid=(rows // GRAD_BLOCK,),
        in_specs=[pl.BlockSpec(x.shape, whole) for x in (payload, embed, query_weight, key_weight, slope)]
        + [pl.BlockSpec((C0, GRAD_BLOCK), lambda i: (0, i))],
        out_specs=[pl.BlockSpec((co, half), whole)] * 2,
        out_shape=[
            jax.ShapeDtypeStruct((co, half), jnp.float32),
            jax.ShapeDtypeStruct((co, half), jnp.bfloat16),
        ],
        scratch_shapes=[
            pltpu.VMEM((co, rows + 2 * PAD), jnp.float32),
            pltpu.VMEM((K1 * co, C0), jnp.float32),
            pltpu.VMEM((co, 2 * PC), jnp.float32),
        ],
        compiler_params=params(),
        name="gradients",
    )(payload, embed, query_weight, key_weight, slope, pooled)


def add_kernel(a_ref, b_ref, out_ref):
    out_ref[...] = (a_ref[...].astype(jnp.float32) + b_ref[...].astype(jnp.float32)).astype(
        jnp.bfloat16
    )


def add_half(a, b):
    return pl.pallas_call(
        add_kernel,
        out_shape=jax.ShapeDtypeStruct(b.shape, jnp.bfloat16),
        compiler_params=params(),
        name="add_half",
    )(a, b)


def join_kernel(mine_ref, other_ref, conv_ref, query_ref, key_ref):
    half = mine_ref.shape[1]
    rest = K1 * C0 - half
    core = lax.axis_index("dp") % 2

    def write(low, high):
        conv_ref[:, :half] = low[...].astype(jnp.float32)
        conv_ref[:, half:] = high[:, :rest].astype(jnp.float32)
        query_ref[...] = high[:, rest : rest + PC].astype(jnp.float32)
        key_ref[...] = high[:, rest + PC :].astype(jnp.float32)

    @pl.when(core == 0)
    def _():
        write(mine_ref, other_ref)

    @pl.when(core == 1)
    def _():
        write(other_ref, mine_ref)


def join(mine, other):
    co = mine.shape[0]
    return pl.pallas_call(
        join_kernel,
        out_shape=[
            jax.ShapeDtypeStruct((co, K1 * C0), jnp.float32),
            jax.ShapeDtypeStruct((co, PC), jnp.float32),
            jax.ShapeDtypeStruct((co, PC), jnp.float32),
        ],
        compiler_params=params(),
        name="join",
    )(mine, other)


def body(bases, stem_table, conv_weight, query_weight, key_weight, pair_grad):
    n = lax.axis_size("seq")
    rows_dev = bases.shape[1] // POOL
    own_pos, npos = pair_grad.shape[1:]

    rest = pair_grad[0]
    parts = []
    for _ in range(3):
        part = lax.reduce_precision(rest, 8, 7)
        parts.append(part)
        rest = rest - part
    grad_rows = jnp.stack(parts, axis=1).reshape(3 * own_pos, npos).astype(jnp.bfloat16)
    grad_rows = jnp.pad(grad_rows, ((0, 8 - 3 * own_pos), (0, rows_dev - npos)))
    base_rows = bases.reshape(rows_dev, POOL).T.astype(jnp.bfloat16)
    payload = gather_xor(jnp.concatenate([base_rows, grad_rows], axis=0), "seq", 1)

    first_table = jnp.pad(
        stem_table.transpose(2, 1, 0), ((0, 0), (0, 0), (1, WINDOW - 1 - K0))
    ).reshape(C0, 4 * WINDOW)
    first_table = jnp.pad(first_table, ((0, 0), (0, 128 - 4 * WINDOW))).astype(jnp.float32)

    pooled, slope, embed = stem_and_conv(n, payload, first_table, conv_weight)
    embed_all = gather_xor(embed, "seq", 0)
    keep, send = gradients(n, payload, embed_all, query_weight, key_weight, slope, pooled)

    mine = add_half(keep, swap(send, "dp", 1))
    bit = 2
    while bit < lax.axis_size("dp"):
        mine = add_half(mine, swap(mine, "dp", bit))
        bit *= 2
    return tuple(join(mine, swap(mine, "dp", 1)))


def solution(mesh):
    return jax.shard_map(
        body,
        mesh=mesh,
        in_specs=(P("dp", "seq"), P(), P("seq", None), P(), P(), P("dp", "seq", None)),
        out_specs=(P("seq", None), P("seq", None), P("seq", None)),
        check_vma=False,
    )
```

```python
import functools

import jax
import jax.numpy as jnp
from jax import lax
from jax.experimental import pallas as pl
from jax.experimental.pallas import tpu as pltpu
from jax.sharding import PartitionSpec as P

C0 = 768
C1 = 768
PC = 128
K0 = 15
K1 = 5
POOL = 8
BIN_ROWS = 256
WINDOW = 24
CHUNK = 128
BLOCK = 512
LAG = 3
PAD = 128
SLOT = 128

ROOT = 0.7978845608028654
CUBE = 0.044715
HIGH = lax.Precision.HIGHEST
MIB = 1024 * 1024


def params(mib):
    return pltpu.CompilerParams(vmem_limit_bytes=mib * MIB)


def swap(x, axis, bit):
    size = lax.axis_size(axis)
    return lax.ppermute(x, axis, [(i, i ^ bit) for i in range(size)])


def gather_xor(x, axis):
    x = x[None]
    bit = 1
    while bit < lax.axis_size(axis):
        x = jnp.concatenate([x, swap(x, axis, bit)], axis=0)
        bit *= 2
    return x


def gather_direct(x, axis):
    return lax.all_to_all(jnp.broadcast_to(x[None], (lax.axis_size(axis),) + x.shape), axis, 0, 0)


def twice_gelu(v):
    return v + v * jnp.tanh(v * (ROOT + (ROOT * CUBE) * (v * v)))


def prepare_kernel(n, co, t0_ref, w_ref, wq_ref, wk_ref, table_ref, weights_ref, proj_ref):
    for chunk in range(C0 // CHUNK):
        part = t0_ref[chunk * CHUNK : (chunk + 1) * CHUNK, :]
        for pos in range(POOL):
            shifted = part if pos == 0 else pltpu.roll(part, pos, 1)
            first = (chunk * POOL + pos) * CHUNK
            table_ref[first : first + CHUNK, :] = shifted.astype(jnp.bfloat16)
    for tap in range(K1):
        weights_ref[tap * co : (tap + 1) * co, :] = w_ref[:, tap * C0 : (tap + 1) * C0]
    for slot in range(n):
        rows = slice(slot * co, (slot + 1) * co)
        proj_ref[slot * SLOT : slot * SLOT + co, :PC] = wq_ref[rows, :]
        proj_ref[slot * SLOT : slot * SLOT + co, PC:] = wk_ref[rows, :]
        proj_ref[slot * SLOT + co : (slot + 1) * SLOT, :] = jnp.zeros(
            (SLOT - co, 2 * PC), jnp.bfloat16
        )


def prepare(n, first_table, conv_weight, query_weight, key_weight):
    co = conv_weight.shape[0]
    return pl.pallas_call(
        functools.partial(prepare_kernel, n, co),
        out_shape=[
            jax.ShapeDtypeStruct((POOL * C0, 128), jnp.bfloat16),
            jax.ShapeDtypeStruct((K1 * co, C0), jnp.bfloat16),
            jax.ShapeDtypeStruct((n * SLOT, 2 * PC), jnp.bfloat16),
        ],
        compiler_params=params(8),
        cost_estimate=pl.CostEstimate(flops=0, bytes_accessed=5 * MIB, transcendentals=0),
        name="prepare",
    )(first_table, conv_weight, query_weight, key_weight)


def stem_kernel(
    n, rows_dev, co, pay_ref, table, weights, grad_ref, p_ref, slope_ref, emb_ref, bases, ybuf, prev, sums, sa, sb, slopes
):
    step = pl.program_id(0)
    rows = n * rows_dev
    blocks = rows // BLOCK
    front = LAG * BLOCK + PAD
    piece = 256

    def convolve(block):
        first = pl.multiple_of((block + LAG) * BLOCK, 128)
        conv = None
        for tap in range(K1):
            near = ybuf[tap * co : (tap + 1) * co, pl.ds(first, BLOCK + 2 * PAD)]
            begin = PAD + tap - K1 // 2
            part = near[:, begin : begin + BLOCK]
            conv = part if conv is None else conv + part
        square = conv * conv
        tangent = jnp.tanh(conv * (ROOT + (ROOT * CUBE) * square))
        half = 0.5 * conv
        gelu = half + half * tangent
        slopes[...] = (0.5 + 0.5 * tangent) + half * (1.0 - tangent * tangent) * (
            ROOT + (3.0 * ROOT * CUBE) * square
        )
        lane = lax.broadcasted_iota(jnp.int32, (co, 128), 1)
        total = sums[:co, :]
        for part in range(BLOCK // BIN_ROWS):
            mean = jnp.sum(
                gelu[:, part * BIN_ROWS : (part + 1) * BIN_ROWS], axis=1, keepdims=True
            ) * (1.0 / BIN_ROWS)
            total = jnp.where(lane == block * (BLOCK // BIN_ROWS) + part, mean, total)
        sums[:co, :] = total

    def taps(block):
        ybuf[:, pl.ds(pl.multiple_of(front + block * BLOCK, 128), BLOCK)] = jnp.dot(
            weights[...], prev[...], preferred_element_type=jnp.float32
        )

    @pl.when(step == 0)
    def _():
        me = lax.axis_index("seq")
        bases[:, :PAD] = jnp.full((POOL, PAD), -1.0, jnp.float32)
        bases[:, PAD + rows :] = jnp.full((POOL, PAD), -1.0, jnp.float32)
        half = rows_dev // 2
        for slab in range(n):
            block = pay_ref[jnp.bitwise_xor(me, slab)].astype(jnp.float32)
            first = PAD + slab * rows_dev
            bases[:, first : first + half] = block[:POOL]
            bases[:, first + half : first + 2 * half] = block[POOL:]
        ybuf[:, front + rows :] = jnp.zeros((K1 * co, PAD), jnp.float32)
        prev[...] = jnp.zeros(prev.shape, jnp.bfloat16)
        sums[...] = jnp.zeros(sums.shape, jnp.float32)

    @pl.when(step < blocks)
    def _():
        first = pl.multiple_of(step * BLOCK, 128)
        near = bases[:, pl.ds(first, BLOCK + 2 * PAD)]
        window = jnp.concatenate(
            [near[:, PAD + q : PAD + q + BLOCK] for q in (-1, 0, 1)], axis=0
        )
        onehot = jnp.concatenate(
            [(window == b).astype(jnp.float32) for b in range(4)]
            + [jnp.zeros((128 - 4 * WINDOW, BLOCK), jnp.float32)],
            axis=0,
        ).astype(jnp.bfloat16)
        convolve(step - LAG)
        taps(step - 1)
        stage = (sa, sb)

        def multiply(chunk, at):
            stage[chunk % 2][:, at : at + piece] = jnp.dot(
                table[chunk * POOL * CHUNK : (chunk + 1) * POOL * CHUNK, :],
                onehot[:, at : at + piece],
                preferred_element_type=jnp.float32,
            )

        def pool(chunk, at):
            stem = stage[chunk % 2]
            for row in range(0, CHUNK, 16):
                most = least = stem[row : row + 16, at : at + piece]
                for pos in range(1, POOL):
                    part = stem[pos * CHUNK + row : pos * CHUNK + row + 16, at : at + piece]
                    most = jnp.maximum(most, part)
                    least = jnp.minimum(least, part)
                pooled = (0.5 * jnp.maximum(twice_gelu(most), twice_gelu(least))).astype(jnp.bfloat16)
                to = chunk * CHUNK + row
                prev[to : to + 16, at : at + piece] = pooled

        chunks = C0 // CHUNK
        for at in range(0, BLOCK, piece):
            multiply(0, at)
        for chunk in range(chunks):
            for at in range(0, BLOCK, piece):
                if chunk + 1 < chunks:
                    multiply(chunk + 1, at)
                pool(chunk, at)
        p_ref[...] = prev[...]
        slope_ref[...] = slopes[...]

    @pl.when(step >= blocks)
    def _():
        @pl.when(step == blocks)
        def _():
            taps(blocks - 1)

        convolve(step - LAG)
        slope_ref[...] = slopes[...]

    @pl.when(step == blocks + LAG - 1)
    def _():
        own_pos, npos = grad_ref.shape
        embed = sums[...].T[:npos, :].astype(jnp.bfloat16).astype(jnp.float32)
        rest = grad_ref[...]
        parts = []
        for _ in range(3):
            part = rest.astype(jnp.bfloat16).astype(jnp.float32)
            parts.append(part)
            rest = rest - part
        grads = jnp.concatenate(
            parts + [jnp.zeros((npos - 3 * own_pos, npos), jnp.float32)], axis=0
        )
        emb_ref[...] = jnp.concatenate(
            [embed[:, :co], grads, jnp.zeros((npos, SLOT - co - npos), jnp.float32)], axis=1
        ).astype(jnp.bfloat16)


def stem_and_conv(n, payload, table, weights, pair_grad):
    co = weights.shape[0] // K1
    rows_dev = payload.shape[2] * 2
    rows = n * rows_dev
    npos = rows // BIN_ROWS
    blocks = rows // BLOCK
    whole = lambda i: (0, 0)
    return pl.pallas_call(
        functools.partial(stem_kernel, n, rows_dev, co),
        grid=(blocks + LAG,),
        in_specs=[
            pl.BlockSpec(payload.shape, lambda i: (0, 0, 0)),
            pl.BlockSpec(table.shape, whole),
            pl.BlockSpec(weights.shape, whole),
            pl.BlockSpec(pair_grad.shape, whole),
        ],
        out_specs=[
            pl.BlockSpec((C0, BLOCK), lambda i: (0, jnp.minimum(i, blocks - 1))),
            pl.BlockSpec((co, BLOCK), lambda i: (0, jnp.maximum(i - LAG, 0))),
            pl.BlockSpec((npos, SLOT), whole),
        ],
        out_shape=[
            jax.ShapeDtypeStruct((C0, rows), jnp.bfloat16),
            jax.ShapeDtypeStruct((co, rows), jnp.float32),
            jax.ShapeDtypeStruct((npos, SLOT), jnp.bfloat16),
        ],
        scratch_shapes=[
            pltpu.VMEM((POOL, rows + 2 * PAD), jnp.float32),
            pltpu.VMEM((K1 * co, LAG * BLOCK + rows + 2 * PAD), jnp.float32),
            pltpu.VMEM((C0, BLOCK), jnp.bfloat16),
            pltpu.VMEM((128, 128), jnp.float32),
            pltpu.VMEM((POOL * CHUNK, BLOCK), jnp.float32),
            pltpu.VMEM((POOL * CHUNK, BLOCK), jnp.float32),
            pltpu.VMEM((co, BLOCK), jnp.float32),
        ],
        compiler_params=params(36),
        name="stem_and_conv",
    )(payload, table, weights, pair_grad)


WIDE = K1 * C0 + 2 * PC
PARTS = ((0, K1 * C0), (K1 * C0, K1 * C0 + PC), (K1 * C0 + PC, WIDE))
CODED = WIDE + 128


def encode(values, out_ref):
    exponents = []
    for (begin, end), x in zip(PARTS, values):
        top = jnp.maximum(jnp.max(jnp.abs(x), axis=1, keepdims=True), 1e-30)
        exponent = jnp.floor(jnp.log2(32000.0 / top))
        scaled = jnp.floor(x * jnp.exp2(exponent) + 0.5)
        out_ref[:, begin:end] = scaled.astype(jnp.int32).astype(jnp.int16)
        exponents.append(exponent)
    lane = lax.broadcasted_iota(jnp.int32, (out_ref.shape[0], 128), 1)
    packed = jnp.where(lane == 0, exponents[0], jnp.where(lane == 1, exponents[1], exponents[2]))
    out_ref[:, WIDE:] = packed.astype(jnp.int32).astype(jnp.int16)


def decode(ref):
    exponents = ref[:, WIDE:].astype(jnp.int32).astype(jnp.float32)
    return [
        ref[:, begin:end].astype(jnp.int32).astype(jnp.float32) * jnp.exp2(-exponents[:, at : at + 1])
        for at, (begin, end) in enumerate(PARTS)
    ]


def half_gradient(half, dconv, qk_ref, pooled_ref, out_ref, shifted):
    size = out_ref.shape[0]
    held = dconv.shape[1]
    rows = pooled_ref.shape[1]
    shifted[K1 * held :, :] = jnp.zeros((shifted.shape[0] - K1 * held, rows), jnp.bfloat16)
    for first in range(0, rows, BLOCK):
        near = dconv[half, :, first : first + BLOCK + 2 * PAD]
        for tap in range(K1):
            begin = PAD - tap + K1 // 2
            shifted[tap * held : (tap + 1) * held, first : first + BLOCK] = near[
                :, begin : begin + BLOCK
            ]
    product = lax.dot_general(
        pooled_ref[...], shifted[...], (((1,), (1,)), ((), ())), preferred_element_type=jnp.float32
    ).T
    conv = jnp.concatenate(
        [product[tap * held : tap * held + size, :] for tap in range(K1)], axis=1
    )
    if out_ref.dtype == jnp.int16:
        qk = qk_ref[half]
        encode((conv, qk[:, :PC], qk[:, PC:]), out_ref)
    else:
        out_ref[:, : K1 * C0] = conv
        out_ref[:, K1 * C0 :] = qk_ref[half]


def send_kernel(n, emb_ref, proj_ref, slope_ref, pooled_ref, send_ref, dconv_ref, qk_ref, shifted):
    co, rows = slope_ref.shape
    size, held = co // 2, dconv_ref.shape[1]
    npos = rows // BIN_ROWS
    own_pos = npos // n
    scale = PC**-0.5
    me = lax.axis_index("seq")
    both = jnp.dot(
        jnp.concatenate([emb_ref[slot] for slot in range(n)], axis=1),
        proj_ref[...],
        preferred_element_type=jnp.float32,
    )
    query, keys = both[:, :PC], both[:, PC:]
    pieces = []
    for slab in range(n):
        block = emb_ref[slab].astype(jnp.float32)
        total = block[:own_pos]
        for part in range(1, 3):
            total = total + block[part * own_pos : (part + 1) * own_pos]
        pieces.append(total)
    grad = jnp.concatenate(pieces, axis=0)[:, co : co + npos]
    dquery = jnp.dot(grad, keys, precision=HIGH, preferred_element_type=jnp.float32) * scale
    dkeys = (
        lax.dot_general(
            grad, query, (((0,), (0,)), ((), ())), precision=HIGH,
            preferred_element_type=jnp.float32,
        )
        * scale
    )
    cotangent = jnp.concatenate([dquery, dkeys], axis=1)
    own = pl.ds(pl.multiple_of(me * SLOT, SLOT), SLOT)
    dembed = lax.dot_general(
        proj_ref[own, :].astype(jnp.float32), cotangent,
        (((1,), (1,)), ((), ())), precision=HIGH, preferred_element_type=jnp.float32,
    ) * (1.0 / BIN_ROWS)
    qk = lax.dot_general(
        emb_ref[me].astype(jnp.float32), cotangent, (((0,), (0,)), ((), ())),
        precision=HIGH, preferred_element_type=jnp.float32,
    )
    edge = jnp.zeros((held, PAD), jnp.bfloat16)
    for half in range(2):
        channels = slice(half * size, (half + 1) * size)
        qk_ref[half] = qk[channels]
        dconv_ref[half, :, :PAD] = edge
        dconv_ref[half, :, PAD + rows :] = edge
        for pos in range(npos):
            part = slope_ref[channels, pos * BIN_ROWS : (pos + 1) * BIN_ROWS] * dembed[
                channels, pos : pos + 1
            ]
            if held > size:
                part = jnp.concatenate(
                    [part, jnp.zeros((held - size, BIN_ROWS), jnp.float32)], axis=0
                )
            dconv_ref[half, :, PAD + pos * BIN_ROWS : PAD + (pos + 1) * BIN_ROWS] = part.astype(
                jnp.bfloat16
            )
    half_gradient(1 - lax.axis_index("dp") % 2, dconv_ref, qk_ref, pooled_ref, send_ref, shifted)


def keep_kernel(dconv_ref, qk_ref, pooled_ref, keep_ref, shifted):
    half_gradient(lax.axis_index("dp") % 2, dconv_ref, qk_ref, pooled_ref, keep_ref, shifted)


def send_half(n, embed, proj, slope, pooled):
    co, rows = slope.shape
    size = co // 2
    held = -(-size // 16) * 16
    return pl.pallas_call(
        functools.partial(send_kernel, n),
        out_shape=[
            jax.ShapeDtypeStruct((size, CODED), jnp.int16),
            jax.ShapeDtypeStruct((2, held, rows + 2 * PAD), jnp.bfloat16),
            jax.ShapeDtypeStruct((2, size, 2 * PC), jnp.float32),
        ],
        scratch_shapes=[pltpu.VMEM((256, rows), jnp.bfloat16)],
        compiler_params=params(32),
        name="send_half",
    )(embed, proj, slope, pooled)


def keep_half(dconv, qk, pooled):
    size, rows = qk.shape[1], pooled.shape[1]
    return pl.pallas_call(
        keep_kernel,
        out_shape=jax.ShapeDtypeStruct((size, WIDE), jnp.float32),
        scratch_shapes=[pltpu.VMEM((256, rows), jnp.bfloat16)],
        compiler_params=params(32),
        cost_estimate=pl.CostEstimate(
            flops=2 * K1 * size * C0 * rows, bytes_accessed=12 * MIB, transcendentals=0
        ),
        name="keep_half",
    )(dconv, qk, pooled)


def add_kernel(a_ref, b_ref, out_ref):
    if a_ref.dtype == jnp.int16:
        a = decode(a_ref)
    else:
        a = [a_ref[:, begin:end] for begin, end in PARTS]
    encode([x + y for x, y in zip(a, decode(b_ref))], out_ref)


def add_half(a, b):
    return pl.pallas_call(
        add_kernel,
        out_shape=jax.ShapeDtypeStruct(b.shape, jnp.int16),
        compiler_params=params(8),
        name="add_half",
    )(a, b)


def join_kernel(mine_ref, other_ref, conv_ref, query_ref, key_ref):
    size = mine_ref.shape[0]
    core = lax.axis_index("dp") % 2
    for half, ref in ((core, mine_ref), (1 - core, other_ref)):
        rows = pl.ds(pl.multiple_of(half * size, 8), size)
        for x, out_ref in zip(decode(ref), (conv_ref, query_ref, key_ref)):
            out_ref[rows, :] = x


def join(mine, other):
    co = 2 * mine.shape[0]
    return pl.pallas_call(
        join_kernel,
        out_shape=[
            jax.ShapeDtypeStruct((co, K1 * C0), jnp.float32),
            jax.ShapeDtypeStruct((co, PC), jnp.float32),
            jax.ShapeDtypeStruct((co, PC), jnp.float32),
        ],
        compiler_params=params(8),
        name="join",
    )(mine, other)


def body(bases, stem_table, conv_weight, query_weight, key_weight, pair_grad):
    n = lax.axis_size("seq")
    rows_dev = bases.shape[1] // POOL

    own = bases.astype(jnp.bfloat16).reshape(2, rows_dev // 2, POOL).transpose(0, 2, 1)
    payload = gather_xor(own.reshape(2 * POOL, rows_dev // 2), "seq")

    first_table = jnp.pad(
        stem_table.transpose(2, 1, 0), ((0, 0), (0, 0), (1, WINDOW - 1 - K0))
    ).reshape(C0, 4 * WINDOW)
    first_table = jnp.pad(first_table, ((0, 0), (0, 128 - 4 * WINDOW))).astype(jnp.float32)
    table, weights, proj = prepare(n, first_table, conv_weight, query_weight, key_weight)

    pooled, slope, embed = stem_and_conv(n, payload, table, weights, pair_grad[0])
    embed_all = gather_direct(embed, "seq")
    send, dconv, qk = send_half(n, embed_all, proj, slope, pooled)
    received = swap(send, "dp", 1)
    keep = keep_half(dconv, qk, pooled)

    mine = add_half(keep, received)
    bit = 2
    while bit < lax.axis_size("dp"):
        mine = add_half(mine, swap(mine, "dp", bit))
        bit *= 2
    return tuple(join(mine, swap(mine, "dp", 1)))


def solution(mesh):
    return jax.shard_map(
        body,
        mesh=mesh,
        in_specs=(P("dp", "seq"), P(), P("seq", None), P(), P(), P("dp", "seq", None)),
        out_specs=(P("seq", None), P("seq", None), P("seq", None)),
        check_vma=False,
    )
```

```python
import functools

import jax
import jax.numpy as jnp
from jax import lax
from jax.experimental import pallas as pl
from jax.experimental.pallas import tpu as pltpu
from jax.sharding import PartitionSpec as P

C0 = 768
C1 = 768
PC = 128
K0 = 15
K1 = 5
POOL = 8
BIN_ROWS = 256
WINDOW = 24
CHUNK = 128
BLOCK = 512
LAG = 3
PAD = 128
SLOT = 128

ROOT = 0.7978845608028654
CUBE = 0.044715
HIGH = lax.Precision.HIGHEST
MIB = 1024 * 1024


def params(mib):
    return pltpu.CompilerParams(vmem_limit_bytes=mib * MIB)


def swap(x, axis, bit):
    size = lax.axis_size(axis)
    return lax.ppermute(x, axis, [(i, i ^ bit) for i in range(size)])


def gather_xor(x, axis):
    x = x[None]
    bit = 1
    while bit < lax.axis_size(axis):
        x = jnp.concatenate([x, swap(x, axis, bit)], axis=0)
        bit *= 2
    return x


def gather_direct(x, axis):
    return lax.all_to_all(jnp.broadcast_to(x[None], (lax.axis_size(axis),) + x.shape), axis, 0, 0)


def twice_gelu(v):
    return v + v * jnp.tanh(v * (ROOT + (ROOT * CUBE) * (v * v)))


def prepare_kernel(n, co, t0_ref, w_ref, wq_ref, wk_ref, table_ref, weights_ref, proj_ref):
    for chunk in range(C0 // CHUNK):
        part = t0_ref[chunk * CHUNK : (chunk + 1) * CHUNK, :]
        for pos in range(POOL):
            shifted = part if pos == 0 else pltpu.roll(part, pos, 1)
            first = (chunk * POOL + pos) * CHUNK
            table_ref[first : first + CHUNK, :] = shifted.astype(jnp.bfloat16)
    for tap in range(K1):
        weights_ref[tap * co : (tap + 1) * co, :] = w_ref[:, tap * C0 : (tap + 1) * C0]
    for slot in range(n):
        rows = slice(slot * co, (slot + 1) * co)
        proj_ref[slot * SLOT : slot * SLOT + co, :PC] = wq_ref[rows, :]
        proj_ref[slot * SLOT : slot * SLOT + co, PC:] = wk_ref[rows, :]
        proj_ref[slot * SLOT + co : (slot + 1) * SLOT, :] = jnp.zeros(
            (SLOT - co, 2 * PC), jnp.bfloat16
        )


def prepare(n, first_table, conv_weight, query_weight, key_weight):
    co = conv_weight.shape[0]
    return pl.pallas_call(
        functools.partial(prepare_kernel, n, co),
        out_shape=[
            jax.ShapeDtypeStruct((POOL * C0, 128), jnp.bfloat16),
            jax.ShapeDtypeStruct((K1 * co, C0), jnp.bfloat16),
            jax.ShapeDtypeStruct((n * SLOT, 2 * PC), jnp.bfloat16),
        ],
        compiler_params=params(8),
        cost_estimate=pl.CostEstimate(flops=0, bytes_accessed=5 * MIB, transcendentals=0),
        name="prepare",
    )(first_table, conv_weight, query_weight, key_weight)


def stem_kernel(
    n, rows_dev, co, pay_ref, table_ref, weights_ref, grad_ref, p_ref, slope_ref, emb_ref,
    table, weights, bases, ybuf, prev, sums, sa, sb, slopes
):
    step = pl.program_id(0)
    rows = n * rows_dev
    blocks = rows // BLOCK
    front = LAG * BLOCK + PAD
    piece = 256

    def convolve(block):
        first = pl.multiple_of((block + LAG) * BLOCK, 128)
        conv = None
        for tap in range(K1):
            near = ybuf[tap * co : (tap + 1) * co, pl.ds(first, BLOCK + 2 * PAD)]
            begin = PAD + tap - K1 // 2
            part = near[:, begin : begin + BLOCK]
            conv = part if conv is None else conv + part
        square = conv * conv
        tangent = jnp.tanh(conv * (ROOT + (ROOT * CUBE) * square))
        half = 0.5 * conv
        gelu = half + half * tangent
        slopes[...] = (0.5 + 0.5 * tangent) + half * (1.0 - tangent * tangent) * (
            ROOT + (3.0 * ROOT * CUBE) * square
        )
        lane = lax.broadcasted_iota(jnp.int32, (co, 128), 1)
        total = sums[:co, :]
        for part in range(BLOCK // BIN_ROWS):
            mean = jnp.sum(
                gelu[:, part * BIN_ROWS : (part + 1) * BIN_ROWS], axis=1, keepdims=True
            ) * (1.0 / BIN_ROWS)
            total = jnp.where(lane == block * (BLOCK // BIN_ROWS) + part, mean, total)
        sums[:co, :] = total

    def taps(block):
        ybuf[:, pl.ds(pl.multiple_of(front + block * BLOCK, 128), BLOCK)] = jnp.dot(
            weights[...], prev[...], preferred_element_type=jnp.float32
        )

    @pl.when(step == 0)
    def _():
        me = lax.axis_index("seq")
        bases[:, :PAD] = jnp.full((POOL, PAD), -1.0, jnp.float32)
        bases[:, PAD + rows :] = jnp.full((POOL, PAD), -1.0, jnp.float32)
        half = rows_dev // 2
        for slab in range(n):
            block = pay_ref[jnp.bitwise_xor(me, slab)].astype(jnp.float32)
            first = PAD + slab * rows_dev
            bases[:, first : first + half] = block[:POOL]
            bases[:, first + half : first + 2 * half] = block[POOL:]
        table[...] = table_ref[...]
        weights[...] = weights_ref[...]
        ybuf[:, front + rows :] = jnp.zeros((K1 * co, PAD), jnp.float32)
        prev[...] = jnp.zeros(prev.shape, jnp.bfloat16)
        sums[...] = jnp.zeros(sums.shape, jnp.float32)

    @pl.when(step < blocks)
    def _():
        first = pl.multiple_of(step * BLOCK, 128)
        near = bases[:, pl.ds(first, BLOCK + 2 * PAD)]
        window = jnp.concatenate(
            [near[:, PAD + q : PAD + q + BLOCK] for q in (-1, 0, 1)], axis=0
        )
        onehot = jnp.concatenate(
            [(window == b).astype(jnp.float32) for b in range(4)]
            + [jnp.zeros((128 - 4 * WINDOW, BLOCK), jnp.float32)],
            axis=0,
        ).astype(jnp.bfloat16)
        convolve(step - LAG)
        taps(step - 1)
        stage = (sa, sb)

        def multiply(chunk, at):
            stage[chunk % 2][:, at : at + piece] = jnp.dot(
                table[chunk * POOL * CHUNK : (chunk + 1) * POOL * CHUNK, :],
                onehot[:, at : at + piece],
                preferred_element_type=jnp.float32,
            )

        def pool(chunk, at):
            stem = stage[chunk % 2]
            for row in range(0, CHUNK, 16):
                most = least = stem[row : row + 16, at : at + piece]
                for pos in range(1, POOL):
                    part = stem[pos * CHUNK + row : pos * CHUNK + row + 16, at : at + piece]
                    most = jnp.maximum(most, part)
                    least = jnp.minimum(least, part)
                pooled = (0.5 * jnp.maximum(twice_gelu(most), twice_gelu(least))).astype(jnp.bfloat16)
                to = chunk * CHUNK + row
                prev[to : to + 16, at : at + piece] = pooled

        chunks = C0 // CHUNK
        for at in range(0, BLOCK, piece):
            multiply(0, at)
        for chunk in range(chunks):
            for at in range(0, BLOCK, piece):
                if chunk + 1 < chunks:
                    multiply(chunk + 1, at)
                pool(chunk, at)
        p_ref[...] = prev[...]
        slope_ref[...] = slopes[...]

    @pl.when(step >= blocks)
    def _():
        @pl.when(step == blocks)
        def _():
            taps(blocks - 1)

        convolve(step - LAG)
        slope_ref[...] = slopes[...]

    @pl.when(step == blocks + LAG - 1)
    def _():
        own_pos, npos = grad_ref.shape
        embed = sums[...].T[:npos, :].astype(jnp.bfloat16).astype(jnp.float32)
        rest = grad_ref[...]
        parts = []
        for _ in range(3):
            part = rest.astype(jnp.bfloat16).astype(jnp.float32)
            parts.append(part)
            rest = rest - part
        grads = jnp.concatenate(
            parts + [jnp.zeros((npos - 3 * own_pos, npos), jnp.float32)], axis=0
        )
        emb_ref[...] = jnp.concatenate(
            [embed[:, :co], grads, jnp.zeros((npos, SLOT - co - npos), jnp.float32)], axis=1
        ).astype(jnp.bfloat16)


def stem_and_conv(n, payload, table, weights, pair_grad):
    co = weights.shape[0] // K1
    rows_dev = payload.shape[2] * 2
    rows = n * rows_dev
    npos = rows // BIN_ROWS
    blocks = rows // BLOCK
    whole = lambda i: (0, 0)
    return pl.pallas_call(
        functools.partial(stem_kernel, n, rows_dev, co),
        grid=(blocks + LAG,),
        in_specs=[
            pl.BlockSpec(payload.shape, lambda i: (0, 0, 0)),
            pl.BlockSpec(table.shape, whole),
            pl.BlockSpec(weights.shape, whole),
            pl.BlockSpec(pair_grad.shape, whole),
        ],
        out_specs=[
            pl.BlockSpec((C0, BLOCK), lambda i: (0, jnp.minimum(i, blocks - 1))),
            pl.BlockSpec((co, BLOCK), lambda i: (0, jnp.maximum(i - LAG, 0))),
            pl.BlockSpec((npos, SLOT), whole),
        ],
        out_shape=[
            jax.ShapeDtypeStruct((C0, rows), jnp.bfloat16),
            jax.ShapeDtypeStruct((co, rows), jnp.float32),
            jax.ShapeDtypeStruct((npos, SLOT), jnp.bfloat16),
        ],
        scratch_shapes=[
            pltpu.VMEM(table.shape, jnp.bfloat16),
            pltpu.VMEM(weights.shape, jnp.bfloat16),
            pltpu.VMEM((POOL, rows + 2 * PAD), jnp.float32),
            pltpu.VMEM((K1 * co, LAG * BLOCK + rows + 2 * PAD), jnp.float32),
            pltpu.VMEM((C0, BLOCK), jnp.bfloat16),
            pltpu.VMEM((128, 128), jnp.float32),
            pltpu.VMEM((POOL * CHUNK, BLOCK), jnp.float32),
            pltpu.VMEM((POOL * CHUNK, BLOCK), jnp.float32),
            pltpu.VMEM((co, BLOCK), jnp.float32),
        ],
        compiler_params=params(36),
        name="stem_and_conv",
    )(payload, table, weights, pair_grad)


WIDE = K1 * C0 + 2 * PC
PARTS = ((0, K1 * C0), (K1 * C0, K1 * C0 + PC), (K1 * C0 + PC, WIDE))
CODED = WIDE + 128


def encode(values, out_ref):
    exponents = []
    for (begin, end), x in zip(PARTS, values):
        top = jnp.maximum(jnp.max(jnp.abs(x), axis=1, keepdims=True), 1e-30)
        exponent = jnp.floor(jnp.log2(32000.0 / top))
        scaled = jnp.floor(x * jnp.exp2(exponent) + 0.5)
        out_ref[:, begin:end] = scaled.astype(jnp.int32).astype(jnp.int16)
        exponents.append(exponent)
    lane = lax.broadcasted_iota(jnp.int32, (out_ref.shape[0], 128), 1)
    packed = jnp.where(lane == 0, exponents[0], jnp.where(lane == 1, exponents[1], exponents[2]))
    out_ref[:, WIDE:] = packed.astype(jnp.int32).astype(jnp.int16)


def decode(ref):
    exponents = ref[:, WIDE:].astype(jnp.int32).astype(jnp.float32)
    return [
        ref[:, begin:end].astype(jnp.int32).astype(jnp.float32) * jnp.exp2(-exponents[:, at : at + 1])
        for at, (begin, end) in enumerate(PARTS)
    ]


def half_gradient(half, dconv, qk_ref, pooled_ref, out_ref, shifted):
    size = out_ref.shape[0]
    held = dconv.shape[1]
    rows = pooled_ref.shape[1]
    shifted[K1 * held :, :] = jnp.zeros((shifted.shape[0] - K1 * held, rows), jnp.bfloat16)
    for first in range(0, rows, BLOCK):
        near = dconv[half, :, first : first + BLOCK + 2 * PAD]
        for tap in range(K1):
            begin = PAD - tap + K1 // 2
            shifted[tap * held : (tap + 1) * held, first : first + BLOCK] = near[
                :, begin : begin + BLOCK
            ]
    product = lax.dot_general(
        pooled_ref[...], shifted[...], (((1,), (1,)), ((), ())), preferred_element_type=jnp.float32
    ).T
    conv = jnp.concatenate(
        [product[tap * held : tap * held + size, :] for tap in range(K1)], axis=1
    )
    if out_ref.dtype == jnp.int16:
        qk = qk_ref[half]
        encode((conv, qk[:, :PC], qk[:, PC:]), out_ref)
    else:
        out_ref[:, : K1 * C0] = conv
        out_ref[:, K1 * C0 :] = qk_ref[half]


def send_kernel(n, emb_ref, proj_ref, slope_ref, pooled_ref, send_ref, dconv_ref, qk_ref, shifted):
    co, rows = slope_ref.shape
    size, held = co // 2, dconv_ref.shape[1]
    npos = rows // BIN_ROWS
    own_pos = npos // n
    scale = PC**-0.5
    me = lax.axis_index("seq")
    both = jnp.dot(
        jnp.concatenate([emb_ref[slot] for slot in range(n)], axis=1),
        proj_ref[...],
        preferred_element_type=jnp.float32,
    )
    query, keys = both[:, :PC], both[:, PC:]
    pieces = []
    for slab in range(n):
        block = emb_ref[slab].astype(jnp.float32)
        total = block[:own_pos]
        for part in range(1, 3):
            total = total + block[part * own_pos : (part + 1) * own_pos]
        pieces.append(total)
    grad = jnp.concatenate(pieces, axis=0)[:, co : co + npos]
    dquery = jnp.dot(grad, keys, precision=HIGH, preferred_element_type=jnp.float32) * scale
    dkeys = (
        lax.dot_general(
            grad, query, (((0,), (0,)), ((), ())), precision=HIGH,
            preferred_element_type=jnp.float32,
        )
        * scale
    )
    cotangent = jnp.concatenate([dquery, dkeys], axis=1)
    own = pl.ds(pl.multiple_of(me * SLOT, SLOT), SLOT)
    dembed = lax.dot_general(
        proj_ref[own, :].astype(jnp.float32), cotangent,
        (((1,), (1,)), ((), ())), precision=HIGH, preferred_element_type=jnp.float32,
    ) * (1.0 / BIN_ROWS)
    qk = lax.dot_general(
        emb_ref[me].astype(jnp.float32), cotangent, (((0,), (0,)), ((), ())),
        precision=HIGH, preferred_element_type=jnp.float32,
    )
    edge = jnp.zeros((held, PAD), jnp.bfloat16)
    for half in range(2):
        channels = slice(half * size, (half + 1) * size)
        qk_ref[half] = qk[channels]
        dconv_ref[half, :, :PAD] = edge
        dconv_ref[half, :, PAD + rows :] = edge
        for pos in range(npos):
            part = slope_ref[channels, pos * BIN_ROWS : (pos + 1) * BIN_ROWS] * dembed[
                channels, pos : pos + 1
            ]
            if held > size:
                part = jnp.concatenate(
                    [part, jnp.zeros((held - size, BIN_ROWS), jnp.float32)], axis=0
                )
            dconv_ref[half, :, PAD + pos * BIN_ROWS : PAD + (pos + 1) * BIN_ROWS] = part.astype(
                jnp.bfloat16
            )
    half_gradient(1 - lax.axis_index("dp") % 2, dconv_ref, qk_ref, pooled_ref, send_ref, shifted)


def keep_kernel(dconv_ref, qk_ref, pooled_ref, keep_ref, shifted):
    half_gradient(lax.axis_index("dp") % 2, dconv_ref, qk_ref, pooled_ref, keep_ref, shifted)


def send_half(n, embed, proj, slope, pooled):
    co, rows = slope.shape
    size = co // 2
    held = -(-size // 16) * 16
    return pl.pallas_call(
        functools.partial(send_kernel, n),
        out_shape=[
            jax.ShapeDtypeStruct((size, CODED), jnp.int16),
            jax.ShapeDtypeStruct((2, held, rows + 2 * PAD), jnp.bfloat16),
            jax.ShapeDtypeStruct((2, size, 2 * PC), jnp.float32),
        ],
        scratch_shapes=[pltpu.VMEM((256, rows), jnp.bfloat16)],
        compiler_params=params(32),
        name="send_half",
    )(embed, proj, slope, pooled)


def keep_half(dconv, qk, pooled):
    size, rows = qk.shape[1], pooled.shape[1]
    return pl.pallas_call(
        keep_kernel,
        out_shape=jax.ShapeDtypeStruct((size, WIDE), jnp.float32),
        scratch_shapes=[pltpu.VMEM((256, rows), jnp.bfloat16)],
        compiler_params=params(32),
        cost_estimate=pl.CostEstimate(
            flops=2 * K1 * size * C0 * rows, bytes_accessed=12 * MIB, transcendentals=0
        ),
        name="keep_half",
    )(dconv, qk, pooled)


def add_kernel(a_ref, b_ref, out_ref):
    if a_ref.dtype == jnp.int16:
        a = decode(a_ref)
    else:
        a = [a_ref[:, begin:end] for begin, end in PARTS]
    encode([x + y for x, y in zip(a, decode(b_ref))], out_ref)


def add_half(a, b):
    return pl.pallas_call(
        add_kernel,
        out_shape=jax.ShapeDtypeStruct(b.shape, jnp.int16),
        compiler_params=params(8),
        name="add_half",
    )(a, b)


def join_kernel(mine_ref, other_ref, conv_ref, query_ref, key_ref):
    size = mine_ref.shape[0]
    core = lax.axis_index("dp") % 2
    for half, ref in ((core, mine_ref), (1 - core, other_ref)):
        rows = pl.ds(pl.multiple_of(half * size, 8), size)
        for x, out_ref in zip(decode(ref), (conv_ref, query_ref, key_ref)):
            out_ref[rows, :] = x


def join(mine, other):
    co = 2 * mine.shape[0]
    return pl.pallas_call(
        join_kernel,
        out_shape=[
            jax.ShapeDtypeStruct((co, K1 * C0), jnp.float32),
            jax.ShapeDtypeStruct((co, PC), jnp.float32),
            jax.ShapeDtypeStruct((co, PC), jnp.float32),
        ],
        compiler_params=params(8),
        name="join",
    )(mine, other)


def body(bases, stem_table, conv_weight, query_weight, key_weight, pair_grad):
    n = lax.axis_size("seq")
    rows_dev = bases.shape[1] // POOL

    own = bases.astype(jnp.bfloat16).reshape(2, rows_dev // 2, POOL).transpose(0, 2, 1)
    payload = gather_xor(own.reshape(2 * POOL, rows_dev // 2), "seq")

    first_table = jnp.pad(
        stem_table.transpose(2, 1, 0), ((0, 0), (0, 0), (1, WINDOW - 1 - K0))
    ).reshape(C0, 4 * WINDOW)
    first_table = jnp.pad(first_table, ((0, 0), (0, 128 - 4 * WINDOW))).astype(jnp.float32)
    table, weights, proj = prepare(n, first_table, conv_weight, query_weight, key_weight)

    pooled, slope, embed = stem_and_conv(n, payload, table, weights, pair_grad[0])
    embed_all = gather_direct(embed, "seq")
    send, dconv, qk = send_half(n, embed_all, proj, slope, pooled)
    received = swap(send, "dp", 1)
    keep = keep_half(dconv, qk, pooled)

    mine = add_half(keep, received)
    bit = 2
    while bit < lax.axis_size("dp"):
        mine = add_half(mine, swap(mine, "dp", bit))
        bit *= 2
    return tuple(join(mine, swap(mine, "dp", 1)))


def solution(mesh):
    return jax.shard_map(
        body,
        mesh=mesh,
        in_specs=(P("dp", "seq"), P(), P("seq", None), P(), P(), P("dp", "seq", None)),
        out_specs=(P("seq", None), P("seq", None), P("seq", None)),
        check_vma=False,
    )
```

```python
import functools

import jax
import jax.numpy as jnp
from jax import lax
from jax.experimental import pallas as pl
from jax.experimental.pallas import tpu as pltpu
from jax.sharding import PartitionSpec as P

C0 = 768
C1 = 768
PC = 128
K0 = 15
K1 = 5
POOL = 8
BIN_ROWS = 256
WINDOW = 24
CHUNK = 64
BLOCK = 512
LAG = 3
PAD = 128
SLOT = 128

ROOT = 0.7978845608028654
CUBE = 0.044715
HIGH = lax.Precision.HIGHEST
MIB = 1024 * 1024


def params(mib):
    return pltpu.CompilerParams(vmem_limit_bytes=mib * MIB)


def swap(x, axis, bit):
    size = lax.axis_size(axis)
    return lax.ppermute(x, axis, [(i, i ^ bit) for i in range(size)])


def gather_xor(x, axis):
    x = x[None]
    bit = 1
    while bit < lax.axis_size(axis):
        x = jnp.concatenate([x, swap(x, axis, bit)], axis=0)
        bit *= 2
    return x


def gather_direct(x, axis):
    return lax.all_to_all(jnp.broadcast_to(x[None], (lax.axis_size(axis),) + x.shape), axis, 0, 0)


def twice_gelu(v):
    return v + v * jnp.tanh(v * (ROOT + (ROOT * CUBE) * (v * v)))


def prepare_kernel(n, co, t0_ref, w_ref, wq_ref, wk_ref, table_ref, weights_ref, proj_ref):
    for chunk in range(C0 // CHUNK):
        part = t0_ref[chunk * CHUNK : (chunk + 1) * CHUNK, :]
        for pos in range(POOL):
            shifted = part if pos == 0 else pltpu.roll(part, pos, 1)
            first = (chunk * POOL + pos) * CHUNK
            table_ref[first : first + CHUNK, :] = shifted.astype(jnp.bfloat16)
    for tap in range(K1):
        weights_ref[tap * co : (tap + 1) * co, :] = w_ref[:, tap * C0 : (tap + 1) * C0] * 0.5
    for slot in range(n):
        rows = slice(slot * co, (slot + 1) * co)
        proj_ref[slot * SLOT : slot * SLOT + co, :PC] = wq_ref[rows, :]
        proj_ref[slot * SLOT : slot * SLOT + co, PC:] = wk_ref[rows, :]
        proj_ref[slot * SLOT + co : (slot + 1) * SLOT, :] = jnp.zeros(
            (SLOT - co, 2 * PC), jnp.bfloat16
        )


def prepare(n, first_table, conv_weight, query_weight, key_weight):
    co = conv_weight.shape[0]
    return pl.pallas_call(
        functools.partial(prepare_kernel, n, co),
        out_shape=[
            jax.ShapeDtypeStruct((POOL * C0, 128), jnp.bfloat16),
            jax.ShapeDtypeStruct((K1 * co, C0), jnp.bfloat16),
            jax.ShapeDtypeStruct((n * SLOT, 2 * PC), jnp.bfloat16),
        ],
        compiler_params=params(8),
        cost_estimate=pl.CostEstimate(flops=0, bytes_accessed=5 * MIB, transcendentals=0),
        name="prepare",
    )(first_table, conv_weight, query_weight, key_weight)


def stem_kernel(
    n, rows_dev, co, pay_ref, table_ref, weights_ref, grad_ref, p_ref, slope_ref, emb_ref,
    table, weights, bases, ybuf, prev, sums, sa, sb, slopes, codes
):
    step = pl.program_id(0)
    rows = n * rows_dev
    blocks = rows // BLOCK
    front = LAG * BLOCK + PAD
    piece = 256

    def convolve(block):
        first = pl.multiple_of((block + LAG) * BLOCK, 128)
        conv = None
        for tap in range(K1):
            near = ybuf[tap * co : (tap + 1) * co, pl.ds(first, BLOCK + 2 * PAD)]
            begin = PAD + tap - K1 // 2
            part = near[:, begin : begin + BLOCK]
            conv = part if conv is None else conv + part
        square = conv * conv
        tangent = jnp.tanh(conv * (ROOT + (ROOT * CUBE) * square))
        half = 0.5 * conv
        gelu = half + half * tangent
        slopes[...] = (0.5 + 0.5 * tangent) + half * (1.0 - tangent * tangent) * (
            ROOT + (3.0 * ROOT * CUBE) * square
        )
        lane = lax.broadcasted_iota(jnp.int32, (co, 128), 1)
        total = sums[:co, :]
        for part in range(BLOCK // BIN_ROWS):
            mean = jnp.sum(
                gelu[:, part * BIN_ROWS : (part + 1) * BIN_ROWS], axis=1, keepdims=True
            ) * (1.0 / BIN_ROWS)
            total = jnp.where(lane == block * (BLOCK // BIN_ROWS) + part, mean, total)
        sums[:co, :] = total

    def taps(block):
        ybuf[:, pl.ds(pl.multiple_of(front + block * BLOCK, 128), BLOCK)] = jnp.dot(
            weights[...], prev[...], preferred_element_type=jnp.float32
        )

    @pl.when(step == 0)
    def _():
        me = lax.axis_index("seq")
        bases[:, :PAD] = jnp.full((POOL, PAD), -1.0, jnp.float32)
        bases[:, PAD + rows :] = jnp.full((POOL, PAD), -1.0, jnp.float32)
        half = rows_dev // 2
        for slab in range(n):
            block = pay_ref[jnp.bitwise_xor(me, slab)].astype(jnp.float32)
            first = PAD + slab * rows_dev
            bases[:, first : first + half] = block[:POOL]
            bases[:, first + half : first + 2 * half] = block[POOL:]
        table[...] = table_ref[...]
        weights[...] = weights_ref[...]
        ybuf[:, front + rows :] = jnp.zeros((K1 * co, PAD), jnp.float32)
        prev[...] = jnp.zeros(prev.shape, jnp.bfloat16)
        sums[...] = jnp.zeros(sums.shape, jnp.float32)

    @pl.when(step < blocks)
    def _():
        first = pl.multiple_of(step * BLOCK, 128)
        near = bases[:, pl.ds(first, BLOCK + 2 * PAD)]
        window = jnp.concatenate(
            [near[:, PAD + q : PAD + q + BLOCK] for q in (-1, 0, 1)], axis=0
        )
        onehot = jnp.concatenate(
            [(window == b).astype(jnp.float32) for b in range(4)]
            + [jnp.zeros((128 - 4 * WINDOW, BLOCK), jnp.float32)],
            axis=0,
        ).astype(jnp.bfloat16)
        convolve(step - LAG)
        taps(step - 1)
        codes[...] = onehot

        def multiply(chunk, at, stage):
            first = pl.multiple_of(chunk * (POOL * CHUNK), POOL * CHUNK)
            stage[...] = jnp.dot(
                table[pl.ds(first, POOL * CHUNK), :],
                codes[:, at : at + piece],
                preferred_element_type=jnp.float32,
            )

        def pool(chunk, at, stage):
            for row in range(0, CHUNK, 16):
                most = least = stage[row : row + 16, :]
                for pos in range(1, POOL):
                    part = stage[pos * CHUNK + row : pos * CHUNK + row + 16, :]
                    most = jnp.maximum(most, part)
                    least = jnp.minimum(least, part)
                to = pl.multiple_of(chunk * CHUNK + row, 16)
                prev[pl.ds(to, 16), at : at + piece] = jnp.maximum(
                    twice_gelu(most), twice_gelu(least)
                ).astype(jnp.bfloat16)

        chunks = C0 // CHUNK
        multiply(0, 0, sa)

        def turn(chunk, carry):
            multiply(chunk, piece, sb)
            pool(chunk, 0, sa)
            multiply(jnp.minimum(chunk + 1, chunks - 1), 0, sa)
            pool(chunk, piece, sb)
            return carry

        lax.fori_loop(0, chunks, turn, 0)
        p_ref[...] = prev[...]
        slope_ref[...] = slopes[...]

    @pl.when(step >= blocks)
    def _():
        @pl.when(step == blocks)
        def _():
            taps(blocks - 1)

        convolve(step - LAG)
        slope_ref[...] = slopes[...]

    @pl.when(step == blocks + LAG - 1)
    def _():
        own_pos, npos = grad_ref.shape
        embed = sums[...].T[:npos, :].astype(jnp.bfloat16).astype(jnp.float32)
        rest = grad_ref[...]
        parts = []
        for _ in range(3):
            part = rest.astype(jnp.bfloat16).astype(jnp.float32)
            parts.append(part)
            rest = rest - part
        grads = jnp.concatenate(
            parts + [jnp.zeros((npos - 3 * own_pos, npos), jnp.float32)], axis=0
        )
        emb_ref[...] = jnp.concatenate(
            [embed[:, :co], grads, jnp.zeros((npos, SLOT - co - npos), jnp.float32)], axis=1
        ).astype(jnp.bfloat16)


def stem_and_conv(n, payload, table, weights, pair_grad):
    co = weights.shape[0] // K1
    rows_dev = payload.shape[2] * 2
    rows = n * rows_dev
    npos = rows // BIN_ROWS
    blocks = rows // BLOCK
    whole = lambda i: (0, 0)
    return pl.pallas_call(
        functools.partial(stem_kernel, n, rows_dev, co),
        grid=(blocks + LAG,),
        in_specs=[
            pl.BlockSpec(payload.shape, lambda i: (0, 0, 0)),
            pl.BlockSpec(table.shape, whole),
            pl.BlockSpec(weights.shape, whole),
            pl.BlockSpec(pair_grad.shape, whole),
        ],
        out_specs=[
            pl.BlockSpec((C0, BLOCK), lambda i: (0, jnp.minimum(i, blocks - 1))),
            pl.BlockSpec((co, BLOCK), lambda i: (0, jnp.maximum(i - LAG, 0))),
            pl.BlockSpec((npos, SLOT), whole),
        ],
        out_shape=[
            jax.ShapeDtypeStruct((C0, rows), jnp.bfloat16),
            jax.ShapeDtypeStruct((co, rows), jnp.float32),
            jax.ShapeDtypeStruct((npos, SLOT), jnp.bfloat16),
        ],
        scratch_shapes=[
            pltpu.VMEM(table.shape, jnp.bfloat16),
            pltpu.VMEM(weights.shape, jnp.bfloat16),
            pltpu.VMEM((POOL, rows + 2 * PAD), jnp.float32),
            pltpu.VMEM((K1 * co, LAG * BLOCK + rows + 2 * PAD), jnp.float32),
            pltpu.VMEM((C0, BLOCK), jnp.bfloat16),
            pltpu.VMEM((128, 128), jnp.float32),
            pltpu.VMEM((POOL * CHUNK, 256), jnp.float32),
            pltpu.VMEM((POOL * CHUNK, 256), jnp.float32),
            pltpu.VMEM((co, BLOCK), jnp.float32),
            pltpu.VMEM((128, BLOCK), jnp.bfloat16),
        ],
        compiler_params=params(36),
        name="stem_and_conv",
    )(payload, table, weights, pair_grad)


WIDE = K1 * C0 + 2 * PC
PARTS = ((0, K1 * C0), (K1 * C0, K1 * C0 + PC), (K1 * C0 + PC, WIDE))
CODED = WIDE + 128


def encode(values, out_ref):
    exponents = []
    for (begin, end), x in zip(PARTS, values):
        top = jnp.maximum(jnp.max(jnp.abs(x), axis=1, keepdims=True), 1e-30)
        exponent = jnp.floor(jnp.log2(32000.0 / top))
        scaled = jnp.floor(x * jnp.exp2(exponent) + 0.5)
        out_ref[:, begin:end] = scaled.astype(jnp.int32).astype(jnp.int16)
        exponents.append(exponent)
    lane = lax.broadcasted_iota(jnp.int32, (out_ref.shape[0], 128), 1)
    packed = jnp.where(lane == 0, exponents[0], jnp.where(lane == 1, exponents[1], exponents[2]))
    out_ref[:, WIDE:] = packed.astype(jnp.int32).astype(jnp.int16)


def decode(ref):
    exponents = ref[:, WIDE:].astype(jnp.int32).astype(jnp.float32)
    return [
        ref[:, begin:end].astype(jnp.int32).astype(jnp.float32) * jnp.exp2(-exponents[:, at : at + 1])
        for at, (begin, end) in enumerate(PARTS)
    ]


def half_gradient(half, dconv, qk_ref, pooled_ref, out_ref, shifted):
    size = out_ref.shape[0]
    held = dconv.shape[1]
    rows = pooled_ref.shape[1]
    shifted[K1 * held :, :] = jnp.zeros((shifted.shape[0] - K1 * held, rows), jnp.bfloat16)
    for first in range(0, rows, BLOCK):
        near = dconv[half, :, first : first + BLOCK + 2 * PAD]
        for tap in range(K1):
            begin = PAD - tap + K1 // 2
            shifted[tap * held : (tap + 1) * held, first : first + BLOCK] = near[
                :, begin : begin + BLOCK
            ]
    product = lax.dot_general(
        pooled_ref[...], shifted[...], (((1,), (1,)), ((), ())), preferred_element_type=jnp.float32
    ).T
    conv = jnp.concatenate(
        [product[tap * held : tap * held + size, :] for tap in range(K1)], axis=1
    )
    if out_ref.dtype == jnp.int16:
        qk = qk_ref[half]
        encode((conv, qk[:, :PC], qk[:, PC:]), out_ref)
    else:
        out_ref[:, : K1 * C0] = conv
        out_ref[:, K1 * C0 :] = qk_ref[half]


def send_kernel(n, emb_ref, proj_ref, slope_ref, pooled_ref, send_ref, dconv_ref, qk_ref, shifted):
    co, rows = slope_ref.shape
    size, held = co // 2, dconv_ref.shape[1]
    npos = rows // BIN_ROWS
    own_pos = npos // n
    scale = PC**-0.5
    me = lax.axis_index("seq")
    both = jnp.dot(
        jnp.concatenate([emb_ref[slot] for slot in range(n)], axis=1),
        proj_ref[...],
        preferred_element_type=jnp.float32,
    )
    query, keys = both[:, :PC], both[:, PC:]
    pieces = []
    for slab in range(n):
        block = emb_ref[slab].astype(jnp.float32)
        total = block[:own_pos]
        for part in range(1, 3):
            total = total + block[part * own_pos : (part + 1) * own_pos]
        pieces.append(total)
    grad = jnp.concatenate(pieces, axis=0)[:, co : co + npos]
    dquery = jnp.dot(grad, keys, precision=HIGH, preferred_element_type=jnp.float32) * scale
    dkeys = (
        lax.dot_general(
            grad, query, (((0,), (0,)), ((), ())), precision=HIGH,
            preferred_element_type=jnp.float32,
        )
        * scale
    )
    cotangent = jnp.concatenate([dquery, dkeys], axis=1)
    own = pl.ds(pl.multiple_of(me * SLOT, SLOT), SLOT)
    dembed = lax.dot_general(
        proj_ref[own, :].astype(jnp.float32), cotangent,
        (((1,), (1,)), ((), ())), precision=HIGH, preferred_element_type=jnp.float32,
    ) * (0.5 / BIN_ROWS)
    qk = lax.dot_general(
        emb_ref[me].astype(jnp.float32), cotangent, (((0,), (0,)), ((), ())),
        precision=HIGH, preferred_element_type=jnp.float32,
    )
    edge = jnp.zeros((held, PAD), jnp.bfloat16)
    for half in range(2):
        channels = slice(half * size, (half + 1) * size)
        qk_ref[half] = qk[channels]
        dconv_ref[half, :, :PAD] = edge
        dconv_ref[half, :, PAD + rows :] = edge
        for pos in range(npos):
            part = slope_ref[channels, pos * BIN_ROWS : (pos + 1) * BIN_ROWS] * dembed[
                channels, pos : pos + 1
            ]
            if held > size:
                part = jnp.concatenate(
                    [part, jnp.zeros((held - size, BIN_ROWS), jnp.float32)], axis=0
                )
            dconv_ref[half, :, PAD + pos * BIN_ROWS : PAD + (pos + 1) * BIN_ROWS] = part.astype(
                jnp.bfloat16
            )
    half_gradient(1 - lax.axis_index("dp") % 2, dconv_ref, qk_ref, pooled_ref, send_ref, shifted)


def keep_kernel(dconv_ref, qk_ref, pooled_ref, keep_ref, shifted):
    half_gradient(lax.axis_index("dp") % 2, dconv_ref, qk_ref, pooled_ref, keep_ref, shifted)


def send_half(n, embed, proj, slope, pooled):
    co, rows = slope.shape
    size = co // 2
    held = -(-size // 16) * 16
    return pl.pallas_call(
        functools.partial(send_kernel, n),
        out_shape=[
            jax.ShapeDtypeStruct((size, CODED), jnp.int16),
            jax.ShapeDtypeStruct((2, held, rows + 2 * PAD), jnp.bfloat16),
            jax.ShapeDtypeStruct((2, size, 2 * PC), jnp.float32),
        ],
        scratch_shapes=[pltpu.VMEM((256, rows), jnp.bfloat16)],
        compiler_params=params(32),
        name="send_half",
    )(embed, proj, slope, pooled)


def keep_half(dconv, qk, pooled):
    size, rows = qk.shape[1], pooled.shape[1]
    return pl.pallas_call(
        keep_kernel,
        out_shape=jax.ShapeDtypeStruct((size, WIDE), jnp.float32),
        scratch_shapes=[pltpu.VMEM((256, rows), jnp.bfloat16)],
        compiler_params=params(32),
        cost_estimate=pl.CostEstimate(
            flops=2 * K1 * size * C0 * rows, bytes_accessed=12 * MIB, transcendentals=0
        ),
        name="keep_half",
    )(dconv, qk, pooled)


def add_kernel(a_ref, b_ref, out_ref):
    if a_ref.dtype == jnp.int16:
        a = decode(a_ref)
    else:
        a = [a_ref[:, begin:end] for begin, end in PARTS]
    encode([x + y for x, y in zip(a, decode(b_ref))], out_ref)


def add_half(a, b):
    return pl.pallas_call(
        add_kernel,
        out_shape=jax.ShapeDtypeStruct(b.shape, jnp.int16),
        compiler_params=params(8),
        name="add_half",
    )(a, b)


def join_kernel(mine_ref, other_ref, conv_ref, query_ref, key_ref):
    size = mine_ref.shape[0]
    core = lax.axis_index("dp") % 2
    for half, ref in ((core, mine_ref), (1 - core, other_ref)):
        rows = pl.ds(pl.multiple_of(half * size, 8), size)
        for x, out_ref in zip(decode(ref), (conv_ref, query_ref, key_ref)):
            out_ref[rows, :] = x


def join(mine, other):
    co = 2 * mine.shape[0]
    return pl.pallas_call(
        join_kernel,
        out_shape=[
            jax.ShapeDtypeStruct((co, K1 * C0), jnp.float32),
            jax.ShapeDtypeStruct((co, PC), jnp.float32),
            jax.ShapeDtypeStruct((co, PC), jnp.float32),
        ],
        compiler_params=params(8),
        name="join",
    )(mine, other)


def body(bases, stem_table, conv_weight, query_weight, key_weight, pair_grad):
    n = lax.axis_size("seq")
    rows_dev = bases.shape[1] // POOL

    own = bases.astype(jnp.bfloat16).reshape(2, rows_dev // 2, POOL).transpose(0, 2, 1)
    payload = gather_xor(own.reshape(2 * POOL, rows_dev // 2), "seq")

    first_table = jnp.pad(
        stem_table.transpose(2, 1, 0), ((0, 0), (0, 0), (1, WINDOW - 1 - K0))
    ).reshape(C0, 4 * WINDOW)
    first_table = jnp.pad(first_table, ((0, 0), (0, 128 - 4 * WINDOW))).astype(jnp.float32)
    table, weights, proj = prepare(n, first_table, conv_weight, query_weight, key_weight)

    pooled, slope, embed = stem_and_conv(n, payload, table, weights, pair_grad[0])
    embed_all = gather_direct(embed, "seq")
    send, dconv, qk = send_half(n, embed_all, proj, slope, pooled)
    received = swap(send, "dp", 1)
    keep = keep_half(dconv, qk, pooled)

    mine = add_half(keep, received)
    bit = 2
    while bit < lax.axis_size("dp"):
        mine = add_half(mine, swap(mine, "dp", bit))
        bit *= 2
    return tuple(join(mine, swap(mine, "dp", 1)))


def solution(mesh):
    return jax.shard_map(
        body,
        mesh=mesh,
        in_specs=(P("dp", "seq"), P(), P("seq", None), P(), P(), P("dp", "seq", None)),
        out_specs=(P("seq", None), P("seq", None), P("seq", None)),
        check_vma=False,
    )
```

```python
import functools

import jax
import jax.numpy as jnp
from jax import lax
from jax.experimental import pallas as pl
from jax.experimental.pallas import tpu as pltpu
from jax.sharding import PartitionSpec as P

C0 = 768
C1 = 768
PC = 128
K0 = 15
K1 = 5
POOL = 8
BIN_ROWS = 256
WINDOW = 24
CHUNK = 128
BLOCK = 512
LAG = 3
PAD = 128
SLOT = 128

ROOT = 0.7978845608028654
CUBE = 0.044715
HIGH = lax.Precision.HIGHEST
MIB = 1024 * 1024


def params(mib):
    return pltpu.CompilerParams(vmem_limit_bytes=mib * MIB)


def swap(x, axis, bit):
    size = lax.axis_size(axis)
    return lax.ppermute(x, axis, [(i, i ^ bit) for i in range(size)])


def gather_xor(x, axis):
    x = x[None]
    bit = 1
    while bit < lax.axis_size(axis):
        x = jnp.concatenate([x, swap(x, axis, bit)], axis=0)
        bit *= 2
    return x


def gather_direct(x, axis):
    return lax.all_to_all(jnp.broadcast_to(x[None], (lax.axis_size(axis),) + x.shape), axis, 0, 0)


def twice_gelu(v):
    return v + v * jnp.tanh(v * (ROOT + (ROOT * CUBE) * (v * v)))


def prepare_kernel(n, co, t0_ref, w_ref, wq_ref, wk_ref, table_ref, weights_ref, proj_ref):
    for chunk in range(C0 // CHUNK):
        part = t0_ref[chunk * CHUNK : (chunk + 1) * CHUNK, :]
        for pos in range(POOL):
            shifted = part if pos == 0 else pltpu.roll(part, pos, 1)
            first = (chunk * POOL + pos) * CHUNK
            table_ref[first : first + CHUNK, :] = shifted.astype(jnp.bfloat16)
    for tap in range(K1):
        weights_ref[tap * co : (tap + 1) * co, :] = w_ref[:, tap * C0 : (tap + 1) * C0] * 0.5
    for slot in range(n):
        rows = slice(slot * co, (slot + 1) * co)
        proj_ref[slot * SLOT : slot * SLOT + co, :PC] = wq_ref[rows, :]
        proj_ref[slot * SLOT : slot * SLOT + co, PC:] = wk_ref[rows, :]
        proj_ref[slot * SLOT + co : (slot + 1) * SLOT, :] = jnp.zeros(
            (SLOT - co, 2 * PC), jnp.bfloat16
        )


def prepare(n, first_table, conv_weight, query_weight, key_weight):
    co = conv_weight.shape[0]
    return pl.pallas_call(
        functools.partial(prepare_kernel, n, co),
        out_shape=[
            jax.ShapeDtypeStruct((POOL * C0, 128), jnp.bfloat16),
            jax.ShapeDtypeStruct((K1 * co, C0), jnp.bfloat16),
            jax.ShapeDtypeStruct((n * SLOT, 2 * PC), jnp.bfloat16),
        ],
        compiler_params=params(8),
        cost_estimate=pl.CostEstimate(flops=0, bytes_accessed=5 * MIB, transcendentals=0),
        name="prepare",
    )(first_table, conv_weight, query_weight, key_weight)


def stem_kernel(
    n, rows_dev, co, pay_ref, table_ref, weights_ref, grad_ref, p_ref, slope_ref, emb_ref,
    table, weights, bases, ybuf, prev, sums, sa, sb, slopes
):
    step = pl.program_id(0)
    rows = n * rows_dev
    blocks = rows // BLOCK
    front = LAG * BLOCK + PAD

    def convolve(block):
        first = pl.multiple_of((block + LAG) * BLOCK, 128)
        conv = None
        for tap in range(K1):
            near = ybuf[tap * co : (tap + 1) * co, pl.ds(first, BLOCK + 2 * PAD)]
            begin = PAD + tap - K1 // 2
            part = near[:, begin : begin + BLOCK]
            conv = part if conv is None else conv + part
        square = conv * conv
        tangent = jnp.tanh(conv * (ROOT + (ROOT * CUBE) * square))
        half = 0.5 * conv
        gelu = half + half * tangent
        slopes[...] = (0.5 + 0.5 * tangent) + half * (1.0 - tangent * tangent) * (
            ROOT + (3.0 * ROOT * CUBE) * square
        )
        lane = lax.broadcasted_iota(jnp.int32, (co, 128), 1)
        total = sums[:co, :]
        for part in range(BLOCK // BIN_ROWS):
            mean = jnp.sum(
                gelu[:, part * BIN_ROWS : (part + 1) * BIN_ROWS], axis=1, keepdims=True
            ) * (1.0 / BIN_ROWS)
            total = jnp.where(lane == block * (BLOCK // BIN_ROWS) + part, mean, total)
        sums[:co, :] = total

    def taps(block):
        ybuf[:, pl.ds(pl.multiple_of(front + block * BLOCK, 128), BLOCK)] = jnp.dot(
            weights[...], prev[...], preferred_element_type=jnp.float32
        )

    @pl.when(step == 0)
    def _():
        me = lax.axis_index("seq")
        bases[:, :PAD] = jnp.full((POOL, PAD), -1.0, jnp.float32)
        bases[:, PAD + rows :] = jnp.full((POOL, PAD), -1.0, jnp.float32)
        half = rows_dev // 2
        for slab in range(n):
            block = pay_ref[jnp.bitwise_xor(me, slab)].astype(jnp.float32)
            first = PAD + slab * rows_dev
            bases[:, first : first + half] = block[:POOL]
            bases[:, first + half : first + 2 * half] = block[POOL:]
        table[...] = table_ref[...]
        weights[...] = weights_ref[...]
        ybuf[:, front + rows :] = jnp.zeros((K1 * co, PAD), jnp.float32)
        prev[...] = jnp.zeros(prev.shape, jnp.bfloat16)
        sums[...] = jnp.zeros(sums.shape, jnp.float32)

    @pl.when(step < blocks)
    def _():
        first = pl.multiple_of(step * BLOCK, 128)
        near = bases[:, pl.ds(first, BLOCK + 2 * PAD)]
        window = jnp.concatenate(
            [near[:, PAD + q : PAD + q + BLOCK] for q in (-1, 0, 1)], axis=0
        )
        onehot = jnp.concatenate(
            [(window == b).astype(jnp.float32) for b in range(4)]
            + [jnp.zeros((128 - 4 * WINDOW, BLOCK), jnp.float32)],
            axis=0,
        ).astype(jnp.bfloat16)
        convolve(step - LAG)
        taps(step - 1)
        stage = (sa, sb)

        def multiply(chunk):
            stage[chunk % 2][...] = jnp.dot(
                table[chunk * POOL * CHUNK : (chunk + 1) * POOL * CHUNK, :],
                onehot,
                preferred_element_type=jnp.float32,
            )

        def pool(chunk):
            stem = stage[chunk % 2]
            for row in range(0, CHUNK, 16):
                for at in range(0, BLOCK, 256):
                    most = least = stem[row : row + 16, at : at + 256]
                    for pos in range(1, POOL):
                        part = stem[pos * CHUNK + row : pos * CHUNK + row + 16, at : at + 256]
                        most = jnp.maximum(most, part)
                        least = jnp.minimum(least, part)
                    prev[chunk * CHUNK + row : chunk * CHUNK + row + 16, at : at + 256] = (
                        jnp.maximum(twice_gelu(most), twice_gelu(least)).astype(jnp.bfloat16)
                    )

        chunks = C0 // CHUNK
        multiply(0)
        for chunk in range(chunks):
            if chunk + 1 < chunks:
                multiply(chunk + 1)
            pool(chunk)
        p_ref[...] = prev[...]
        slope_ref[...] = slopes[...]

    @pl.when(step >= blocks)
    def _():
        @pl.when(step == blocks)
        def _():
            taps(blocks - 1)

        convolve(step - LAG)
        slope_ref[...] = slopes[...]

    @pl.when(step == blocks + LAG - 1)
    def _():
        own_pos, npos = grad_ref.shape
        embed = sums[...].T[:npos, :].astype(jnp.bfloat16).astype(jnp.float32)
        rest = grad_ref[...]
        parts = []
        for _ in range(3):
            part = rest.astype(jnp.bfloat16).astype(jnp.float32)
            parts.append(part)
            rest = rest - part
        grads = jnp.concatenate(
            parts + [jnp.zeros((npos - 3 * own_pos, npos), jnp.float32)], axis=0
        )
        emb_ref[...] = jnp.concatenate(
            [embed[:, :co], grads, jnp.zeros((npos, SLOT - co - npos), jnp.float32)], axis=1
        ).astype(jnp.bfloat16)


def stem_and_conv(n, payload, table, weights, pair_grad):
    co = weights.shape[0] // K1
    rows_dev = payload.shape[2] * 2
    rows = n * rows_dev
    npos = rows // BIN_ROWS
    blocks = rows // BLOCK
    whole = lambda i: (0, 0)
    return pl.pallas_call(
        functools.partial(stem_kernel, n, rows_dev, co),
        grid=(blocks + LAG,),
        in_specs=[
            pl.BlockSpec(payload.shape, lambda i: (0, 0, 0)),
            pl.BlockSpec(table.shape, whole),
            pl.BlockSpec(weights.shape, whole),
            pl.BlockSpec(pair_grad.shape, whole),
        ],
        out_specs=[
            pl.BlockSpec((C0, BLOCK), lambda i: (0, jnp.minimum(i, blocks - 1))),
            pl.BlockSpec((co, BLOCK), lambda i: (0, jnp.maximum(i - LAG, 0))),
            pl.BlockSpec((npos, SLOT), whole),
        ],
        out_shape=[
            jax.ShapeDtypeStruct((C0, rows), jnp.bfloat16),
            jax.ShapeDtypeStruct((co, rows), jnp.float32),
            jax.ShapeDtypeStruct((npos, SLOT), jnp.bfloat16),
        ],
        scratch_shapes=[
            pltpu.VMEM(table.shape, jnp.bfloat16),
            pltpu.VMEM(weights.shape, jnp.bfloat16),
            pltpu.VMEM((POOL, rows + 2 * PAD), jnp.float32),
            pltpu.VMEM((K1 * co, LAG * BLOCK + rows + 2 * PAD), jnp.float32),
            pltpu.VMEM((C0, BLOCK), jnp.bfloat16),
            pltpu.VMEM((128, 128), jnp.float32),
            pltpu.VMEM((POOL * CHUNK, BLOCK), jnp.float32),
            pltpu.VMEM((POOL * CHUNK, BLOCK), jnp.float32),
            pltpu.VMEM((co, BLOCK), jnp.float32),
        ],
        compiler_params=params(36),
        name="stem_and_conv",
    )(payload, table, weights, pair_grad)


WIDE = K1 * C0 + 2 * PC
PARTS = ((0, K1 * C0), (K1 * C0, K1 * C0 + PC), (K1 * C0 + PC, WIDE))
CODED = WIDE + 128


def encode(values, out_ref):
    exponents = []
    for (begin, end), x in zip(PARTS, values):
        top = jnp.maximum(jnp.max(jnp.abs(x), axis=1, keepdims=True), 1e-30)
        exponent = jnp.floor(jnp.log2(32000.0 / top))
        scaled = jnp.floor(x * jnp.exp2(exponent) + 0.5)
        out_ref[:, begin:end] = scaled.astype(jnp.int32).astype(jnp.int16)
        exponents.append(exponent)
    lane = lax.broadcasted_iota(jnp.int32, (out_ref.shape[0], 128), 1)
    packed = jnp.where(lane == 0, exponents[0], jnp.where(lane == 1, exponents[1], exponents[2]))
    out_ref[:, WIDE:] = packed.astype(jnp.int32).astype(jnp.int16)


def decode(ref):
    exponents = ref[:, WIDE:].astype(jnp.int32).astype(jnp.float32)
    return [
        ref[:, begin:end].astype(jnp.int32).astype(jnp.float32) * jnp.exp2(-exponents[:, at : at + 1])
        for at, (begin, end) in enumerate(PARTS)
    ]


def half_gradient(half, dconv, qk_ref, pooled_ref, out_ref, shifted):
    size = out_ref.shape[0]
    held = dconv.shape[1]
    rows = pooled_ref.shape[1]
    shifted[K1 * held :, :] = jnp.zeros((shifted.shape[0] - K1 * held, rows), jnp.bfloat16)
    for first in range(0, rows, BLOCK):
        near = dconv[half, :, first : first + BLOCK + 2 * PAD]
        for tap in range(K1):
            begin = PAD - tap + K1 // 2
            shifted[tap * held : (tap + 1) * held, first : first + BLOCK] = near[
                :, begin : begin + BLOCK
            ]
    product = lax.dot_general(
        pooled_ref[...], shifted[...], (((1,), (1,)), ((), ())), preferred_element_type=jnp.float32
    ).T
    conv = jnp.concatenate(
        [product[tap * held : tap * held + size, :] for tap in range(K1)], axis=1
    )
    if out_ref.dtype == jnp.int16:
        qk = qk_ref[half]
        encode((conv, qk[:, :PC], qk[:, PC:]), out_ref)
    else:
        out_ref[:, : K1 * C0] = conv
        out_ref[:, K1 * C0 :] = qk_ref[half]


def send_kernel(n, emb_ref, proj_ref, slope_ref, pooled_ref, send_ref, dconv_ref, qk_ref, shifted):
    co, rows = slope_ref.shape
    size, held = co // 2, dconv_ref.shape[1]
    npos = rows // BIN_ROWS
    own_pos = npos // n
    scale = PC**-0.5
    me = lax.axis_index("seq")
    both = jnp.dot(
        jnp.concatenate([emb_ref[slot] for slot in range(n)], axis=1),
        proj_ref[...],
        preferred_element_type=jnp.float32,
    )
    query, keys = both[:, :PC], both[:, PC:]
    pieces = []
    for slab in range(n):
        block = emb_ref[slab].astype(jnp.float32)
        total = block[:own_pos]
        for part in range(1, 3):
            total = total + block[part * own_pos : (part + 1) * own_pos]
        pieces.append(total)
    grad = jnp.concatenate(pieces, axis=0)[:, co : co + npos]
    dquery = jnp.dot(grad, keys, precision=HIGH, preferred_element_type=jnp.float32) * scale
    dkeys = (
        lax.dot_general(
            grad, query, (((0,), (0,)), ((), ())), precision=HIGH,
            preferred_element_type=jnp.float32,
        )
        * scale
    )
    cotangent = jnp.concatenate([dquery, dkeys], axis=1)
    own = pl.ds(pl.multiple_of(me * SLOT, SLOT), SLOT)
    dembed = lax.dot_general(
        proj_ref[own, :].astype(jnp.float32), cotangent,
        (((1,), (1,)), ((), ())), precision=HIGH, preferred_element_type=jnp.float32,
    ) * (0.5 / BIN_ROWS)
    qk = lax.dot_general(
        emb_ref[me].astype(jnp.float32), cotangent, (((0,), (0,)), ((), ())),
        precision=HIGH, preferred_element_type=jnp.float32,
    )
    edge = jnp.zeros((held, PAD), jnp.bfloat16)
    for half in range(2):
        channels = slice(half * size, (half + 1) * size)
        qk_ref[half] = qk[channels]
        dconv_ref[half, :, :PAD] = edge
        dconv_ref[half, :, PAD + rows :] = edge
        for pos in range(npos):
            part = slope_ref[channels, pos * BIN_ROWS : (pos + 1) * BIN_ROWS] * dembed[
                channels, pos : pos + 1
            ]
            if held > size:
                part = jnp.concatenate(
                    [part, jnp.zeros((held - size, BIN_ROWS), jnp.float32)], axis=0
                )
            dconv_ref[half, :, PAD + pos * BIN_ROWS : PAD + (pos + 1) * BIN_ROWS] = part.astype(
                jnp.bfloat16
            )
    half_gradient(1 - lax.axis_index("dp") % 2, dconv_ref, qk_ref, pooled_ref, send_ref, shifted)


def keep_kernel(dconv_ref, qk_ref, pooled_ref, keep_ref, shifted):
    half_gradient(lax.axis_index("dp") % 2, dconv_ref, qk_ref, pooled_ref, keep_ref, shifted)


def send_half(n, embed, proj, slope, pooled):
    co, rows = slope.shape
    size = co // 2
    held = -(-size // 16) * 16
    return pl.pallas_call(
        functools.partial(send_kernel, n),
        out_shape=[
            jax.ShapeDtypeStruct((size, CODED), jnp.int16),
            jax.ShapeDtypeStruct((2, held, rows + 2 * PAD), jnp.bfloat16),
            jax.ShapeDtypeStruct((2, size, 2 * PC), jnp.float32),
        ],
        scratch_shapes=[pltpu.VMEM((256, rows), jnp.bfloat16)],
        compiler_params=params(32),
        name="send_half",
    )(embed, proj, slope, pooled)


def keep_half(dconv, qk, pooled):
    size, rows = qk.shape[1], pooled.shape[1]
    return pl.pallas_call(
        keep_kernel,
        out_shape=jax.ShapeDtypeStruct((size, WIDE), jnp.float32),
        scratch_shapes=[pltpu.VMEM((256, rows), jnp.bfloat16)],
        compiler_params=params(32),
        cost_estimate=pl.CostEstimate(
            flops=2 * K1 * size * C0 * rows, bytes_accessed=12 * MIB, transcendentals=0
        ),
        name="keep_half",
    )(dconv, qk, pooled)


def add_kernel(a_ref, b_ref, out_ref):
    if a_ref.dtype == jnp.int16:
        a = decode(a_ref)
    else:
        a = [a_ref[:, begin:end] for begin, end in PARTS]
    encode([x + y for x, y in zip(a, decode(b_ref))], out_ref)


def add_half(a, b):
    return pl.pallas_call(
        add_kernel,
        out_shape=jax.ShapeDtypeStruct(b.shape, jnp.int16),
        compiler_params=params(8),
        name="add_half",
    )(a, b)


def join_kernel(mine_ref, other_ref, conv_ref, query_ref, key_ref):
    size = mine_ref.shape[0]
    core = lax.axis_index("dp") % 2
    for half, ref in ((core, mine_ref), (1 - core, other_ref)):
        rows = pl.ds(pl.multiple_of(half * size, 8), size)
        for x, out_ref in zip(decode(ref), (conv_ref, query_ref, key_ref)):
            out_ref[rows, :] = x


def join(mine, other):
    co = 2 * mine.shape[0]
    return pl.pallas_call(
        join_kernel,
        out_shape=[
            jax.ShapeDtypeStruct((co, K1 * C0), jnp.float32),
            jax.ShapeDtypeStruct((co, PC), jnp.float32),
            jax.ShapeDtypeStruct((co, PC), jnp.float32),
        ],
        compiler_params=params(8),
        name="join",
    )(mine, other)


def body(bases, stem_table, conv_weight, query_weight, key_weight, pair_grad):
    n = lax.axis_size("seq")
    rows_dev = bases.shape[1] // POOL

    own = bases.astype(jnp.bfloat16).reshape(2, rows_dev // 2, POOL).transpose(0, 2, 1)
    payload = gather_xor(own.reshape(2 * POOL, rows_dev // 2), "seq")

    first_table = jnp.pad(
        stem_table.transpose(2, 1, 0), ((0, 0), (0, 0), (1, WINDOW - 1 - K0))
    ).reshape(C0, 4 * WINDOW)
    first_table = jnp.pad(first_table, ((0, 0), (0, 128 - 4 * WINDOW))).astype(jnp.float32)
    table, weights, proj = prepare(n, first_table, conv_weight, query_weight, key_weight)

    pooled, slope, embed = stem_and_conv(n, payload, table, weights, pair_grad[0])
    embed_all = gather_direct(embed, "seq")
    send, dconv, qk = send_half(n, embed_all, proj, slope, pooled)
    received = swap(send, "dp", 1)
    keep = keep_half(dconv, qk, pooled)

    mine = add_half(keep, received)
    bit = 2
    while bit < lax.axis_size("dp"):
        mine = add_half(mine, swap(mine, "dp", bit))
        bit *= 2
    return tuple(join(mine, swap(mine, "dp", 1)))


def solution(mesh):
    return jax.shard_map(
        body,
        mesh=mesh,
        in_specs=(P("dp", "seq"), P(), P("seq", None), P(), P(), P("dp", "seq", None)),
        out_specs=(P("seq", None), P("seq", None), P("seq", None)),
        check_vma=False,
    )
```

```python
import functools

import jax
import jax.numpy as jnp
from jax import lax
from jax.experimental import pallas as pl
from jax.experimental.pallas import tpu as pltpu
from jax.sharding import PartitionSpec as P

C0 = 768
C1 = 768
PC = 128
K0 = 15
K1 = 5
POOL = 8
BIN_ROWS = 256
WINDOW = 24
CHUNK = 128
BLOCK = 512
LAG = 3
PAD = 128
SLOT = 128

ROOT = 0.7978845608028654
CUBE = 0.044715
HIGH = lax.Precision.HIGHEST
MIB = 1024 * 1024


def params(mib):
    return pltpu.CompilerParams(vmem_limit_bytes=mib * MIB)


def swap(x, axis, bit):
    size = lax.axis_size(axis)
    return lax.ppermute(x, axis, [(i, i ^ bit) for i in range(size)])


def gather_xor(x, axis):
    x = x[None]
    bit = 1
    while bit < lax.axis_size(axis):
        x = jnp.concatenate([x, swap(x, axis, bit)], axis=0)
        bit *= 2
    return x


def gather_direct(x, axis):
    return lax.all_to_all(jnp.broadcast_to(x[None], (lax.axis_size(axis),) + x.shape), axis, 0, 0)


EXPO = -2.0 * ROOT * 1.4426950408889634


def gelu_ratio(v):
    power = jnp.exp2(v * (EXPO + (EXPO * CUBE) * (v * v)))
    return v * pl.reciprocal(1.0 + power, approx=True)


def prepare_kernel(n, co, t0_ref, w_ref, wq_ref, wk_ref, table_ref, weights_ref, proj_ref):
    for chunk in range(C0 // CHUNK):
        part = t0_ref[chunk * CHUNK : (chunk + 1) * CHUNK, :]
        for pos in range(POOL):
            shifted = part if pos == 0 else pltpu.roll(part, pos, 1)
            first = (chunk * POOL + pos) * CHUNK
            table_ref[first : first + CHUNK, :] = shifted.astype(jnp.bfloat16)
    for tap in range(K1):
        weights_ref[tap * co : (tap + 1) * co, :] = w_ref[:, tap * C0 : (tap + 1) * C0]
    for slot in range(n):
        rows = slice(slot * co, (slot + 1) * co)
        proj_ref[slot * SLOT : slot * SLOT + co, :PC] = wq_ref[rows, :]
        proj_ref[slot * SLOT : slot * SLOT + co, PC:] = wk_ref[rows, :]
        proj_ref[slot * SLOT + co : (slot + 1) * SLOT, :] = jnp.zeros(
            (SLOT - co, 2 * PC), jnp.bfloat16
        )


def prepare(n, first_table, conv_weight, query_weight, key_weight):
    co = conv_weight.shape[0]
    return pl.pallas_call(
        functools.partial(prepare_kernel, n, co),
        out_shape=[
            jax.ShapeDtypeStruct((POOL * C0, 128), jnp.bfloat16),
            jax.ShapeDtypeStruct((K1 * co, C0), jnp.bfloat16),
            jax.ShapeDtypeStruct((n * SLOT, 2 * PC), jnp.bfloat16),
        ],
        compiler_params=params(8),
        cost_estimate=pl.CostEstimate(flops=0, bytes_accessed=5 * MIB, transcendentals=0),
        name="prepare",
    )(first_table, conv_weight, query_weight, key_weight)


def stem_kernel(
    n, rows_dev, co, pay_ref, table_ref, weights_ref, grad_ref, p_ref, slope_ref, emb_ref,
    table, weights, bases, ybuf, prev, sums, sa, sb, slopes
):
    step = pl.program_id(0)
    rows = n * rows_dev
    blocks = rows // BLOCK
    front = LAG * BLOCK + PAD

    def convolve(block):
        first = pl.multiple_of((block + LAG) * BLOCK, 128)
        conv = None
        for tap in range(K1):
            near = ybuf[tap * co : (tap + 1) * co, pl.ds(first, BLOCK + 2 * PAD)]
            begin = PAD + tap - K1 // 2
            part = near[:, begin : begin + BLOCK]
            conv = part if conv is None else conv + part
        square = conv * conv
        tangent = jnp.tanh(conv * (ROOT + (ROOT * CUBE) * square))
        half = 0.5 * conv
        gelu = half + half * tangent
        slopes[...] = (0.5 + 0.5 * tangent) + half * (1.0 - tangent * tangent) * (
            ROOT + (3.0 * ROOT * CUBE) * square
        )
        lane = lax.broadcasted_iota(jnp.int32, (co, 128), 1)
        total = sums[:co, :]
        for part in range(BLOCK // BIN_ROWS):
            mean = jnp.sum(
                gelu[:, part * BIN_ROWS : (part + 1) * BIN_ROWS], axis=1, keepdims=True
            ) * (1.0 / BIN_ROWS)
            total = jnp.where(lane == block * (BLOCK // BIN_ROWS) + part, mean, total)
        sums[:co, :] = total

    def taps(block):
        ybuf[:, pl.ds(pl.multiple_of(front + block * BLOCK, 128), BLOCK)] = jnp.dot(
            weights[...], prev[...], preferred_element_type=jnp.float32
        )

    @pl.when(step == 0)
    def _():
        me = lax.axis_index("seq")
        bases[:, :PAD] = jnp.full((POOL, PAD), -1.0, jnp.float32)
        bases[:, PAD + rows :] = jnp.full((POOL, PAD), -1.0, jnp.float32)
        half = rows_dev // 2
        for slab in range(n):
            block = pay_ref[jnp.bitwise_xor(me, slab)].astype(jnp.float32)
            first = PAD + slab * rows_dev
            bases[:, first : first + half] = block[:POOL]
            bases[:, first + half : first + 2 * half] = block[POOL:]
        table[...] = table_ref[...]
        weights[...] = weights_ref[...]
        ybuf[:, front + rows :] = jnp.zeros((K1 * co, PAD), jnp.float32)
        prev[...] = jnp.zeros(prev.shape, jnp.bfloat16)
        sums[...] = jnp.zeros(sums.shape, jnp.float32)

    @pl.when(step < blocks)
    def _():
        first = pl.multiple_of(step * BLOCK, 128)
        near = bases[:, pl.ds(first, BLOCK + 2 * PAD)]
        window = jnp.concatenate(
            [near[:, PAD + q : PAD + q + BLOCK] for q in (-1, 0, 1)], axis=0
        )
        onehot = jnp.concatenate(
            [(window == b).astype(jnp.float32) for b in range(4)]
            + [jnp.zeros((128 - 4 * WINDOW, BLOCK), jnp.float32)],
            axis=0,
        ).astype(jnp.bfloat16)
        convolve(step - LAG)
        taps(step - 1)
        stage = (sa, sb)

        def multiply(chunk):
            stage[chunk % 2][...] = jnp.dot(
                table[chunk * POOL * CHUNK : (chunk + 1) * POOL * CHUNK, :],
                onehot,
                preferred_element_type=jnp.float32,
            )

        def pool(chunk):
            stem = stage[chunk % 2]
            for row in range(0, CHUNK, 16):
                for at in range(0, BLOCK, 256):
                    most = least = stem[row : row + 16, at : at + 256]
                    for pos in range(1, POOL):
                        part = stem[pos * CHUNK + row : pos * CHUNK + row + 16, at : at + 256]
                        most = jnp.maximum(most, part)
                        least = jnp.minimum(least, part)
                    prev[chunk * CHUNK + row : chunk * CHUNK + row + 16, at : at + 256] = (
                        jnp.maximum(gelu_ratio(most), gelu_ratio(least)).astype(jnp.bfloat16)
                    )

        chunks = C0 // CHUNK
        multiply(0)
        for chunk in range(chunks):
            if chunk + 1 < chunks:
                multiply(chunk + 1)
            pool(chunk)
        p_ref[...] = prev[...]
        slope_ref[...] = slopes[...]

    @pl.when(step >= blocks)
    def _():
        @pl.when(step == blocks)
        def _():
            taps(blocks - 1)

        convolve(step - LAG)
        slope_ref[...] = slopes[...]

    @pl.when(step == blocks + LAG - 1)
    def _():
        own_pos, npos = grad_ref.shape
        embed = sums[...].T[:npos, :].astype(jnp.bfloat16).astype(jnp.float32)
        rest = grad_ref[...]
        parts = []
        for _ in range(3):
            part = rest.astype(jnp.bfloat16).astype(jnp.float32)
            parts.append(part)
            rest = rest - part
        grads = jnp.concatenate(
            parts + [jnp.zeros((npos - 3 * own_pos, npos), jnp.float32)], axis=0
        )
        emb_ref[...] = jnp.concatenate(
            [embed[:, :co], grads, jnp.zeros((npos, SLOT - co - npos), jnp.float32)], axis=1
        ).astype(jnp.bfloat16)


def stem_and_conv(n, payload, table, weights, pair_grad):
    co = weights.shape[0] // K1
    rows_dev = payload.shape[2] * 2
    rows = n * rows_dev
    npos = rows // BIN_ROWS
    blocks = rows // BLOCK
    whole = lambda i: (0, 0)
    return pl.pallas_call(
        functools.partial(stem_kernel, n, rows_dev, co),
        grid=(blocks + LAG,),
        in_specs=[
            pl.BlockSpec(payload.shape, lambda i: (0, 0, 0)),
            pl.BlockSpec(table.shape, whole),
            pl.BlockSpec(weights.shape, whole),
            pl.BlockSpec(pair_grad.shape, whole),
        ],
        out_specs=[
            pl.BlockSpec((C0, BLOCK), lambda i: (0, jnp.minimum(i, blocks - 1))),
            pl.BlockSpec((co, BLOCK), lambda i: (0, jnp.maximum(i - LAG, 0))),
            pl.BlockSpec((npos, SLOT), whole),
        ],
        out_shape=[
            jax.ShapeDtypeStruct((C0, rows), jnp.bfloat16),
            jax.ShapeDtypeStruct((co, rows), jnp.float32),
            jax.ShapeDtypeStruct((npos, SLOT), jnp.bfloat16),
        ],
        scratch_shapes=[
            pltpu.VMEM(table.shape, jnp.bfloat16),
            pltpu.VMEM(weights.shape, jnp.bfloat16),
            pltpu.VMEM((POOL, rows + 2 * PAD), jnp.float32),
            pltpu.VMEM((K1 * co, LAG * BLOCK + rows + 2 * PAD), jnp.float32),
            pltpu.VMEM((C0, BLOCK), jnp.bfloat16),
            pltpu.VMEM((128, 128), jnp.float32),
            pltpu.VMEM((POOL * CHUNK, BLOCK), jnp.float32),
            pltpu.VMEM((POOL * CHUNK, BLOCK), jnp.float32),
            pltpu.VMEM((co, BLOCK), jnp.float32),
        ],
        compiler_params=params(36),
        name="stem_and_conv",
    )(payload, table, weights, pair_grad)


WIDE = K1 * C0 + 2 * PC
PARTS = ((0, K1 * C0), (K1 * C0, K1 * C0 + PC), (K1 * C0 + PC, WIDE))
CODED = WIDE + 128


def encode(values, out_ref):
    exponents = []
    for (begin, end), x in zip(PARTS, values):
        top = jnp.maximum(jnp.max(jnp.abs(x), axis=1, keepdims=True), 1e-30)
        exponent = jnp.floor(jnp.log2(32000.0 / top))
        scaled = jnp.floor(x * jnp.exp2(exponent) + 0.5)
        out_ref[:, begin:end] = scaled.astype(jnp.int32).astype(jnp.int16)
        exponents.append(exponent)
    lane = lax.broadcasted_iota(jnp.int32, (out_ref.shape[0], 128), 1)
    packed = jnp.where(lane == 0, exponents[0], jnp.where(lane == 1, exponents[1], exponents[2]))
    out_ref[:, WIDE:] = packed.astype(jnp.int32).astype(jnp.int16)


def decode(ref):
    exponents = ref[:, WIDE:].astype(jnp.int32).astype(jnp.float32)
    return [
        ref[:, begin:end].astype(jnp.int32).astype(jnp.float32) * jnp.exp2(-exponents[:, at : at + 1])
        for at, (begin, end) in enumerate(PARTS)
    ]


def half_gradient(half, dconv, qk_ref, pooled_ref, out_ref, shifted):
    size = out_ref.shape[0]
    held = dconv.shape[1]
    rows = pooled_ref.shape[1]
    shifted[K1 * held :, :] = jnp.zeros((shifted.shape[0] - K1 * held, rows), jnp.bfloat16)
    for first in range(0, rows, BLOCK):
        near = dconv[half, :, first : first + BLOCK + 2 * PAD]
        for tap in range(K1):
            begin = PAD - tap + K1 // 2
            shifted[tap * held : (tap + 1) * held, first : first + BLOCK] = near[
                :, begin : begin + BLOCK
            ]
    product = lax.dot_general(
        pooled_ref[...], shifted[...], (((1,), (1,)), ((), ())), preferred_element_type=jnp.float32
    ).T
    conv = jnp.concatenate(
        [product[tap * held : tap * held + size, :] for tap in range(K1)], axis=1
    )
    if out_ref.dtype == jnp.int16:
        qk = qk_ref[half]
        encode((conv, qk[:, :PC], qk[:, PC:]), out_ref)
    else:
        out_ref[:, : K1 * C0] = conv
        out_ref[:, K1 * C0 :] = qk_ref[half]


def send_kernel(n, emb_ref, proj_ref, slope_ref, pooled_ref, send_ref, dconv_ref, qk_ref, shifted):
    co, rows = slope_ref.shape
    size, held = co // 2, dconv_ref.shape[1]
    npos = rows // BIN_ROWS
    own_pos = npos // n
    scale = PC**-0.5
    me = lax.axis_index("seq")
    both = jnp.dot(
        jnp.concatenate([emb_ref[slot] for slot in range(n)], axis=1),
        proj_ref[...],
        preferred_element_type=jnp.float32,
    )
    query, keys = both[:, :PC], both[:, PC:]
    pieces = []
    for slab in range(n):
        block = emb_ref[slab].astype(jnp.float32)
        total = block[:own_pos]
        for part in range(1, 3):
            total = total + block[part * own_pos : (part + 1) * own_pos]
        pieces.append(total)
    grad = jnp.concatenate(pieces, axis=0)[:, co : co + npos]
    dquery = jnp.dot(grad, keys, precision=HIGH, preferred_element_type=jnp.float32) * scale
    dkeys = (
        lax.dot_general(
            grad, query, (((0,), (0,)), ((), ())), precision=HIGH,
            preferred_element_type=jnp.float32,
        )
        * scale
    )
    cotangent = jnp.concatenate([dquery, dkeys], axis=1)
    own = pl.ds(pl.multiple_of(me * SLOT, SLOT), SLOT)
    dembed = lax.dot_general(
        proj_ref[own, :].astype(jnp.float32), cotangent,
        (((1,), (1,)), ((), ())), precision=HIGH, preferred_element_type=jnp.float32,
    ) * (1.0 / BIN_ROWS)
    qk = lax.dot_general(
        emb_ref[me].astype(jnp.float32), cotangent, (((0,), (0,)), ((), ())),
        precision=HIGH, preferred_element_type=jnp.float32,
    )
    edge = jnp.zeros((held, PAD), jnp.bfloat16)
    for half in range(2):
        channels = slice(half * size, (half + 1) * size)
        qk_ref[half] = qk[channels]
        dconv_ref[half, :, :PAD] = edge
        dconv_ref[half, :, PAD + rows :] = edge
        for pos in range(npos):
            part = slope_ref[channels, pos * BIN_ROWS : (pos + 1) * BIN_ROWS] * dembed[
                channels, pos : pos + 1
            ]
            if held > size:
                part = jnp.concatenate(
                    [part, jnp.zeros((held - size, BIN_ROWS), jnp.float32)], axis=0
                )
            dconv_ref[half, :, PAD + pos * BIN_ROWS : PAD + (pos + 1) * BIN_ROWS] = part.astype(
                jnp.bfloat16
            )
    half_gradient(1 - lax.axis_index("dp") % 2, dconv_ref, qk_ref, pooled_ref, send_ref, shifted)


def keep_kernel(dconv_ref, qk_ref, pooled_ref, keep_ref, shifted):
    half_gradient(lax.axis_index("dp") % 2, dconv_ref, qk_ref, pooled_ref, keep_ref, shifted)


def send_half(n, embed, proj, slope, pooled):
    co, rows = slope.shape
    size = co // 2
    held = -(-size // 16) * 16
    return pl.pallas_call(
        functools.partial(send_kernel, n),
        out_shape=[
            jax.ShapeDtypeStruct((size, CODED), jnp.int16),
            jax.ShapeDtypeStruct((2, held, rows + 2 * PAD), jnp.bfloat16),
            jax.ShapeDtypeStruct((2, size, 2 * PC), jnp.float32),
        ],
        scratch_shapes=[pltpu.VMEM((256, rows), jnp.bfloat16)],
        compiler_params=params(32),
        name="send_half",
    )(embed, proj, slope, pooled)


def keep_half(dconv, qk, pooled):
    size, rows = qk.shape[1], pooled.shape[1]
    return pl.pallas_call(
        keep_kernel,
        out_shape=jax.ShapeDtypeStruct((size, WIDE), jnp.float32),
        scratch_shapes=[pltpu.VMEM((256, rows), jnp.bfloat16)],
        compiler_params=params(32),
        cost_estimate=pl.CostEstimate(
            flops=2 * K1 * size * C0 * rows, bytes_accessed=12 * MIB, transcendentals=0
        ),
        name="keep_half",
    )(dconv, qk, pooled)


def add_kernel(a_ref, b_ref, out_ref):
    if a_ref.dtype == jnp.int16:
        a = decode(a_ref)
    else:
        a = [a_ref[:, begin:end] for begin, end in PARTS]
    encode([x + y for x, y in zip(a, decode(b_ref))], out_ref)


def add_half(a, b):
    return pl.pallas_call(
        add_kernel,
        out_shape=jax.ShapeDtypeStruct(b.shape, jnp.int16),
        compiler_params=params(8),
        name="add_half",
    )(a, b)


def join_kernel(mine_ref, other_ref, conv_ref, query_ref, key_ref):
    size = mine_ref.shape[0]
    core = lax.axis_index("dp") % 2
    for half, ref in ((core, mine_ref), (1 - core, other_ref)):
        rows = pl.ds(pl.multiple_of(half * size, 8), size)
        for x, out_ref in zip(decode(ref), (conv_ref, query_ref, key_ref)):
            out_ref[rows, :] = x


def join(mine, other):
    co = 2 * mine.shape[0]
    return pl.pallas_call(
        join_kernel,
        out_shape=[
            jax.ShapeDtypeStruct((co, K1 * C0), jnp.float32),
            jax.ShapeDtypeStruct((co, PC), jnp.float32),
            jax.ShapeDtypeStruct((co, PC), jnp.float32),
        ],
        compiler_params=params(8),
        name="join",
    )(mine, other)


def body(bases, stem_table, conv_weight, query_weight, key_weight, pair_grad):
    n = lax.axis_size("seq")
    rows_dev = bases.shape[1] // POOL

    own = bases.astype(jnp.bfloat16).reshape(2, rows_dev // 2, POOL).transpose(0, 2, 1)
    payload = gather_xor(own.reshape(2 * POOL, rows_dev // 2), "seq")

    first_table = jnp.pad(
        stem_table.transpose(2, 1, 0), ((0, 0), (0, 0), (1, WINDOW - 1 - K0))
    ).reshape(C0, 4 * WINDOW)
    first_table = jnp.pad(first_table, ((0, 0), (0, 128 - 4 * WINDOW))).astype(jnp.float32)
    table, weights, proj = prepare(n, first_table, conv_weight, query_weight, key_weight)

    pooled, slope, embed = stem_and_conv(n, payload, table, weights, pair_grad[0])
    embed_all = gather_direct(embed, "seq")
    send, dconv, qk = send_half(n, embed_all, proj, slope, pooled)
    received = swap(send, "dp", 1)
    keep = keep_half(dconv, qk, pooled)

    mine = add_half(keep, received)
    bit = 2
    while bit < lax.axis_size("dp"):
        mine = add_half(mine, swap(mine, "dp", bit))
        bit *= 2
    return tuple(join(mine, swap(mine, "dp", 1)))


def solution(mesh):
    return jax.shard_map(
        body,
        mesh=mesh,
        in_specs=(P("dp", "seq"), P(), P("seq", None), P(), P(), P("dp", "seq", None)),
        out_specs=(P("seq", None), P("seq", None), P("seq", None)),
        check_vma=False,
    )
```

```python
import functools

import jax
import jax.numpy as jnp
from jax import lax
from jax.experimental import pallas as pl
from jax.experimental.pallas import tpu as pltpu
from jax.sharding import PartitionSpec as P

C0 = 768
C1 = 768
PC = 128
K0 = 15
K1 = 5
POOL = 8
BIN_ROWS = 256
WINDOW = 24
CHUNK = 16
BLOCK = 512
LAG = 3
PAD = 128
SLOT = 128

ROOT = 0.7978845608028654
CUBE = 0.044715
HIGH = lax.Precision.HIGHEST
MIB = 1024 * 1024


def params(mib):
    return pltpu.CompilerParams(vmem_limit_bytes=mib * MIB)


def swap(x, axis, bit):
    size = lax.axis_size(axis)
    return lax.ppermute(x, axis, [(i, i ^ bit) for i in range(size)])


def gather_xor(x, axis):
    x = x[None]
    bit = 1
    while bit < lax.axis_size(axis):
        x = jnp.concatenate([x, swap(x, axis, bit)], axis=0)
        bit *= 2
    return x


def gather_direct(x, axis):
    return lax.all_to_all(jnp.broadcast_to(x[None], (lax.axis_size(axis),) + x.shape), axis, 0, 0)


def twice_gelu(v):
    return v + v * jnp.tanh(v * (ROOT + (ROOT * CUBE) * (v * v)))


def prepare_kernel(n, co, t0_ref, w_ref, wq_ref, wk_ref, table_ref, weights_ref, proj_ref):
    for chunk in range(C0 // CHUNK):
        part = t0_ref[chunk * CHUNK : (chunk + 1) * CHUNK, :]
        for pos in range(POOL):
            shifted = part if pos == 0 else pltpu.roll(part, pos, 1)
            first = (chunk * POOL + pos) * CHUNK
            table_ref[first : first + CHUNK, :] = shifted.astype(jnp.bfloat16)
    for tap in range(K1):
        weights_ref[tap * co : (tap + 1) * co, :] = w_ref[:, tap * C0 : (tap + 1) * C0] * 0.5
    for slot in range(n):
        rows = slice(slot * co, (slot + 1) * co)
        proj_ref[slot * SLOT : slot * SLOT + co, :PC] = wq_ref[rows, :]
        proj_ref[slot * SLOT : slot * SLOT + co, PC:] = wk_ref[rows, :]
        proj_ref[slot * SLOT + co : (slot + 1) * SLOT, :] = jnp.zeros(
            (SLOT - co, 2 * PC), jnp.bfloat16
        )


def prepare(n, first_table, conv_weight, query_weight, key_weight):
    co = conv_weight.shape[0]
    return pl.pallas_call(
        functools.partial(prepare_kernel, n, co),
        out_shape=[
            jax.ShapeDtypeStruct((POOL * C0, 128), jnp.bfloat16),
            jax.ShapeDtypeStruct((K1 * co, C0), jnp.bfloat16),
            jax.ShapeDtypeStruct((n * SLOT, 2 * PC), jnp.bfloat16),
        ],
        compiler_params=params(8),
        cost_estimate=pl.CostEstimate(flops=0, bytes_accessed=5 * MIB, transcendentals=0),
        name="prepare",
    )(first_table, conv_weight, query_weight, key_weight)


def stem_kernel(
    n, rows_dev, co, pay_ref, table_ref, weights_ref, grad_ref, p_ref, slope_ref, emb_ref,
    table, weights, bases, ybuf, prev, sums, slopes
):
    step = pl.program_id(0)
    rows = n * rows_dev
    blocks = rows // BLOCK
    front = LAG * BLOCK + PAD

    def convolve(block):
        first = pl.multiple_of((block + LAG) * BLOCK, 128)
        conv = None
        for tap in range(K1):
            near = ybuf[tap * co : (tap + 1) * co, pl.ds(first, BLOCK + 2 * PAD)]
            begin = PAD + tap - K1 // 2
            part = near[:, begin : begin + BLOCK]
            conv = part if conv is None else conv + part
        square = conv * conv
        tangent = jnp.tanh(conv * (ROOT + (ROOT * CUBE) * square))
        half = 0.5 * conv
        gelu = half + half * tangent
        slopes[...] = (0.5 + 0.5 * tangent) + half * (1.0 - tangent * tangent) * (
            ROOT + (3.0 * ROOT * CUBE) * square
        )
        lane = lax.broadcasted_iota(jnp.int32, (co, 128), 1)
        total = sums[:co, :]
        for part in range(BLOCK // BIN_ROWS):
            mean = jnp.sum(
                gelu[:, part * BIN_ROWS : (part + 1) * BIN_ROWS], axis=1, keepdims=True
            ) * (1.0 / BIN_ROWS)
            total = jnp.where(lane == block * (BLOCK // BIN_ROWS) + part, mean, total)
        sums[:co, :] = total

    def taps(block):
        ybuf[:, pl.ds(pl.multiple_of(front + block * BLOCK, 128), BLOCK)] = jnp.dot(
            weights[...], prev[...], preferred_element_type=jnp.float32
        )

    @pl.when(step == 0)
    def _():
        me = lax.axis_index("seq")
        bases[:, :PAD] = jnp.full((POOL, PAD), -1.0, jnp.float32)
        bases[:, PAD + rows :] = jnp.full((POOL, PAD), -1.0, jnp.float32)
        half = rows_dev // 2
        for slab in range(n):
            block = pay_ref[jnp.bitwise_xor(me, slab)].astype(jnp.float32)
            first = PAD + slab * rows_dev
            bases[:, first : first + half] = block[:POOL]
            bases[:, first + half : first + 2 * half] = block[POOL:]
        table[...] = table_ref[...]
        weights[...] = weights_ref[...]
        ybuf[:, front + rows :] = jnp.zeros((K1 * co, PAD), jnp.float32)
        prev[...] = jnp.zeros(prev.shape, jnp.bfloat16)
        sums[...] = jnp.zeros(sums.shape, jnp.float32)

    @pl.when(step < blocks)
    def _():
        first = pl.multiple_of(step * BLOCK, 128)
        near = bases[:, pl.ds(first, BLOCK + 2 * PAD)]
        window = jnp.concatenate(
            [near[:, PAD + q : PAD + q + BLOCK] for q in (-1, 0, 1)], axis=0
        )
        onehot = jnp.concatenate(
            [(window == b).astype(jnp.float32) for b in range(4)]
            + [jnp.zeros((128 - 4 * WINDOW, BLOCK), jnp.float32)],
            axis=0,
        ).astype(jnp.bfloat16)
        convolve(step - LAG)
        taps(step - 1)
        for chunk in range(C0 // CHUNK):
            for at in range(0, BLOCK, 256):
                stem = jnp.dot(
                    table[chunk * POOL * CHUNK : (chunk + 1) * POOL * CHUNK, :],
                    onehot[:, at : at + 256],
                    preferred_element_type=jnp.float32,
                )
                most = least = stem[:CHUNK]
                for pos in range(1, POOL):
                    part = stem[pos * CHUNK : (pos + 1) * CHUNK]
                    most = jnp.maximum(most, part)
                    least = jnp.minimum(least, part)
                prev[chunk * CHUNK : (chunk + 1) * CHUNK, at : at + 256] = jnp.maximum(
                    twice_gelu(most), twice_gelu(least)
                ).astype(jnp.bfloat16)
        p_ref[...] = prev[...]
        slope_ref[...] = slopes[...]

    @pl.when(step >= blocks)
    def _():
        @pl.when(step == blocks)
        def _():
            taps(blocks - 1)

        convolve(step - LAG)
        slope_ref[...] = slopes[...]

    @pl.when(step == blocks + LAG - 1)
    def _():
        own_pos, npos = grad_ref.shape
        embed = sums[...].T[:npos, :].astype(jnp.bfloat16).astype(jnp.float32)
        rest = grad_ref[...]
        parts = []
        for _ in range(3):
            part = rest.astype(jnp.bfloat16).astype(jnp.float32)
            parts.append(part)
            rest = rest - part
        grads = jnp.concatenate(
            parts + [jnp.zeros((npos - 3 * own_pos, npos), jnp.float32)], axis=0
        )
        emb_ref[...] = jnp.concatenate(
            [embed[:, :co], grads, jnp.zeros((npos, SLOT - co - npos), jnp.float32)], axis=1
        ).astype(jnp.bfloat16)


def stem_and_conv(n, payload, table, weights, pair_grad):
    co = weights.shape[0] // K1
    rows_dev = payload.shape[2] * 2
    rows = n * rows_dev
    npos = rows // BIN_ROWS
    blocks = rows // BLOCK
    whole = lambda i: (0, 0)
    return pl.pallas_call(
        functools.partial(stem_kernel, n, rows_dev, co),
        grid=(blocks + LAG,),
        in_specs=[
            pl.BlockSpec(payload.shape, lambda i: (0, 0, 0)),
            pl.BlockSpec(table.shape, whole),
            pl.BlockSpec(weights.shape, whole),
            pl.BlockSpec(pair_grad.shape, whole),
        ],
        out_specs=[
            pl.BlockSpec((C0, BLOCK), lambda i: (0, jnp.minimum(i, blocks - 1))),
            pl.BlockSpec((co, BLOCK), lambda i: (0, jnp.maximum(i - LAG, 0))),
            pl.BlockSpec((npos, SLOT), whole),
        ],
        out_shape=[
            jax.ShapeDtypeStruct((C0, rows), jnp.bfloat16),
            jax.ShapeDtypeStruct((co, rows), jnp.float32),
            jax.ShapeDtypeStruct((npos, SLOT), jnp.bfloat16),
        ],
        scratch_shapes=[
            pltpu.VMEM(table.shape, jnp.bfloat16),
            pltpu.VMEM(weights.shape, jnp.bfloat16),
            pltpu.VMEM((POOL, rows + 2 * PAD), jnp.float32),
            pltpu.VMEM((K1 * co, LAG * BLOCK + rows + 2 * PAD), jnp.float32),
            pltpu.VMEM((C0, BLOCK), jnp.bfloat16),
            pltpu.VMEM((128, 128), jnp.float32),
            pltpu.VMEM((co, BLOCK), jnp.float32),
        ],
        compiler_params=params(36),
        name="stem_and_conv",
    )(payload, table, weights, pair_grad)


WIDE = K1 * C0 + 2 * PC
PARTS = ((0, K1 * C0), (K1 * C0, K1 * C0 + PC), (K1 * C0 + PC, WIDE))
CODED = WIDE + 128


def encode(values, out_ref):
    exponents = []
    for (begin, end), x in zip(PARTS, values):
        top = jnp.maximum(jnp.max(jnp.abs(x), axis=1, keepdims=True), 1e-30)
        exponent = jnp.floor(jnp.log2(32000.0 / top))
        scaled = jnp.floor(x * jnp.exp2(exponent) + 0.5)
        out_ref[:, begin:end] = scaled.astype(jnp.int32).astype(jnp.int16)
        exponents.append(exponent)
    lane = lax.broadcasted_iota(jnp.int32, (out_ref.shape[0], 128), 1)
    packed = jnp.where(lane == 0, exponents[0], jnp.where(lane == 1, exponents[1], exponents[2]))
    out_ref[:, WIDE:] = packed.astype(jnp.int32).astype(jnp.int16)


def decode(ref):
    exponents = ref[:, WIDE:].astype(jnp.int32).astype(jnp.float32)
    return [
        ref[:, begin:end].astype(jnp.int32).astype(jnp.float32) * jnp.exp2(-exponents[:, at : at + 1])
        for at, (begin, end) in enumerate(PARTS)
    ]


def half_gradient(half, dconv, qk_ref, pooled_ref, out_ref, shifted):
    size = out_ref.shape[0]
    held = dconv.shape[1]
    rows = pooled_ref.shape[1]
    shifted[K1 * held :, :] = jnp.zeros((shifted.shape[0] - K1 * held, rows), jnp.bfloat16)
    for first in range(0, rows, BLOCK):
        near = dconv[half, :, first : first + BLOCK + 2 * PAD]
        for tap in range(K1):
            begin = PAD - tap + K1 // 2
            shifted[tap * held : (tap + 1) * held, first : first + BLOCK] = near[
                :, begin : begin + BLOCK
            ]
    product = lax.dot_general(
        pooled_ref[...], shifted[...], (((1,), (1,)), ((), ())), preferred_element_type=jnp.float32
    ).T
    conv = jnp.concatenate(
        [product[tap * held : tap * held + size, :] for tap in range(K1)], axis=1
    )
    if out_ref.dtype == jnp.int16:
        qk = qk_ref[half]
        encode((conv, qk[:, :PC], qk[:, PC:]), out_ref)
    else:
        out_ref[:, : K1 * C0] = conv
        out_ref[:, K1 * C0 :] = qk_ref[half]


def send_kernel(n, emb_ref, proj_ref, slope_ref, pooled_ref, send_ref, dconv_ref, qk_ref, shifted):
    co, rows = slope_ref.shape
    size, held = co // 2, dconv_ref.shape[1]
    npos = rows // BIN_ROWS
    own_pos = npos // n
    scale = PC**-0.5
    me = lax.axis_index("seq")
    both = jnp.dot(
        jnp.concatenate([emb_ref[slot] for slot in range(n)], axis=1),
        proj_ref[...],
        preferred_element_type=jnp.float32,
    )
    query, keys = both[:, :PC], both[:, PC:]
    pieces = []
    for slab in range(n):
        block = emb_ref[slab].astype(jnp.float32)
        total = block[:own_pos]
        for part in range(1, 3):
            total = total + block[part * own_pos : (part + 1) * own_pos]
        pieces.append(total)
    grad = jnp.concatenate(pieces, axis=0)[:, co : co + npos]
    dquery = jnp.dot(grad, keys, precision=HIGH, preferred_element_type=jnp.float32) * scale
    dkeys = (
        lax.dot_general(
            grad, query, (((0,), (0,)), ((), ())), precision=HIGH,
            preferred_element_type=jnp.float32,
        )
        * scale
    )
    cotangent = jnp.concatenate([dquery, dkeys], axis=1)
    own = pl.ds(pl.multiple_of(me * SLOT, SLOT), SLOT)
    dembed = lax.dot_general(
        proj_ref[own, :].astype(jnp.float32), cotangent,
        (((1,), (1,)), ((), ())), precision=HIGH, preferred_element_type=jnp.float32,
    ) * (0.5 / BIN_ROWS)
    qk = lax.dot_general(
        emb_ref[me].astype(jnp.float32), cotangent, (((0,), (0,)), ((), ())),
        precision=HIGH, preferred_element_type=jnp.float32,
    )
    edge = jnp.zeros((held, PAD), jnp.bfloat16)
    for half in range(2):
        channels = slice(half * size, (half + 1) * size)
        qk_ref[half] = qk[channels]
        dconv_ref[half, :, :PAD] = edge
        dconv_ref[half, :, PAD + rows :] = edge
        for pos in range(npos):
            part = slope_ref[channels, pos * BIN_ROWS : (pos + 1) * BIN_ROWS] * dembed[
                channels, pos : pos + 1
            ]
            if held > size:
                part = jnp.concatenate(
                    [part, jnp.zeros((held - size, BIN_ROWS), jnp.float32)], axis=0
                )
            dconv_ref[half, :, PAD + pos * BIN_ROWS : PAD + (pos + 1) * BIN_ROWS] = part.astype(
                jnp.bfloat16
            )
    half_gradient(1 - lax.axis_index("dp") % 2, dconv_ref, qk_ref, pooled_ref, send_ref, shifted)


def keep_kernel(dconv_ref, qk_ref, pooled_ref, keep_ref, shifted):
    half_gradient(lax.axis_index("dp") % 2, dconv_ref, qk_ref, pooled_ref, keep_ref, shifted)


def send_half(n, embed, proj, slope, pooled):
    co, rows = slope.shape
    size = co // 2
    held = -(-size // 16) * 16
    return pl.pallas_call(
        functools.partial(send_kernel, n),
        out_shape=[
            jax.ShapeDtypeStruct((size, CODED), jnp.int16),
            jax.ShapeDtypeStruct((2, held, rows + 2 * PAD), jnp.bfloat16),
            jax.ShapeDtypeStruct((2, size, 2 * PC), jnp.float32),
        ],
        scratch_shapes=[pltpu.VMEM((256, rows), jnp.bfloat16)],
        compiler_params=params(32),
        name="send_half",
    )(embed, proj, slope, pooled)


def keep_half(dconv, qk, pooled):
    size, rows = qk.shape[1], pooled.shape[1]
    return pl.pallas_call(
        keep_kernel,
        out_shape=jax.ShapeDtypeStruct((size, WIDE), jnp.float32),
        scratch_shapes=[pltpu.VMEM((256, rows), jnp.bfloat16)],
        compiler_params=params(32),
        cost_estimate=pl.CostEstimate(
            flops=2 * K1 * size * C0 * rows, bytes_accessed=12 * MIB, transcendentals=0
        ),
        name="keep_half",
    )(dconv, qk, pooled)


def add_kernel(a_ref, b_ref, out_ref):
    if a_ref.dtype == jnp.int16:
        a = decode(a_ref)
    else:
        a = [a_ref[:, begin:end] for begin, end in PARTS]
    encode([x + y for x, y in zip(a, decode(b_ref))], out_ref)


def add_half(a, b):
    return pl.pallas_call(
        add_kernel,
        out_shape=jax.ShapeDtypeStruct(b.shape, jnp.int16),
        compiler_params=params(8),
        name="add_half",
    )(a, b)


def join_kernel(mine_ref, other_ref, conv_ref, query_ref, key_ref):
    size = mine_ref.shape[0]
    core = lax.axis_index("dp") % 2
    for half, ref in ((core, mine_ref), (1 - core, other_ref)):
        rows = pl.ds(pl.multiple_of(half * size, 8), size)
        for x, out_ref in zip(decode(ref), (conv_ref, query_ref, key_ref)):
            out_ref[rows, :] = x


def join(mine, other):
    co = 2 * mine.shape[0]
    return pl.pallas_call(
        join_kernel,
        out_shape=[
            jax.ShapeDtypeStruct((co, K1 * C0), jnp.float32),
            jax.ShapeDtypeStruct((co, PC), jnp.float32),
            jax.ShapeDtypeStruct((co, PC), jnp.float32),
        ],
        compiler_params=params(8),
        name="join",
    )(mine, other)


def body(bases, stem_table, conv_weight, query_weight, key_weight, pair_grad):
    n = lax.axis_size("seq")
    rows_dev = bases.shape[1] // POOL

    own = bases.astype(jnp.bfloat16).reshape(2, rows_dev // 2, POOL).transpose(0, 2, 1)
    payload = gather_xor(own.reshape(2 * POOL, rows_dev // 2), "seq")

    first_table = jnp.pad(
        stem_table.transpose(2, 1, 0), ((0, 0), (0, 0), (1, WINDOW - 1 - K0))
    ).reshape(C0, 4 * WINDOW)
    first_table = jnp.pad(first_table, ((0, 0), (0, 128 - 4 * WINDOW))).astype(jnp.float32)
    table, weights, proj = prepare(n, first_table, conv_weight, query_weight, key_weight)

    pooled, slope, embed = stem_and_conv(n, payload, table, weights, pair_grad[0])
    embed_all = gather_direct(embed, "seq")
    send, dconv, qk = send_half(n, embed_all, proj, slope, pooled)
    received = swap(send, "dp", 1)
    keep = keep_half(dconv, qk, pooled)

    mine = add_half(keep, received)
    bit = 2
    while bit < lax.axis_size("dp"):
        mine = add_half(mine, swap(mine, "dp", bit))
        bit *= 2
    return tuple(join(mine, swap(mine, "dp", 1)))


def solution(mesh):
    return jax.shard_map(
        body,
        mesh=mesh,
        in_specs=(P("dp", "seq"), P(), P("seq", None), P(), P(), P("dp", "seq", None)),
        out_specs=(P("seq", None), P("seq", None), P("seq", None)),
        check_vma=False,
    )
```

```python
import functools

import jax
import jax.numpy as jnp
from jax import lax
from jax.experimental import pallas as pl
from jax.experimental.pallas import tpu as pltpu
from jax.sharding import PartitionSpec as P

C0 = 768
C1 = 768
PC = 128
K0 = 15
K1 = 5
POOL = 8
BIN_ROWS = 256
WINDOW = 24
CHUNK = 32
BLOCK = 512
LAG = 3
PAD = 128
SLOT = 128

ROOT = 0.7978845608028654
CUBE = 0.044715
HIGH = lax.Precision.HIGHEST
MIB = 1024 * 1024


def params(mib):
    return pltpu.CompilerParams(vmem_limit_bytes=mib * MIB)


def swap(x, axis, bit):
    size = lax.axis_size(axis)
    return lax.ppermute(x, axis, [(i, i ^ bit) for i in range(size)])


def gather_xor(x, axis):
    x = x[None]
    bit = 1
    while bit < lax.axis_size(axis):
        x = jnp.concatenate([x, swap(x, axis, bit)], axis=0)
        bit *= 2
    return x


def gather_direct(x, axis):
    return lax.all_to_all(jnp.broadcast_to(x[None], (lax.axis_size(axis),) + x.shape), axis, 0, 0)


def twice_gelu(v):
    return v + v * jnp.tanh(v * (ROOT + (ROOT * CUBE) * (v * v)))


def prepare_kernel(n, co, t0_ref, w_ref, wq_ref, wk_ref, table_ref, weights_ref, proj_ref):
    for chunk in range(C0 // CHUNK):
        part = t0_ref[chunk * CHUNK : (chunk + 1) * CHUNK, :]
        for pos in range(POOL):
            shifted = part if pos == 0 else pltpu.roll(part, pos, 1)
            first = (chunk * POOL + pos) * CHUNK
            table_ref[first : first + CHUNK, :] = shifted.astype(jnp.bfloat16)
    for tap in range(K1):
        weights_ref[tap * co : (tap + 1) * co, :] = w_ref[:, tap * C0 : (tap + 1) * C0] * 0.5
    for slot in range(n):
        rows = slice(slot * co, (slot + 1) * co)
        proj_ref[slot * SLOT : slot * SLOT + co, :PC] = wq_ref[rows, :]
        proj_ref[slot * SLOT : slot * SLOT + co, PC:] = wk_ref[rows, :]
        proj_ref[slot * SLOT + co : (slot + 1) * SLOT, :] = jnp.zeros(
            (SLOT - co, 2 * PC), jnp.bfloat16
        )


def prepare(n, first_table, conv_weight, query_weight, key_weight):
    co = conv_weight.shape[0]
    return pl.pallas_call(
        functools.partial(prepare_kernel, n, co),
        out_shape=[
            jax.ShapeDtypeStruct((POOL * C0, 128), jnp.bfloat16),
            jax.ShapeDtypeStruct((K1 * co, C0), jnp.bfloat16),
            jax.ShapeDtypeStruct((n * SLOT, 2 * PC), jnp.bfloat16),
        ],
        compiler_params=params(8),
        cost_estimate=pl.CostEstimate(flops=0, bytes_accessed=5 * MIB, transcendentals=0),
        name="prepare",
    )(first_table, conv_weight, query_weight, key_weight)


def stem_kernel(
    n, rows_dev, co, pay_ref, table, weights, grad_ref, p_ref, slope_ref, emb_ref,
    bases, ybuf, prev, sums, slopes
):
    step = pl.program_id(0)
    rows = n * rows_dev
    blocks = rows // BLOCK
    front = LAG * BLOCK + PAD

    def convolve(block):
        first = pl.multiple_of((block + LAG) * BLOCK, 128)
        conv = None
        for tap in range(K1):
            near = ybuf[tap * co : (tap + 1) * co, pl.ds(first, BLOCK + 2 * PAD)]
            begin = PAD + tap - K1 // 2
            part = near[:, begin : begin + BLOCK]
            conv = part if conv is None else conv + part
        square = conv * conv
        tangent = jnp.tanh(conv * (ROOT + (ROOT * CUBE) * square))
        half = 0.5 * conv
        gelu = half + half * tangent
        slopes[...] = (0.5 + 0.5 * tangent) + half * (1.0 - tangent * tangent) * (
            ROOT + (3.0 * ROOT * CUBE) * square
        )
        lane = lax.broadcasted_iota(jnp.int32, (co, 128), 1)
        total = sums[:co, :]
        for part in range(BLOCK // BIN_ROWS):
            mean = jnp.sum(
                gelu[:, part * BIN_ROWS : (part + 1) * BIN_ROWS], axis=1, keepdims=True
            ) * (1.0 / BIN_ROWS)
            total = jnp.where(lane == block * (BLOCK // BIN_ROWS) + part, mean, total)
        sums[:co, :] = total

    def taps(block):
        ybuf[:, pl.ds(pl.multiple_of(front + block * BLOCK, 128), BLOCK)] = jnp.dot(
            weights[...], prev[...], preferred_element_type=jnp.float32
        )

    @pl.when(step == 0)
    def _():
        me = lax.axis_index("seq")
        bases[:, :PAD] = jnp.full((POOL, PAD), -1.0, jnp.float32)
        bases[:, PAD + rows :] = jnp.full((POOL, PAD), -1.0, jnp.float32)
        half = rows_dev // 2
        for slab in range(n):
            block = pay_ref[jnp.bitwise_xor(me, slab)].astype(jnp.float32)
            first = PAD + slab * rows_dev
            bases[:, first : first + half] = block[:POOL]
            bases[:, first + half : first + 2 * half] = block[POOL:]
        ybuf[:, front + rows :] = jnp.zeros((K1 * co, PAD), jnp.float32)
        prev[...] = jnp.zeros(prev.shape, jnp.bfloat16)
        sums[...] = jnp.zeros(sums.shape, jnp.float32)

    @pl.when(step < blocks)
    def _():
        first = pl.multiple_of(step * BLOCK, 128)
        near = bases[:, pl.ds(first, BLOCK + 2 * PAD)]
        window = jnp.concatenate(
            [near[:, PAD + q : PAD + q + BLOCK] for q in (-1, 0, 1)], axis=0
        )
        onehot = jnp.concatenate(
            [(window == b).astype(jnp.float32) for b in range(4)]
            + [jnp.zeros((128 - 4 * WINDOW, BLOCK), jnp.float32)],
            axis=0,
        ).astype(jnp.bfloat16)
        convolve(step - LAG)
        taps(step - 1)
        for at in range(0, BLOCK, 256):
            for chunk in range(C0 // CHUNK):
                stem = jnp.dot(
                    table[chunk * POOL * CHUNK : (chunk + 1) * POOL * CHUNK, :],
                    onehot[:, at : at + 256],
                    preferred_element_type=jnp.float32,
                )
                most = least = stem[:CHUNK]
                for pos in range(1, POOL):
                    part = stem[pos * CHUNK : (pos + 1) * CHUNK]
                    most = jnp.maximum(most, part)
                    least = jnp.minimum(least, part)
                pooled = jnp.maximum(twice_gelu(most), twice_gelu(least)).astype(jnp.bfloat16)
                prev[chunk * CHUNK : (chunk + 1) * CHUNK, at : at + 256] = pooled
                p_ref[chunk * CHUNK : (chunk + 1) * CHUNK, at : at + 256] = pooled
        slope_ref[...] = slopes[...]

    @pl.when(step >= blocks)
    def _():
        @pl.when(step == blocks)
        def _():
            taps(blocks - 1)

        convolve(step - LAG)
        slope_ref[...] = slopes[...]

    @pl.when(step == blocks + LAG - 1)
    def _():
        own_pos, npos = grad_ref.shape
        embed = sums[...].T[:npos, :].astype(jnp.bfloat16).astype(jnp.float32)
        rest = grad_ref[...]
        parts = []
        for _ in range(3):
            part = rest.astype(jnp.bfloat16).astype(jnp.float32)
            parts.append(part)
            rest = rest - part
        grads = jnp.concatenate(
            parts + [jnp.zeros((npos - 3 * own_pos, npos), jnp.float32)], axis=0
        )
        emb_ref[...] = jnp.concatenate(
            [embed[:, :co], grads, jnp.zeros((npos, SLOT - co - npos), jnp.float32)], axis=1
        ).astype(jnp.bfloat16)


def stem_and_conv(n, payload, table, weights, pair_grad):
    co = weights.shape[0] // K1
    rows_dev = payload.shape[2] * 2
    rows = n * rows_dev
    npos = rows // BIN_ROWS
    blocks = rows // BLOCK
    whole = lambda i: (0, 0)
    return pl.pallas_call(
        functools.partial(stem_kernel, n, rows_dev, co),
        grid=(blocks + LAG,),
        in_specs=[
            pl.BlockSpec(payload.shape, lambda i: (0, 0, 0)),
            pl.BlockSpec(table.shape, whole),
            pl.BlockSpec(weights.shape, whole),
            pl.BlockSpec(pair_grad.shape, whole),
        ],
        out_specs=[
            pl.BlockSpec((C0, BLOCK), lambda i: (0, jnp.minimum(i, blocks - 1))),
            pl.BlockSpec((co, BLOCK), lambda i: (0, jnp.maximum(i - LAG, 0))),
            pl.BlockSpec((npos, SLOT), whole),
        ],
        out_shape=[
            jax.ShapeDtypeStruct((C0, rows), jnp.bfloat16),
            jax.ShapeDtypeStruct((co, rows), jnp.float32),
            jax.ShapeDtypeStruct((npos, SLOT), jnp.bfloat16),
        ],
        scratch_shapes=[
            pltpu.VMEM((POOL, rows + 2 * PAD), jnp.float32),
            pltpu.VMEM((K1 * co, LAG * BLOCK + rows + 2 * PAD), jnp.float32),
            pltpu.VMEM((C0, BLOCK), jnp.bfloat16),
            pltpu.VMEM((128, 128), jnp.float32),
            pltpu.VMEM((co, BLOCK), jnp.float32),
        ],
        compiler_params=params(36),
        name="stem_and_conv",
    )(payload, table, weights, pair_grad)


WIDE = K1 * C0 + 2 * PC
PARTS = ((0, K1 * C0), (K1 * C0, K1 * C0 + PC), (K1 * C0 + PC, WIDE))
CODED = WIDE + 128


def encode(values, out_ref):
    exponents = []
    for (begin, end), x in zip(PARTS, values):
        top = jnp.maximum(jnp.max(jnp.abs(x), axis=1, keepdims=True), 1e-30)
        exponent = jnp.floor(jnp.log2(32000.0 / top))
        scaled = jnp.floor(x * jnp.exp2(exponent) + 0.5)
        out_ref[:, begin:end] = scaled.astype(jnp.int32).astype(jnp.int16)
        exponents.append(exponent)
    lane = lax.broadcasted_iota(jnp.int32, (out_ref.shape[0], 128), 1)
    packed = jnp.where(lane == 0, exponents[0], jnp.where(lane == 1, exponents[1], exponents[2]))
    out_ref[:, WIDE:] = packed.astype(jnp.int32).astype(jnp.int16)


def decode(ref):
    exponents = ref[:, WIDE:].astype(jnp.int32).astype(jnp.float32)
    return [
        ref[:, begin:end].astype(jnp.int32).astype(jnp.float32) * jnp.exp2(-exponents[:, at : at + 1])
        for at, (begin, end) in enumerate(PARTS)
    ]


def half_gradient(half, dconv, qk_ref, pooled_ref, out_ref, shifted):
    size = out_ref.shape[0]
    held = dconv.shape[1]
    rows = pooled_ref.shape[1]
    shifted[K1 * held :, :] = jnp.zeros((shifted.shape[0] - K1 * held, rows), jnp.bfloat16)
    for first in range(0, rows, BLOCK):
        near = dconv[half, :, first : first + BLOCK + 2 * PAD]
        for tap in range(K1):
            begin = PAD - tap + K1 // 2
            shifted[tap * held : (tap + 1) * held, first : first + BLOCK] = near[
                :, begin : begin + BLOCK
            ]
    product = lax.dot_general(
        pooled_ref[...], shifted[...], (((1,), (1,)), ((), ())), preferred_element_type=jnp.float32
    ).T
    conv = jnp.concatenate(
        [product[tap * held : tap * held + size, :] for tap in range(K1)], axis=1
    )
    if out_ref.dtype == jnp.int16:
        qk = qk_ref[half]
        encode((conv, qk[:, :PC], qk[:, PC:]), out_ref)
    else:
        out_ref[:, : K1 * C0] = conv
        out_ref[:, K1 * C0 :] = qk_ref[half]


def send_kernel(n, emb_ref, proj_ref, slope_ref, pooled_ref, send_ref, dconv_ref, qk_ref, shifted):
    co, rows = slope_ref.shape
    size, held = co // 2, dconv_ref.shape[1]
    npos = rows // BIN_ROWS
    own_pos = npos // n
    scale = PC**-0.5
    me = lax.axis_index("seq")
    both = jnp.dot(
        jnp.concatenate([emb_ref[slot] for slot in range(n)], axis=1),
        proj_ref[...],
        preferred_element_type=jnp.float32,
    )
    query, keys = both[:, :PC], both[:, PC:]
    pieces = []
    for slab in range(n):
        block = emb_ref[slab].astype(jnp.float32)
        total = block[:own_pos]
        for part in range(1, 3):
            total = total + block[part * own_pos : (part + 1) * own_pos]
        pieces.append(total)
    grad = jnp.concatenate(pieces, axis=0)[:, co : co + npos]
    dquery = jnp.dot(grad, keys, precision=HIGH, preferred_element_type=jnp.float32) * scale
    dkeys = (
        lax.dot_general(
            grad, query, (((0,), (0,)), ((), ())), precision=HIGH,
            preferred_element_type=jnp.float32,
        )
        * scale
    )
    cotangent = jnp.concatenate([dquery, dkeys], axis=1)
    own = pl.ds(pl.multiple_of(me * SLOT, SLOT), SLOT)
    dembed = lax.dot_general(
        proj_ref[own, :].astype(jnp.float32), cotangent,
        (((1,), (1,)), ((), ())), precision=HIGH, preferred_element_type=jnp.float32,
    ) * (0.5 / BIN_ROWS)
    qk = lax.dot_general(
        emb_ref[me].astype(jnp.float32), cotangent, (((0,), (0,)), ((), ())),
        precision=HIGH, preferred_element_type=jnp.float32,
    )
    edge = jnp.zeros((held, PAD), jnp.bfloat16)
    for half in range(2):
        channels = slice(half * size, (half + 1) * size)
        qk_ref[half] = qk[channels]
        dconv_ref[half, :, :PAD] = edge
        dconv_ref[half, :, PAD + rows :] = edge
        for pos in range(npos):
            part = slope_ref[channels, pos * BIN_ROWS : (pos + 1) * BIN_ROWS] * dembed[
                channels, pos : pos + 1
            ]
            if held > size:
                part = jnp.concatenate(
                    [part, jnp.zeros((held - size, BIN_ROWS), jnp.float32)], axis=0
                )
            dconv_ref[half, :, PAD + pos * BIN_ROWS : PAD + (pos + 1) * BIN_ROWS] = part.astype(
                jnp.bfloat16
            )
    half_gradient(1 - lax.axis_index("dp") % 2, dconv_ref, qk_ref, pooled_ref, send_ref, shifted)


def keep_kernel(dconv_ref, qk_ref, pooled_ref, keep_ref, shifted):
    half_gradient(lax.axis_index("dp") % 2, dconv_ref, qk_ref, pooled_ref, keep_ref, shifted)


def send_half(n, embed, proj, slope, pooled):
    co, rows = slope.shape
    size = co // 2
    held = -(-size // 16) * 16
    return pl.pallas_call(
        functools.partial(send_kernel, n),
        out_shape=[
            jax.ShapeDtypeStruct((size, CODED), jnp.int16),
            jax.ShapeDtypeStruct((2, held, rows + 2 * PAD), jnp.bfloat16),
            jax.ShapeDtypeStruct((2, size, 2 * PC), jnp.float32),
        ],
        scratch_shapes=[pltpu.VMEM((256, rows), jnp.bfloat16)],
        compiler_params=params(32),
        name="send_half",
    )(embed, proj, slope, pooled)


def keep_half(dconv, qk, pooled):
    size, rows = qk.shape[1], pooled.shape[1]
    return pl.pallas_call(
        keep_kernel,
        out_shape=jax.ShapeDtypeStruct((size, WIDE), jnp.float32),
        scratch_shapes=[pltpu.VMEM((256, rows), jnp.bfloat16)],
        compiler_params=params(32),
        cost_estimate=pl.CostEstimate(
            flops=2 * K1 * size * C0 * rows, bytes_accessed=12 * MIB, transcendentals=0
        ),
        name="keep_half",
    )(dconv, qk, pooled)


def add_kernel(a_ref, b_ref, out_ref):
    if a_ref.dtype == jnp.int16:
        a = decode(a_ref)
    else:
        a = [a_ref[:, begin:end] for begin, end in PARTS]
    encode([x + y for x, y in zip(a, decode(b_ref))], out_ref)


def add_half(a, b):
    return pl.pallas_call(
        add_kernel,
        out_shape=jax.ShapeDtypeStruct(b.shape, jnp.int16),
        compiler_params=params(8),
        name="add_half",
    )(a, b)


def join_kernel(mine_ref, other_ref, conv_ref, query_ref, key_ref):
    size = mine_ref.shape[0]
    core = lax.axis_index("dp") % 2
    for half, ref in ((core, mine_ref), (1 - core, other_ref)):
        rows = pl.ds(pl.multiple_of(half * size, 8), size)
        for x, out_ref in zip(decode(ref), (conv_ref, query_ref, key_ref)):
            out_ref[rows, :] = x


def join(mine, other):
    co = 2 * mine.shape[0]
    return pl.pallas_call(
        join_kernel,
        out_shape=[
            jax.ShapeDtypeStruct((co, K1 * C0), jnp.float32),
            jax.ShapeDtypeStruct((co, PC), jnp.float32),
            jax.ShapeDtypeStruct((co, PC), jnp.float32),
        ],
        compiler_params=params(8),
        name="join",
    )(mine, other)


def body(bases, stem_table, conv_weight, query_weight, key_weight, pair_grad):
    n = lax.axis_size("seq")
    rows_dev = bases.shape[1] // POOL

    own = bases.astype(jnp.bfloat16).reshape(2, rows_dev // 2, POOL).transpose(0, 2, 1)
    payload = gather_xor(own.reshape(2 * POOL, rows_dev // 2), "seq")

    first_table = jnp.pad(
        stem_table.transpose(2, 1, 0), ((0, 0), (0, 0), (1, WINDOW - 1 - K0))
    ).reshape(C0, 4 * WINDOW)
    first_table = jnp.pad(first_table, ((0, 0), (0, 128 - 4 * WINDOW))).astype(jnp.float32)
    table, weights, proj = prepare(n, first_table, conv_weight, query_weight, key_weight)

    pooled, slope, embed = stem_and_conv(n, payload, table, weights, pair_grad[0])
    embed_all = gather_direct(embed, "seq")
    send, dconv, qk = send_half(n, embed_all, proj, slope, pooled)
    received = swap(send, "dp", 1)
    keep = keep_half(dconv, qk, pooled)

    mine = add_half(keep, received)
    bit = 2
    while bit < lax.axis_size("dp"):
        mine = add_half(mine, swap(mine, "dp", bit))
        bit *= 2
    return tuple(join(mine, swap(mine, "dp", 1)))


def solution(mesh):
    return jax.shard_map(
        body,
        mesh=mesh,
        in_specs=(P("dp", "seq"), P(), P("seq", None), P(), P(), P("dp", "seq", None)),
        out_specs=(P("seq", None), P("seq", None), P("seq", None)),
        check_vma=False,
    )
```

```python
import functools

import jax
import jax.numpy as jnp
from jax import lax
from jax.experimental import pallas as pl
from jax.experimental.pallas import tpu as pltpu
from jax.sharding import PartitionSpec as P

C0 = 768
C1 = 768
PC = 128
K0 = 15
K1 = 5
POOL = 8
BIN_ROWS = 256
WINDOW = 24
CHUNK = 16
BLOCK = 512
LAG = 3
PAD = 128
SLOT = 128

ROOT = 0.7978845608028654
CUBE = 0.044715
HIGH = lax.Precision.HIGHEST
MIB = 1024 * 1024


def params(mib):
    return pltpu.CompilerParams(vmem_limit_bytes=mib * MIB)


def swap(x, axis, bit):
    size = lax.axis_size(axis)
    return lax.ppermute(x, axis, [(i, i ^ bit) for i in range(size)])


def gather_xor(x, axis):
    x = x[None]
    bit = 1
    while bit < lax.axis_size(axis):
        x = jnp.concatenate([x, swap(x, axis, bit)], axis=0)
        bit *= 2
    return x


def twice_gelu(v):
    return v + v * jnp.tanh(v * (ROOT + (ROOT * CUBE) * (v * v)))


def prepare_kernel(n, co, t0_ref, w_ref, wq_ref, wk_ref, table_ref, weights_ref, proj_ref):
    for chunk in range(C0 // CHUNK):
        part = t0_ref[chunk * CHUNK : (chunk + 1) * CHUNK, :]
        for pos in range(POOL):
            shifted = part if pos == 0 else pltpu.roll(part, pos, 1)
            first = (chunk * POOL + pos) * CHUNK
            table_ref[first : first + CHUNK, :] = shifted.astype(jnp.bfloat16)
    for tap in range(K1):
        weights_ref[tap * co : (tap + 1) * co, :] = w_ref[:, tap * C0 : (tap + 1) * C0] * 0.5
    for slot in range(n):
        rows = slice(slot * co, (slot + 1) * co)
        proj_ref[slot * SLOT : slot * SLOT + co, :PC] = wq_ref[rows, :]
        proj_ref[slot * SLOT : slot * SLOT + co, PC:] = wk_ref[rows, :]
        proj_ref[slot * SLOT + co : (slot + 1) * SLOT, :] = jnp.zeros(
            (SLOT - co, 2 * PC), jnp.bfloat16
        )


def prepare(n, first_table, conv_weight, query_weight, key_weight):
    co = conv_weight.shape[0]
    return pl.pallas_call(
        functools.partial(prepare_kernel, n, co),
        out_shape=[
            jax.ShapeDtypeStruct((POOL * C0, 128), jnp.bfloat16),
            jax.ShapeDtypeStruct((K1 * co, C0), jnp.bfloat16),
            jax.ShapeDtypeStruct((n * SLOT, 2 * PC), jnp.bfloat16),
        ],
        compiler_params=params(8),
        cost_estimate=pl.CostEstimate(flops=0, bytes_accessed=5 * MIB, transcendentals=0),
        name="prepare",
    )(first_table, conv_weight, query_weight, key_weight)


def stem_kernel(
    n, rows_dev, co, pay_ref, table, weights, grad_ref, p_ref, slope_ref, emb_ref,
    bases, ybuf, sums
):
    rows = n * rows_dev
    blocks = rows // BLOCK
    front = LAG * BLOCK + PAD

    def convolve(block):
        first = pl.multiple_of((block + LAG) * BLOCK, 128)
        conv = None
        for tap in range(K1):
            near = ybuf[tap * co : (tap + 1) * co, pl.ds(first, BLOCK + 2 * PAD)]
            begin = PAD + tap - K1 // 2
            part = near[:, begin : begin + BLOCK]
            conv = part if conv is None else conv + part
        square = conv * conv
        tangent = jnp.tanh(conv * (ROOT + (ROOT * CUBE) * square))
        half = 0.5 * conv
        gelu = half + half * tangent
        to = pl.multiple_of(jnp.maximum(block, 0) * BLOCK, 128)
        slope_ref[:, pl.ds(to, BLOCK)] = (0.5 + 0.5 * tangent) + half * (1.0 - tangent * tangent) * (
            ROOT + (3.0 * ROOT * CUBE) * square
        )
        lane = lax.broadcasted_iota(jnp.int32, (co, 128), 1)
        total = sums[:co, :]
        for part in range(BLOCK // BIN_ROWS):
            mean = jnp.sum(
                gelu[:, part * BIN_ROWS : (part + 1) * BIN_ROWS], axis=1, keepdims=True
            ) * (1.0 / BIN_ROWS)
            total = jnp.where(lane == block * (BLOCK // BIN_ROWS) + part, mean, total)
        sums[:co, :] = total

    def taps(block):
        ybuf[:, pl.ds(pl.multiple_of(front + block * BLOCK, 128), BLOCK)] = jnp.dot(
            weights[...],
            p_ref[:, pl.ds(pl.multiple_of(jnp.maximum(block, 0) * BLOCK, 128), BLOCK)],
            preferred_element_type=jnp.float32,
        )

    me = lax.axis_index("seq")
    bases[:, :PAD] = jnp.full((POOL, PAD), -1.0, jnp.float32)
    bases[:, PAD + rows :] = jnp.full((POOL, PAD), -1.0, jnp.float32)
    half = rows_dev // 2
    for slab in range(n):
        block = pay_ref[jnp.bitwise_xor(me, slab)].astype(jnp.float32)
        first = PAD + slab * rows_dev
        bases[:, first : first + half] = block[:POOL]
        bases[:, first + half : first + 2 * half] = block[POOL:]
    ybuf[:, front + rows :] = jnp.zeros((K1 * co, PAD), jnp.float32)
    p_ref[:, :BLOCK] = jnp.zeros((C0, BLOCK), jnp.bfloat16)
    sums[...] = jnp.zeros(sums.shape, jnp.float32)

    def main(step, carry):
        first = pl.multiple_of(step * BLOCK, 128)
        near = bases[:, pl.ds(first, BLOCK + 2 * PAD)]
        window = jnp.concatenate(
            [near[:, PAD + q : PAD + q + BLOCK] for q in (-1, 0, 1)], axis=0
        )
        onehot = jnp.concatenate(
            [(window == b).astype(jnp.float32) for b in range(4)]
            + [jnp.zeros((128 - 4 * WINDOW, BLOCK), jnp.float32)],
            axis=0,
        ).astype(jnp.bfloat16)
        convolve(step - LAG)
        taps(step - 1)
        for chunk in range(C0 // CHUNK):
            for at in range(0, BLOCK, 256):
                stem = jnp.dot(
                    table[chunk * POOL * CHUNK : (chunk + 1) * POOL * CHUNK, :],
                    onehot[:, at : at + 256],
                    preferred_element_type=jnp.float32,
                )
                most = least = stem[:CHUNK]
                for pos in range(1, POOL):
                    part = stem[pos * CHUNK : (pos + 1) * CHUNK]
                    most = jnp.maximum(most, part)
                    least = jnp.minimum(least, part)
                p_ref[
                    chunk * CHUNK : (chunk + 1) * CHUNK, pl.ds(pl.multiple_of(first + at, 128), 256)
                ] = jnp.maximum(twice_gelu(most), twice_gelu(least)).astype(jnp.bfloat16)
        return carry

    lax.fori_loop(0, blocks, main, 0)
    taps(blocks - 1)
    for last in range(LAG):
        convolve(blocks - LAG + last)

    own_pos, npos = grad_ref.shape
    embed = sums[...].T[:npos, :].astype(jnp.bfloat16).astype(jnp.float32)
    rest = grad_ref[...]
    parts = []
    for _ in range(3):
        part = rest.astype(jnp.bfloat16).astype(jnp.float32)
        parts.append(part)
        rest = rest - part
    grads = jnp.concatenate(
        parts + [jnp.zeros((npos - 3 * own_pos, npos), jnp.float32)], axis=0
    )
    emb_ref[...] = jnp.concatenate(
        [embed[:, :co], grads, jnp.zeros((npos, SLOT - co - npos), jnp.float32)], axis=1
    ).astype(jnp.bfloat16)


def stem_and_conv(n, payload, table, weights, pair_grad):
    co = weights.shape[0] // K1
    rows_dev = payload.shape[2] * 2
    rows = n * rows_dev
    npos = rows // BIN_ROWS
    return pl.pallas_call(
        functools.partial(stem_kernel, n, rows_dev, co),
        out_shape=[
            jax.ShapeDtypeStruct((C0, rows), jnp.bfloat16),
            jax.ShapeDtypeStruct((co, rows), jnp.float32),
            jax.ShapeDtypeStruct((npos, SLOT), jnp.bfloat16),
        ],
        scratch_shapes=[
            pltpu.VMEM((POOL, rows + 2 * PAD), jnp.float32),
            pltpu.VMEM((K1 * co, LAG * BLOCK + rows + 2 * PAD), jnp.float32),
            pltpu.VMEM((128, 128), jnp.float32),
        ],
        compiler_params=params(36),
        name="stem_and_conv",
    )(payload, table, weights, pair_grad)


WIDE = K1 * C0 + 2 * PC
PARTS = ((0, K1 * C0), (K1 * C0, K1 * C0 + PC), (K1 * C0 + PC, WIDE))
CODED = WIDE + 128


def encode(values, out_ref):
    exponents = []
    for (begin, end), x in zip(PARTS, values):
        top = jnp.maximum(jnp.max(jnp.abs(x), axis=1, keepdims=True), 1e-30)
        exponent = jnp.floor(jnp.log2(32000.0 / top))
        scaled = jnp.floor(x * jnp.exp2(exponent) + 0.5)
        out_ref[:, begin:end] = scaled.astype(jnp.int32).astype(jnp.int16)
        exponents.append(exponent)
    lane = lax.broadcasted_iota(jnp.int32, (out_ref.shape[0], 128), 1)
    packed = jnp.where(lane == 0, exponents[0], jnp.where(lane == 1, exponents[1], exponents[2]))
    out_ref[:, WIDE:] = packed.astype(jnp.int32).astype(jnp.int16)


def decode(ref):
    exponents = ref[:, WIDE:].astype(jnp.int32).astype(jnp.float32)
    return [
        ref[:, begin:end].astype(jnp.int32).astype(jnp.float32) * jnp.exp2(-exponents[:, at : at + 1])
        for at, (begin, end) in enumerate(PARTS)
    ]


def half_gradient(half, dconv, qk_ref, pooled_ref, out_ref, shifted):
    size = out_ref.shape[0]
    held = dconv.shape[1]
    rows = pooled_ref.shape[1]
    shifted[K1 * held :, :] = jnp.zeros((shifted.shape[0] - K1 * held, rows), jnp.bfloat16)
    for first in range(0, rows, BLOCK):
        near = dconv[half, :, first : first + BLOCK + 2 * PAD]
        for tap in range(K1):
            begin = PAD - tap + K1 // 2
            shifted[tap * held : (tap + 1) * held, first : first + BLOCK] = near[
                :, begin : begin + BLOCK
            ]
    product = lax.dot_general(
        pooled_ref[...], shifted[...], (((1,), (1,)), ((), ())), preferred_element_type=jnp.float32
    ).T
    conv = jnp.concatenate(
        [product[tap * held : tap * held + size, :] for tap in range(K1)], axis=1
    )
    if out_ref.dtype == jnp.int16:
        qk = qk_ref[half]
        encode((conv, qk[:, :PC], qk[:, PC:]), out_ref)
    else:
        out_ref[:, : K1 * C0] = conv
        out_ref[:, K1 * C0 :] = qk_ref[half]


def send_kernel(n, emb_ref, proj_ref, slope_ref, pooled_ref, send_ref, dconv_ref, qk_ref, shifted):
    co, rows = slope_ref.shape
    size, held = co // 2, dconv_ref.shape[1]
    npos = rows // BIN_ROWS
    own_pos = npos // n
    scale = PC**-0.5
    me = lax.axis_index("seq")
    both = jnp.dot(
        jnp.concatenate([emb_ref[jnp.bitwise_xor(me, slab)] for slab in range(n)], axis=1),
        proj_ref[...],
        preferred_element_type=jnp.float32,
    )
    query, keys = both[:, :PC], both[:, PC:]
    pieces = []
    for slab in range(n):
        block = emb_ref[jnp.bitwise_xor(me, slab)].astype(jnp.float32)
        total = block[:own_pos]
        for part in range(1, 3):
            total = total + block[part * own_pos : (part + 1) * own_pos]
        pieces.append(total)
    grad = jnp.concatenate(pieces, axis=0)[:, co : co + npos]
    dquery = jnp.dot(grad, keys, precision=HIGH, preferred_element_type=jnp.float32) * scale
    dkeys = (
        lax.dot_general(
            grad, query, (((0,), (0,)), ((), ())), precision=HIGH,
            preferred_element_type=jnp.float32,
        )
        * scale
    )
    cotangent = jnp.concatenate([dquery, dkeys], axis=1)
    own = pl.ds(pl.multiple_of(me * SLOT, SLOT), SLOT)
    dembed = lax.dot_general(
        proj_ref[own, :].astype(jnp.float32), cotangent,
        (((1,), (1,)), ((), ())), precision=HIGH, preferred_element_type=jnp.float32,
    ) * (0.5 / BIN_ROWS)
    qk = lax.dot_general(
        emb_ref[0].astype(jnp.float32), cotangent, (((0,), (0,)), ((), ())),
        precision=HIGH, preferred_element_type=jnp.float32,
    )
    edge = jnp.zeros((held, PAD), jnp.bfloat16)
    for half in range(2):
        channels = slice(half * size, (half + 1) * size)
        qk_ref[half] = qk[channels]
        dconv_ref[half, :, :PAD] = edge
        dconv_ref[half, :, PAD + rows :] = edge
        for pos in range(npos):
            part = slope_ref[channels, pos * BIN_ROWS : (pos + 1) * BIN_ROWS] * dembed[
                channels, pos : pos + 1
            ]
            if held > size:
                part = jnp.concatenate(
                    [part, jnp.zeros((held - size, BIN_ROWS), jnp.float32)], axis=0
                )
            dconv_ref[half, :, PAD + pos * BIN_ROWS : PAD + (pos + 1) * BIN_ROWS] = part.astype(
                jnp.bfloat16
            )
    half_gradient(1 - lax.axis_index("dp") % 2, dconv_ref, qk_ref, pooled_ref, send_ref, shifted)


def keep_kernel(dconv_ref, qk_ref, pooled_ref, keep_ref, shifted):
    half_gradient(lax.axis_index("dp") % 2, dconv_ref, qk_ref, pooled_ref, keep_ref, shifted)


def send_half(n, embed, proj, slope, pooled):
    co, rows = slope.shape
    size = co // 2
    held = -(-size // 16) * 16
    return pl.pallas_call(
        functools.partial(send_kernel, n),
        out_shape=[
            jax.ShapeDtypeStruct((size, CODED), jnp.int16),
            jax.ShapeDtypeStruct((2, held, rows + 2 * PAD), jnp.bfloat16),
            jax.ShapeDtypeStruct((2, size, 2 * PC), jnp.float32),
        ],
        scratch_shapes=[pltpu.VMEM((256, rows), jnp.bfloat16)],
        compiler_params=params(32),
        name="send_half",
    )(embed, proj, slope, pooled)


def keep_half(dconv, qk, pooled):
    size, rows = qk.shape[1], pooled.shape[1]
    return pl.pallas_call(
        keep_kernel,
        out_shape=jax.ShapeDtypeStruct((size, WIDE), jnp.float32),
        scratch_shapes=[pltpu.VMEM((256, rows), jnp.bfloat16)],
        compiler_params=params(32),
        cost_estimate=pl.CostEstimate(
            flops=2 * K1 * size * C0 * rows, bytes_accessed=12 * MIB, transcendentals=0
        ),
        name="keep_half",
    )(dconv, qk, pooled)


def add_kernel(a_ref, b_ref, out_ref):
    if a_ref.dtype == jnp.int16:
        a = decode(a_ref)
    else:
        a = [a_ref[:, begin:end] for begin, end in PARTS]
    encode([x + y for x, y in zip(a, decode(b_ref))], out_ref)


def add_half(a, b):
    return pl.pallas_call(
        add_kernel,
        out_shape=jax.ShapeDtypeStruct(b.shape, jnp.int16),
        compiler_params=params(8),
        name="add_half",
    )(a, b)


def join_kernel(mine_ref, other_ref, conv_ref, query_ref, key_ref):
    size = mine_ref.shape[0]
    core = lax.axis_index("dp") % 2
    for half, ref in ((core, mine_ref), (1 - core, other_ref)):
        rows = pl.ds(pl.multiple_of(half * size, 8), size)
        for x, out_ref in zip(decode(ref), (conv_ref, query_ref, key_ref)):
            out_ref[rows, :] = x


def join(mine, other):
    co = 2 * mine.shape[0]
    return pl.pallas_call(
        join_kernel,
        out_shape=[
            jax.ShapeDtypeStruct((co, K1 * C0), jnp.float32),
            jax.ShapeDtypeStruct((co, PC), jnp.float32),
            jax.ShapeDtypeStruct((co, PC), jnp.float32),
        ],
        compiler_params=params(8),
        name="join",
    )(mine, other)


def body(bases, stem_table, conv_weight, query_weight, key_weight, pair_grad):
    n = lax.axis_size("seq")
    rows_dev = bases.shape[1] // POOL

    own = bases.astype(jnp.bfloat16).reshape(2, rows_dev // 2, POOL).transpose(0, 2, 1)
    payload = gather_xor(own.reshape(2 * POOL, rows_dev // 2), "seq")

    first_table = jnp.pad(
        stem_table.transpose(2, 1, 0), ((0, 0), (0, 0), (1, WINDOW - 1 - K0))
    ).reshape(C0, 4 * WINDOW)
    first_table = jnp.pad(first_table, ((0, 0), (0, 128 - 4 * WINDOW))).astype(jnp.float32)
    table, weights, proj = prepare(n, first_table, conv_weight, query_weight, key_weight)

    pooled, slope, embed = stem_and_conv(n, payload, table, weights, pair_grad[0])
    embed_all = gather_xor(embed, "seq")
    send, dconv, qk = send_half(n, embed_all, proj, slope, pooled)
    received = swap(send, "dp", 1)
    keep = keep_half(dconv, qk, pooled)

    mine = add_half(keep, received)
    bit = 2
    while bit < lax.axis_size("dp"):
        mine = add_half(mine, swap(mine, "dp", bit))
        bit *= 2
    return tuple(join(mine, swap(mine, "dp", 1)))


def solution(mesh):
    return jax.shard_map(
        body,
        mesh=mesh,
        in_specs=(P("dp", "seq"), P(), P("seq", None), P(), P(), P("dp", "seq", None)),
        out_specs=(P("seq", None), P("seq", None), P("seq", None)),
        check_vma=False,
    )
```

```python
import functools

import jax
import jax.numpy as jnp
from jax import lax
from jax.experimental import pallas as pl
from jax.experimental.pallas import tpu as pltpu
from jax.sharding import PartitionSpec as P

C0 = 768
C1 = 768
PC = 128
K0 = 15
K1 = 5
POOL = 8
BIN_ROWS = 256
WINDOW = 24
CHUNK = 16
BLOCK = 512
LAG = 3
PAD = 128
SLOT = 128

ROOT = 0.7978845608028654
CUBE = 0.044715
HIGH = lax.Precision.HIGHEST
MIB = 1024 * 1024


def params(mib):
    return pltpu.CompilerParams(vmem_limit_bytes=mib * MIB)


def swap(x, axis, bit):
    size = lax.axis_size(axis)
    return lax.ppermute(x, axis, [(i, i ^ bit) for i in range(size)])


def gather_xor(x, axis):
    x = x[None]
    bit = 1
    while bit < lax.axis_size(axis):
        x = jnp.concatenate([x, swap(x, axis, bit)], axis=0)
        bit *= 2
    return x


def twice_gelu(v):
    return v + v * jnp.tanh(v * (ROOT + (ROOT * CUBE) * (v * v)))


def regroup_kernel(bases_ref, out_ref):
    lines, width = bases_ref.shape
    per = width // POOL
    rows = lines * per
    line = lax.broadcasted_iota(jnp.int32, (lines, rows), 0)
    column = lax.broadcasted_iota(jnp.int32, (lines, rows), 1)
    spread = lax.dot_general(
        bases_ref[...].astype(jnp.float32).astype(jnp.bfloat16),
        (column // per == line).astype(jnp.float32).astype(jnp.bfloat16),
        (((0,), (0,)), ((), ())),
        preferred_element_type=jnp.float32,
    )
    place = lax.broadcasted_iota(jnp.int32, (width, rows), 0) // POOL
    column = lax.broadcasted_iota(jnp.int32, (width, rows), 1)
    spread = jnp.where(place == column % per, spread, 0.0)
    grouped = spread[:POOL]
    for i in range(1, per):
        grouped = grouped + spread[i * POOL : (i + 1) * POOL]
    out_ref[...] = jnp.concatenate(
        [grouped[:, : rows // 2], grouped[:, rows // 2 :]], axis=0
    ).astype(jnp.bfloat16)


def regroup(bases):
    rows = bases.shape[1] // POOL
    return pl.pallas_call(
        regroup_kernel,
        out_shape=jax.ShapeDtypeStruct((2 * POOL, rows // 2), jnp.bfloat16),
        compiler_params=params(4),
        name="regroup",
    )(bases.reshape(bases.shape[1] // 128, 128))


def prepare_kernel(n, co, t0_ref, w_ref, wq_ref, wk_ref, table_ref, weights_ref, proj_ref):
    for chunk in range(C0 // CHUNK):
        part = t0_ref[chunk * CHUNK : (chunk + 1) * CHUNK, :]
        for pos in range(POOL):
            shifted = part if pos == 0 else pltpu.roll(part, pos, 1)
            first = (chunk * POOL + pos) * CHUNK
            table_ref[first : first + CHUNK, :] = shifted.astype(jnp.bfloat16)
    for tap in range(K1):
        weights_ref[tap * co : (tap + 1) * co, :] = w_ref[:, tap * C0 : (tap + 1) * C0] * 0.5
    for slot in range(n):
        rows = slice(slot * co, (slot + 1) * co)
        proj_ref[slot * SLOT : slot * SLOT + co, :PC] = wq_ref[rows, :]
        proj_ref[slot * SLOT : slot * SLOT + co, PC:] = wk_ref[rows, :]
        proj_ref[slot * SLOT + co : (slot + 1) * SLOT, :] = jnp.zeros(
            (SLOT - co, 2 * PC), jnp.bfloat16
        )


def prepare(n, first_table, conv_weight, query_weight, key_weight):
    co = conv_weight.shape[0]
    return pl.pallas_call(
        functools.partial(prepare_kernel, n, co),
        out_shape=[
            jax.ShapeDtypeStruct((POOL * C0, 128), jnp.bfloat16),
            jax.ShapeDtypeStruct((K1 * co, C0), jnp.bfloat16),
            jax.ShapeDtypeStruct((n * SLOT, 2 * PC), jnp.bfloat16),
        ],
        compiler_params=params(8),
        cost_estimate=pl.CostEstimate(flops=0, bytes_accessed=5 * MIB, transcendentals=0),
        name="prepare",
    )(first_table, conv_weight, query_weight, key_weight)


def stem_kernel(
    n, rows_dev, co, pay_ref, table, weights, grad_ref, p_ref, slope_ref, emb_ref,
    bases, ybuf, sums
):
    rows = n * rows_dev
    blocks = rows // BLOCK
    front = LAG * BLOCK + PAD

    def convolve(block):
        first = pl.multiple_of((block + LAG) * BLOCK, 128)
        conv = None
        for tap in range(K1):
            near = ybuf[tap * co : (tap + 1) * co, pl.ds(first, BLOCK + 2 * PAD)]
            begin = PAD + tap - K1 // 2
            part = near[:, begin : begin + BLOCK]
            conv = part if conv is None else conv + part
        square = conv * conv
        tangent = jnp.tanh(conv * (ROOT + (ROOT * CUBE) * square))
        half = 0.5 * conv
        gelu = half + half * tangent
        to = pl.multiple_of(jnp.maximum(block, 0) * BLOCK, 128)
        slope_ref[:, pl.ds(to, BLOCK)] = (0.5 + 0.5 * tangent) + half * (1.0 - tangent * tangent) * (
            ROOT + (3.0 * ROOT * CUBE) * square
        )
        lane = lax.broadcasted_iota(jnp.int32, (co, 128), 1)
        total = sums[:co, :]
        for part in range(BLOCK // BIN_ROWS):
            mean = jnp.sum(
                gelu[:, part * BIN_ROWS : (part + 1) * BIN_ROWS], axis=1, keepdims=True
            ) * (1.0 / BIN_ROWS)
            total = jnp.where(lane == block * (BLOCK // BIN_ROWS) + part, mean, total)
        sums[:co, :] = total

    def taps(block):
        ybuf[:, pl.ds(pl.multiple_of(front + block * BLOCK, 128), BLOCK)] = jnp.dot(
            weights[...],
            p_ref[:, pl.ds(pl.multiple_of(jnp.maximum(block, 0) * BLOCK, 128), BLOCK)],
            preferred_element_type=jnp.float32,
        )

    me = lax.axis_index("seq")
    bases[:, :PAD] = jnp.full((POOL, PAD), -1.0, jnp.float32)
    bases[:, PAD + rows :] = jnp.full((POOL, PAD), -1.0, jnp.float32)
    half = rows_dev // 2
    for slab in range(n):
        block = pay_ref[jnp.bitwise_xor(me, slab)].astype(jnp.float32)
        first = PAD + slab * rows_dev
        bases[:, first : first + half] = block[:POOL]
        bases[:, first + half : first + 2 * half] = block[POOL:]
    ybuf[:, front + rows :] = jnp.zeros((K1 * co, PAD), jnp.float32)
    p_ref[:, :BLOCK] = jnp.zeros((C0, BLOCK), jnp.bfloat16)
    sums[...] = jnp.zeros(sums.shape, jnp.float32)

    def main(step, carry):
        first = pl.multiple_of(step * BLOCK, 128)
        near = bases[:, pl.ds(first, BLOCK + 2 * PAD)]
        window = jnp.concatenate(
            [near[:, PAD + q : PAD + q + BLOCK] for q in (-1, 0, 1)], axis=0
        )
        onehot = jnp.concatenate(
            [(window == b).astype(jnp.float32) for b in range(4)]
            + [jnp.zeros((128 - 4 * WINDOW, BLOCK), jnp.float32)],
            axis=0,
        ).astype(jnp.bfloat16)
        convolve(step - LAG)
        taps(step - 1)
        for at in range(0, BLOCK, 256):
            for chunk in range(C0 // CHUNK):
                stem = jnp.dot(
                    table[chunk * POOL * CHUNK : (chunk + 1) * POOL * CHUNK, :],
                    onehot[:, at : at + 256],
                    preferred_element_type=jnp.float32,
                )
                most = least = stem[:CHUNK]
                for pos in range(1, POOL):
                    part = stem[pos * CHUNK : (pos + 1) * CHUNK]
                    most = jnp.maximum(most, part)
                    least = jnp.minimum(least, part)
                p_ref[
                    chunk * CHUNK : (chunk + 1) * CHUNK, pl.ds(pl.multiple_of(first + at, 128), 256)
                ] = jnp.maximum(twice_gelu(most), twice_gelu(least)).astype(jnp.bfloat16)
        return carry

    lax.fori_loop(0, blocks, main, 0)
    taps(blocks - 1)
    for last in range(LAG):
        convolve(blocks - LAG + last)

    own_pos, npos = grad_ref.shape
    embed = sums[...].T[:npos, :].astype(jnp.bfloat16).astype(jnp.float32)
    rest = grad_ref[...]
    parts = []
    for _ in range(3):
        part = rest.astype(jnp.bfloat16).astype(jnp.float32)
        parts.append(part)
        rest = rest - part
    grads = jnp.concatenate(
        parts + [jnp.zeros((npos - 3 * own_pos, npos), jnp.float32)], axis=0
    )
    emb_ref[...] = jnp.concatenate(
        [embed[:, :co], grads, jnp.zeros((npos, SLOT - co - npos), jnp.float32)], axis=1
    ).astype(jnp.bfloat16)


def stem_and_conv(n, payload, table, weights, pair_grad):
    co = weights.shape[0] // K1
    rows_dev = payload.shape[2] * 2
    rows = n * rows_dev
    npos = rows // BIN_ROWS
    return pl.pallas_call(
        functools.partial(stem_kernel, n, rows_dev, co),
        out_shape=[
            jax.ShapeDtypeStruct((C0, rows), jnp.bfloat16),
            jax.ShapeDtypeStruct((co, rows), jnp.float32),
            jax.ShapeDtypeStruct((npos, SLOT), jnp.bfloat16),
        ],
        scratch_shapes=[
            pltpu.VMEM((POOL, rows + 2 * PAD), jnp.float32),
            pltpu.VMEM((K1 * co, LAG * BLOCK + rows + 2 * PAD), jnp.float32),
            pltpu.VMEM((128, 128), jnp.float32),
        ],
        compiler_params=params(36),
        name="stem_and_conv",
    )(payload, table, weights, pair_grad)


WIDE = K1 * C0 + 2 * PC
PARTS = ((0, K1 * C0), (K1 * C0, K1 * C0 + PC), (K1 * C0 + PC, WIDE))
CODED = WIDE + 128


def encode(values, out_ref):
    exponents = []
    for (begin, end), x in zip(PARTS, values):
        top = jnp.maximum(jnp.max(jnp.abs(x), axis=1, keepdims=True), 1e-30)
        exponent = jnp.floor(jnp.log2(32000.0 / top))
        scaled = jnp.floor(x * jnp.exp2(exponent) + 0.5)
        out_ref[:, begin:end] = scaled.astype(jnp.int32).astype(jnp.int16)
        exponents.append(exponent)
    lane = lax.broadcasted_iota(jnp.int32, (out_ref.shape[0], 128), 1)
    packed = jnp.where(lane == 0, exponents[0], jnp.where(lane == 1, exponents[1], exponents[2]))
    out_ref[:, WIDE:] = packed.astype(jnp.int32).astype(jnp.int16)


def decode(ref):
    exponents = ref[:, WIDE:].astype(jnp.int32).astype(jnp.float32)
    return [
        ref[:, begin:end].astype(jnp.int32).astype(jnp.float32) * jnp.exp2(-exponents[:, at : at + 1])
        for at, (begin, end) in enumerate(PARTS)
    ]


def half_gradient(half, dconv, qk_ref, pooled_ref, out_ref, shifted):
    size = out_ref.shape[0]
    held = dconv.shape[1]
    rows = pooled_ref.shape[1]
    shifted[K1 * held :, :] = jnp.zeros((shifted.shape[0] - K1 * held, rows), jnp.bfloat16)
    for first in range(0, rows, BLOCK):
        near = dconv[half, :, first : first + BLOCK + 2 * PAD]
        for tap in range(K1):
            begin = PAD - tap + K1 // 2
            shifted[tap * held : (tap + 1) * held, first : first + BLOCK] = near[
                :, begin : begin + BLOCK
            ]
    product = lax.dot_general(
        pooled_ref[...], shifted[...], (((1,), (1,)), ((), ())), preferred_element_type=jnp.float32
    ).T
    conv = jnp.concatenate(
        [product[tap * held : tap * held + size, :] for tap in range(K1)], axis=1
    )
    if out_ref.dtype == jnp.int16:
        qk = qk_ref[half]
        encode((conv, qk[:, :PC], qk[:, PC:]), out_ref)
    else:
        out_ref[:, : K1 * C0] = conv
        out_ref[:, K1 * C0 :] = qk_ref[half]


def send_kernel(n, emb_ref, proj_ref, slope_ref, pooled_ref, send_ref, dconv_ref, qk_ref, shifted):
    co, rows = slope_ref.shape
    size, held = co // 2, dconv_ref.shape[1]
    npos = rows // BIN_ROWS
    own_pos = npos // n
    scale = PC**-0.5
    me = lax.axis_index("seq")
    both = jnp.dot(
        jnp.concatenate([emb_ref[jnp.bitwise_xor(me, slab)] for slab in range(n)], axis=1),
        proj_ref[...],
        preferred_element_type=jnp.float32,
    )
    query, keys = both[:, :PC], both[:, PC:]
    pieces = []
    for slab in range(n):
        block = emb_ref[jnp.bitwise_xor(me, slab)].astype(jnp.float32)
        total = block[:own_pos]
        for part in range(1, 3):
            total = total + block[part * own_pos : (part + 1) * own_pos]
        pieces.append(total)
    grad = jnp.concatenate(pieces, axis=0)[:, co : co + npos]
    dquery = jnp.dot(grad, keys, precision=HIGH, preferred_element_type=jnp.float32) * scale
    dkeys = (
        lax.dot_general(
            grad, query, (((0,), (0,)), ((), ())), precision=HIGH,
            preferred_element_type=jnp.float32,
        )
        * scale
    )
    cotangent = jnp.concatenate([dquery, dkeys], axis=1)
    own = pl.ds(pl.multiple_of(me * SLOT, SLOT), SLOT)
    dembed = lax.dot_general(
        proj_ref[own, :].astype(jnp.float32), cotangent,
        (((1,), (1,)), ((), ())), precision=HIGH, preferred_element_type=jnp.float32,
    ) * (0.5 / BIN_ROWS)
    qk = lax.dot_general(
        emb_ref[0].astype(jnp.float32), cotangent, (((0,), (0,)), ((), ())),
        precision=HIGH, preferred_element_type=jnp.float32,
    )
    edge = jnp.zeros((held, PAD), jnp.bfloat16)
    for half in range(2):
        channels = slice(half * size, (half + 1) * size)
        qk_ref[half] = qk[channels]
        dconv_ref[half, :, :PAD] = edge
        dconv_ref[half, :, PAD + rows :] = edge
        for pos in range(npos):
            part = slope_ref[channels, pos * BIN_ROWS : (pos + 1) * BIN_ROWS] * dembed[
                channels, pos : pos + 1
            ]
            if held > size:
                part = jnp.concatenate(
                    [part, jnp.zeros((held - size, BIN_ROWS), jnp.float32)], axis=0
                )
            dconv_ref[half, :, PAD + pos * BIN_ROWS : PAD + (pos + 1) * BIN_ROWS] = part.astype(
                jnp.bfloat16
            )
    half_gradient(1 - lax.axis_index("dp") % 2, dconv_ref, qk_ref, pooled_ref, send_ref, shifted)


def keep_kernel(dconv_ref, qk_ref, pooled_ref, keep_ref, shifted):
    half_gradient(lax.axis_index("dp") % 2, dconv_ref, qk_ref, pooled_ref, keep_ref, shifted)


def send_half(n, embed, proj, slope, pooled):
    co, rows = slope.shape
    size = co // 2
    held = -(-size // 16) * 16
    return pl.pallas_call(
        functools.partial(send_kernel, n),
        out_shape=[
            jax.ShapeDtypeStruct((size, CODED), jnp.int16),
            jax.ShapeDtypeStruct((2, held, rows + 2 * PAD), jnp.bfloat16),
            jax.ShapeDtypeStruct((2, size, 2 * PC), jnp.float32),
        ],
        scratch_shapes=[pltpu.VMEM((256, rows), jnp.bfloat16)],
        compiler_params=params(32),
        name="send_half",
    )(embed, proj, slope, pooled)


def keep_half(dconv, qk, pooled):
    size, rows = qk.shape[1], pooled.shape[1]
    return pl.pallas_call(
        keep_kernel,
        out_shape=jax.ShapeDtypeStruct((size, WIDE), jnp.float32),
        scratch_shapes=[pltpu.VMEM((256, rows), jnp.bfloat16)],
        compiler_params=params(32),
        cost_estimate=pl.CostEstimate(
            flops=2 * K1 * size * C0 * rows, bytes_accessed=12 * MIB, transcendentals=0
        ),
        name="keep_half",
    )(dconv, qk, pooled)


def add_kernel(a_ref, b_ref, out_ref):
    if a_ref.dtype == jnp.int16:
        a = decode(a_ref)
    else:
        a = [a_ref[:, begin:end] for begin, end in PARTS]
    encode([x + y for x, y in zip(a, decode(b_ref))], out_ref)


def add_half(a, b):
    return pl.pallas_call(
        add_kernel,
        out_shape=jax.ShapeDtypeStruct(b.shape, jnp.int16),
        compiler_params=params(8),
        name="add_half",
    )(a, b)


def join_kernel(mine_ref, other_ref, conv_ref, query_ref, key_ref):
    size = mine_ref.shape[0]
    core = lax.axis_index("dp") % 2
    for half, ref in ((core, mine_ref), (1 - core, other_ref)):
        rows = pl.ds(pl.multiple_of(half * size, 8), size)
        for x, out_ref in zip(decode(ref), (conv_ref, query_ref, key_ref)):
            out_ref[rows, :] = x


def join(mine, other):
    co = 2 * mine.shape[0]
    return pl.pallas_call(
        join_kernel,
        out_shape=[
            jax.ShapeDtypeStruct((co, K1 * C0), jnp.float32),
            jax.ShapeDtypeStruct((co, PC), jnp.float32),
            jax.ShapeDtypeStruct((co, PC), jnp.float32),
        ],
        compiler_params=params(8),
        name="join",
    )(mine, other)


def body(bases, stem_table, conv_weight, query_weight, key_weight, pair_grad):
    n = lax.axis_size("seq")
    payload = gather_xor(regroup(bases), "seq")

    first_table = jnp.pad(
        stem_table.transpose(2, 1, 0), ((0, 0), (0, 0), (1, WINDOW - 1 - K0))
    ).reshape(C0, 4 * WINDOW)
    first_table = jnp.pad(first_table, ((0, 0), (0, 128 - 4 * WINDOW))).astype(jnp.float32)
    table, weights, proj = prepare(n, first_table, conv_weight, query_weight, key_weight)

    pooled, slope, embed = stem_and_conv(n, payload, table, weights, pair_grad[0])
    embed_all = gather_xor(embed, "seq")
    send, dconv, qk = send_half(n, embed_all, proj, slope, pooled)
    received = swap(send, "dp", 1)
    keep = keep_half(dconv, qk, pooled)

    mine = add_half(keep, received)
    bit = 2
    while bit < lax.axis_size("dp"):
        mine = add_half(mine, swap(mine, "dp", bit))
        bit *= 2
    return tuple(join(mine, swap(mine, "dp", 1)))


def solution(mesh):
    return jax.shard_map(
        body,
        mesh=mesh,
        in_specs=(P("dp", "seq"), P(), P("seq", None), P(), P(), P("dp", "seq", None)),
        out_specs=(P("seq", None), P("seq", None), P("seq", None)),
        check_vma=False,
    )
```

```python
import functools

import jax
import jax.numpy as jnp
from jax import lax
from jax.experimental import pallas as pl
from jax.experimental.pallas import tpu as pltpu
from jax.sharding import PartitionSpec as P

C0 = 768
C1 = 768
PC = 128
K0 = 15
K1 = 5
POOL = 8
BIN_ROWS = 256
WINDOW = 24
CHUNK = 16
BLOCK = 512
LAG = 3
PAD = 128
SLOT = 128

ROOT = 0.7978845608028654
CUBE = 0.044715
HIGH = lax.Precision.HIGHEST
MIB = 1024 * 1024


def params(mib):
    return pltpu.CompilerParams(vmem_limit_bytes=mib * MIB)


def swap(x, axis, bit):
    size = lax.axis_size(axis)
    return lax.ppermute(x, axis, [(i, i ^ bit) for i in range(size)])


def gather_xor(x, axis):
    x = x[None]
    bit = 1
    while bit < lax.axis_size(axis):
        x = jnp.concatenate([x, swap(x, axis, bit)], axis=0)
        bit *= 2
    return x


def twice_gelu(v):
    return v + v * jnp.tanh(v * (ROOT + (ROOT * CUBE) * (v * v)))


def regroup_kernel(bases_ref, out_ref):
    lines, width = bases_ref.shape
    per = width // POOL
    rows = lines * per
    line = lax.broadcasted_iota(jnp.int32, (lines, rows), 0)
    column = lax.broadcasted_iota(jnp.int32, (lines, rows), 1)
    spread = lax.dot_general(
        bases_ref[...].astype(jnp.float32).astype(jnp.bfloat16),
        (column // per == line).astype(jnp.float32).astype(jnp.bfloat16),
        (((0,), (0,)), ((), ())),
        preferred_element_type=jnp.float32,
    )
    place = lax.broadcasted_iota(jnp.int32, (width, rows), 0) // POOL
    column = lax.broadcasted_iota(jnp.int32, (width, rows), 1)
    spread = jnp.where(place == column % per, spread, 0.0)
    grouped = spread[:POOL]
    for i in range(1, per):
        grouped = grouped + spread[i * POOL : (i + 1) * POOL]
    out_ref[...] = jnp.concatenate(
        [grouped[:, : rows // 2], grouped[:, rows // 2 :]], axis=0
    ).astype(jnp.bfloat16)


def regroup(bases):
    rows = bases.shape[1] // POOL
    return pl.pallas_call(
        regroup_kernel,
        out_shape=jax.ShapeDtypeStruct((2 * POOL, rows // 2), jnp.bfloat16),
        compiler_params=params(4),
        name="regroup",
    )(bases.reshape(bases.shape[1] // 128, 128))


def prepare_kernel(n, co, t0_ref, w_ref, wq_ref, wk_ref, table_ref, weights_ref, proj_ref):
    for chunk in range(C0 // CHUNK):
        part = t0_ref[chunk * CHUNK : (chunk + 1) * CHUNK, :]
        for pos in range(POOL):
            shifted = part if pos == 0 else pltpu.roll(part, pos, 1)
            first = (chunk * POOL + pos) * CHUNK
            table_ref[first : first + CHUNK, :] = shifted.astype(jnp.bfloat16)
    for tap in range(K1):
        weights_ref[tap * co : (tap + 1) * co, :] = w_ref[:, tap * C0 : (tap + 1) * C0] * 0.5
    for slot in range(n):
        rows = slice(slot * co, (slot + 1) * co)
        proj_ref[slot * SLOT : slot * SLOT + co, :PC] = wq_ref[rows, :]
        proj_ref[slot * SLOT : slot * SLOT + co, PC:] = wk_ref[rows, :]
        proj_ref[slot * SLOT + co : (slot + 1) * SLOT, :] = jnp.zeros(
            (SLOT - co, 2 * PC), jnp.bfloat16
        )


def prepare(n, first_table, conv_weight, query_weight, key_weight):
    co = conv_weight.shape[0]
    return pl.pallas_call(
        functools.partial(prepare_kernel, n, co),
        out_shape=[
            jax.ShapeDtypeStruct((POOL * C0, 128), jnp.bfloat16),
            jax.ShapeDtypeStruct((K1 * co, C0), jnp.bfloat16),
            jax.ShapeDtypeStruct((n * SLOT, 2 * PC), jnp.bfloat16),
        ],
        compiler_params=params(8),
        cost_estimate=pl.CostEstimate(flops=0, bytes_accessed=5 * MIB, transcendentals=0),
        name="prepare",
    )(first_table, conv_weight, query_weight, key_weight)


def stem_kernel(
    n, rows_dev, co, pay_ref, table, weights, grad_ref, p_ref, slope_ref, emb_ref,
    bases, ybuf, sums
):
    rows = n * rows_dev
    blocks = rows // BLOCK
    front = LAG * BLOCK + PAD

    group = 16

    def convolve(block, row, part):
        first = pl.multiple_of((block + LAG) * BLOCK + part * BIN_ROWS, 128)
        conv = None
        for tap in range(K1):
            near = ybuf[tap * co + row : tap * co + row + group, pl.ds(first, BIN_ROWS + 2 * PAD)]
            begin = PAD + tap - K1 // 2
            shifted = near[:, begin : begin + BIN_ROWS]
            conv = shifted if conv is None else conv + shifted
        square = conv * conv
        tangent = jnp.tanh(conv * (ROOT + (ROOT * CUBE) * square))
        half = 0.5 * conv
        gelu = half + half * tangent
        to = pl.multiple_of(jnp.maximum(block, 0) * BLOCK + part * BIN_ROWS, 128)
        slope_ref[row : row + group, pl.ds(to, BIN_ROWS)] = (0.5 + 0.5 * tangent) + half * (
            1.0 - tangent * tangent
        ) * (ROOT + (3.0 * ROOT * CUBE) * square)
        mean = jnp.sum(gelu, axis=1, keepdims=True) * (1.0 / BIN_ROWS)
        lane = lax.broadcasted_iota(jnp.int32, (group, 128), 1)
        sums[row : row + group, :] = jnp.where(
            lane == block * (BLOCK // BIN_ROWS) + part, mean, sums[row : row + group, :]
        )

    def taps(block):
        ybuf[:, pl.ds(pl.multiple_of(front + block * BLOCK, 128), BLOCK)] = jnp.dot(
            weights[...],
            p_ref[:, pl.ds(pl.multiple_of(jnp.maximum(block, 0) * BLOCK, 128), BLOCK)],
            preferred_element_type=jnp.float32,
        )

    me = lax.axis_index("seq")
    bases[:, :PAD] = jnp.full((POOL, PAD), -1.0, jnp.float32)
    bases[:, PAD + rows :] = jnp.full((POOL, PAD), -1.0, jnp.float32)
    half = rows_dev // 2
    for slab in range(n):
        block = pay_ref[jnp.bitwise_xor(me, slab)].astype(jnp.float32)
        first = PAD + slab * rows_dev
        bases[:, first : first + half] = block[:POOL]
        bases[:, first + half : first + 2 * half] = block[POOL:]
    ybuf[:, front + rows :] = jnp.zeros((K1 * co, PAD), jnp.float32)
    p_ref[:, :BLOCK] = jnp.zeros((C0, BLOCK), jnp.bfloat16)
    sums[...] = jnp.zeros(sums.shape, jnp.float32)

    def main(step, carry):
        first = pl.multiple_of(step * BLOCK, 128)
        near = bases[:, pl.ds(first, BLOCK + 2 * PAD)]
        window = jnp.concatenate(
            [near[:, PAD + q : PAD + q + BLOCK] for q in (-1, 0, 1)], axis=0
        )
        onehot = jnp.concatenate(
            [(window == b).astype(jnp.float32) for b in range(4)]
            + [jnp.zeros((128 - 4 * WINDOW, BLOCK), jnp.float32)],
            axis=0,
        ).astype(jnp.bfloat16)
        taps(step - 1)
        every = (C0 // CHUNK) // (co // group)
        for at in range(0, BLOCK, 256):
            for chunk in range(C0 // CHUNK):
                if chunk % every == 0:
                    convolve(step - LAG, chunk // every * group, at // 256)
                stem = jnp.dot(
                    table[chunk * POOL * CHUNK : (chunk + 1) * POOL * CHUNK, :],
                    onehot[:, at : at + 256],
                    preferred_element_type=jnp.float32,
                )
                most = least = stem[:CHUNK]
                for pos in range(1, POOL):
                    part = stem[pos * CHUNK : (pos + 1) * CHUNK]
                    most = jnp.maximum(most, part)
                    least = jnp.minimum(least, part)
                p_ref[
                    chunk * CHUNK : (chunk + 1) * CHUNK, pl.ds(pl.multiple_of(first + at, 128), 256)
                ] = jnp.maximum(twice_gelu(most), twice_gelu(least)).astype(jnp.bfloat16)
        return carry

    lax.fori_loop(0, blocks, main, 0)
    taps(blocks - 1)
    for last in range(LAG):
        for row in range(0, co, group):
            for part in range(BLOCK // BIN_ROWS):
                convolve(blocks - LAG + last, row, part)

    own_pos, npos = grad_ref.shape
    embed = sums[...].T[:npos, :].astype(jnp.bfloat16).astype(jnp.float32)
    rest = grad_ref[...]
    parts = []
    for _ in range(3):
        part = rest.astype(jnp.bfloat16).astype(jnp.float32)
        parts.append(part)
        rest = rest - part
    grads = jnp.concatenate(
        parts + [jnp.zeros((npos - 3 * own_pos, npos), jnp.float32)], axis=0
    )
    emb_ref[...] = jnp.concatenate(
        [embed[:, :co], grads, jnp.zeros((npos, SLOT - co - npos), jnp.float32)], axis=1
    ).astype(jnp.bfloat16)


def stem_and_conv(n, payload, table, weights, pair_grad):
    co = weights.shape[0] // K1
    rows_dev = payload.shape[2] * 2
    rows = n * rows_dev
    npos = rows // BIN_ROWS
    return pl.pallas_call(
        functools.partial(stem_kernel, n, rows_dev, co),
        out_shape=[
            jax.ShapeDtypeStruct((C0, rows), jnp.bfloat16),
            jax.ShapeDtypeStruct((co, rows), jnp.float32),
            jax.ShapeDtypeStruct((npos, SLOT), jnp.bfloat16),
        ],
        scratch_shapes=[
            pltpu.VMEM((POOL, rows + 2 * PAD), jnp.float32),
            pltpu.VMEM((K1 * co, LAG * BLOCK + rows + 2 * PAD), jnp.float32),
            pltpu.VMEM((128, 128), jnp.float32),
        ],
        compiler_params=params(36),
        name="stem_and_conv",
    )(payload, table, weights, pair_grad)


WIDE = K1 * C0 + 2 * PC
PARTS = ((0, K1 * C0), (K1 * C0, K1 * C0 + PC), (K1 * C0 + PC, WIDE))
CODED = WIDE + 128


def encode(values, out_ref):
    exponents = []
    for (begin, end), x in zip(PARTS, values):
        top = jnp.maximum(jnp.max(jnp.abs(x), axis=1, keepdims=True), 1e-30)
        exponent = jnp.floor(jnp.log2(32000.0 / top))
        scaled = jnp.floor(x * jnp.exp2(exponent) + 0.5)
        out_ref[:, begin:end] = scaled.astype(jnp.int32).astype(jnp.int16)
        exponents.append(exponent)
    lane = lax.broadcasted_iota(jnp.int32, (out_ref.shape[0], 128), 1)
    packed = jnp.where(lane == 0, exponents[0], jnp.where(lane == 1, exponents[1], exponents[2]))
    out_ref[:, WIDE:] = packed.astype(jnp.int32).astype(jnp.int16)


def decode(ref):
    exponents = ref[:, WIDE:].astype(jnp.int32).astype(jnp.float32)
    return [
        ref[:, begin:end].astype(jnp.int32).astype(jnp.float32) * jnp.exp2(-exponents[:, at : at + 1])
        for at, (begin, end) in enumerate(PARTS)
    ]


def half_gradient(half, dconv, qk_ref, pooled_ref, out_ref, shifted):
    size = out_ref.shape[0]
    held = dconv.shape[1]
    rows = pooled_ref.shape[1]
    shifted[K1 * held :, :] = jnp.zeros((shifted.shape[0] - K1 * held, rows), jnp.bfloat16)
    for first in range(0, rows, BLOCK):
        near = dconv[half, :, first : first + BLOCK + 2 * PAD]
        for tap in range(K1):
            begin = PAD - tap + K1 // 2
            shifted[tap * held : (tap + 1) * held, first : first + BLOCK] = near[
                :, begin : begin + BLOCK
            ]
    product = lax.dot_general(
        pooled_ref[...], shifted[...], (((1,), (1,)), ((), ())), preferred_element_type=jnp.float32
    ).T
    conv = jnp.concatenate(
        [product[tap * held : tap * held + size, :] for tap in range(K1)], axis=1
    )
    if out_ref.dtype == jnp.int16:
        qk = qk_ref[half]
        encode((conv, qk[:, :PC], qk[:, PC:]), out_ref)
    else:
        out_ref[:, : K1 * C0] = conv
        out_ref[:, K1 * C0 :] = qk_ref[half]


def send_kernel(n, emb_ref, proj_ref, slope_ref, pooled_ref, send_ref, dconv_ref, qk_ref, shifted):
    co, rows = slope_ref.shape
    size, held = co // 2, dconv_ref.shape[1]
    npos = rows // BIN_ROWS
    own_pos = npos // n
    scale = PC**-0.5
    me = lax.axis_index("seq")
    both = jnp.dot(
        jnp.concatenate([emb_ref[jnp.bitwise_xor(me, slab)] for slab in range(n)], axis=1),
        proj_ref[...],
        preferred_element_type=jnp.float32,
    )
    query, keys = both[:, :PC], both[:, PC:]
    pieces = []
    for slab in range(n):
        block = emb_ref[jnp.bitwise_xor(me, slab)].astype(jnp.float32)
        total = block[:own_pos]
        for part in range(1, 3):
            total = total + block[part * own_pos : (part + 1) * own_pos]
        pieces.append(total)
    grad = jnp.concatenate(pieces, axis=0)[:, co : co + npos]
    dquery = jnp.dot(grad, keys, precision=HIGH, preferred_element_type=jnp.float32) * scale
    dkeys = (
        lax.dot_general(
            grad, query, (((0,), (0,)), ((), ())), precision=HIGH,
            preferred_element_type=jnp.float32,
        )
        * scale
    )
    cotangent = jnp.concatenate([dquery, dkeys], axis=1)
    own = pl.ds(pl.multiple_of(me * SLOT, SLOT), SLOT)
    dembed = lax.dot_general(
        proj_ref[own, :].astype(jnp.float32), cotangent,
        (((1,), (1,)), ((), ())), precision=HIGH, preferred_element_type=jnp.float32,
    ) * (0.5 / BIN_ROWS)
    qk = lax.dot_general(
        emb_ref[0].astype(jnp.float32), cotangent, (((0,), (0,)), ((), ())),
        precision=HIGH, preferred_element_type=jnp.float32,
    )
    edge = jnp.zeros((held, PAD), jnp.bfloat16)
    for half in range(2):
        channels = slice(half * size, (half + 1) * size)
        qk_ref[half] = qk[channels]
        dconv_ref[half, :, :PAD] = edge
        dconv_ref[half, :, PAD + rows :] = edge
        for pos in range(npos):
            part = slope_ref[channels, pos * BIN_ROWS : (pos + 1) * BIN_ROWS] * dembed[
                channels, pos : pos + 1
            ]
            if held > size:
                part = jnp.concatenate(
                    [part, jnp.zeros((held - size, BIN_ROWS), jnp.float32)], axis=0
                )
            dconv_ref[half, :, PAD + pos * BIN_ROWS : PAD + (pos + 1) * BIN_ROWS] = part.astype(
                jnp.bfloat16
            )
    half_gradient(1 - lax.axis_index("dp") % 2, dconv_ref, qk_ref, pooled_ref, send_ref, shifted)


def keep_kernel(dconv_ref, qk_ref, pooled_ref, keep_ref, shifted):
    half_gradient(lax.axis_index("dp") % 2, dconv_ref, qk_ref, pooled_ref, keep_ref, shifted)


def send_half(n, embed, proj, slope, pooled):
    co, rows = slope.shape
    size = co // 2
    held = -(-size // 16) * 16
    return pl.pallas_call(
        functools.partial(send_kernel, n),
        out_shape=[
            jax.ShapeDtypeStruct((size, CODED), jnp.int16),
            jax.ShapeDtypeStruct((2, held, rows + 2 * PAD), jnp.bfloat16),
            jax.ShapeDtypeStruct((2, size, 2 * PC), jnp.float32),
        ],
        scratch_shapes=[pltpu.VMEM((256, rows), jnp.bfloat16)],
        compiler_params=params(32),
        name="send_half",
    )(embed, proj, slope, pooled)


def keep_half(dconv, qk, pooled):
    size, rows = qk.shape[1], pooled.shape[1]
    return pl.pallas_call(
        keep_kernel,
        out_shape=jax.ShapeDtypeStruct((size, WIDE), jnp.float32),
        scratch_shapes=[pltpu.VMEM((256, rows), jnp.bfloat16)],
        compiler_params=params(32),
        cost_estimate=pl.CostEstimate(
            flops=2 * K1 * size * C0 * rows, bytes_accessed=12 * MIB, transcendentals=0
        ),
        name="keep_half",
    )(dconv, qk, pooled)


def add_kernel(a_ref, b_ref, out_ref):
    if a_ref.dtype == jnp.int16:
        a = decode(a_ref)
    else:
        a = [a_ref[:, begin:end] for begin, end in PARTS]
    encode([x + y for x, y in zip(a, decode(b_ref))], out_ref)


def add_half(a, b):
    return pl.pallas_call(
        add_kernel,
        out_shape=jax.ShapeDtypeStruct(b.shape, jnp.int16),
        compiler_params=params(8),
        name="add_half",
    )(a, b)


def join_kernel(mine_ref, other_ref, conv_ref, query_ref, key_ref):
    size = mine_ref.shape[0]
    core = lax.axis_index("dp") % 2
    for half, ref in ((core, mine_ref), (1 - core, other_ref)):
        rows = pl.ds(pl.multiple_of(half * size, 8), size)
        for x, out_ref in zip(decode(ref), (conv_ref, query_ref, key_ref)):
            out_ref[rows, :] = x


def join(mine, other):
    co = 2 * mine.shape[0]
    return pl.pallas_call(
        join_kernel,
        out_shape=[
            jax.ShapeDtypeStruct((co, K1 * C0), jnp.float32),
            jax.ShapeDtypeStruct((co, PC), jnp.float32),
            jax.ShapeDtypeStruct((co, PC), jnp.float32),
        ],
        compiler_params=params(8),
        name="join",
    )(mine, other)


def body(bases, stem_table, conv_weight, query_weight, key_weight, pair_grad):
    n = lax.axis_size("seq")
    payload = gather_xor(regroup(bases), "seq")

    first_table = jnp.pad(
        stem_table.transpose(2, 1, 0), ((0, 0), (0, 0), (1, WINDOW - 1 - K0))
    ).reshape(C0, 4 * WINDOW)
    first_table = jnp.pad(first_table, ((0, 0), (0, 128 - 4 * WINDOW))).astype(jnp.float32)
    table, weights, proj = prepare(n, first_table, conv_weight, query_weight, key_weight)

    pooled, slope, embed = stem_and_conv(n, payload, table, weights, pair_grad[0])
    embed_all = gather_xor(embed, "seq")
    send, dconv, qk = send_half(n, embed_all, proj, slope, pooled)
    received = swap(send, "dp", 1)
    keep = keep_half(dconv, qk, pooled)

    mine = add_half(keep, received)
    bit = 2
    while bit < lax.axis_size("dp"):
        mine = add_half(mine, swap(mine, "dp", bit))
        bit *= 2
    return tuple(join(mine, swap(mine, "dp", 1)))


def solution(mesh):
    return jax.shard_map(
        body,
        mesh=mesh,
        in_specs=(P("dp", "seq"), P(), P("seq", None), P(), P(), P("dp", "seq", None)),
        out_specs=(P("seq", None), P("seq", None), P("seq", None)),
        check_vma=False,
    )
```

```python
import functools

import jax
import jax.numpy as jnp
from jax import lax
from jax.experimental import pallas as pl
from jax.experimental.pallas import tpu as pltpu
from jax.sharding import PartitionSpec as P

C0 = 768
C1 = 768
PC = 128
K0 = 15
K1 = 5
POOL = 8
BIN_ROWS = 256
WINDOW = 24
CHUNK = 16
BLOCK = 1024
LAG = 3
PAD = 128
SLOT = 128

ROOT = 0.7978845608028654
CUBE = 0.044715
HIGH = lax.Precision.HIGHEST
MIB = 1024 * 1024


def params(mib):
    return pltpu.CompilerParams(vmem_limit_bytes=mib * MIB)


def swap(x, axis, bit):
    size = lax.axis_size(axis)
    return lax.ppermute(x, axis, [(i, i ^ bit) for i in range(size)])


def gather_xor(x, axis):
    x = x[None]
    bit = 1
    while bit < lax.axis_size(axis):
        x = jnp.concatenate([x, swap(x, axis, bit)], axis=0)
        bit *= 2
    return x


def twice_gelu(v):
    return v + v * jnp.tanh(v * (ROOT + (ROOT * CUBE) * (v * v)))


def regroup_kernel(bases_ref, out_ref):
    lines, width = bases_ref.shape
    per = width // POOL
    rows = lines * per
    line = lax.broadcasted_iota(jnp.int32, (lines, rows), 0)
    column = lax.broadcasted_iota(jnp.int32, (lines, rows), 1)
    spread = lax.dot_general(
        bases_ref[...].astype(jnp.float32).astype(jnp.bfloat16),
        (column // per == line).astype(jnp.float32).astype(jnp.bfloat16),
        (((0,), (0,)), ((), ())),
        preferred_element_type=jnp.float32,
    )
    place = lax.broadcasted_iota(jnp.int32, (width, rows), 0) // POOL
    column = lax.broadcasted_iota(jnp.int32, (width, rows), 1)
    spread = jnp.where(place == column % per, spread, 0.0)
    grouped = spread[:POOL]
    for i in range(1, per):
        grouped = grouped + spread[i * POOL : (i + 1) * POOL]
    out_ref[...] = jnp.concatenate(
        [grouped[:, : rows // 2], grouped[:, rows // 2 :]], axis=0
    ).astype(jnp.bfloat16)


def regroup(bases):
    rows = bases.shape[1] // POOL
    return pl.pallas_call(
        regroup_kernel,
        out_shape=jax.ShapeDtypeStruct((2 * POOL, rows // 2), jnp.bfloat16),
        compiler_params=params(4),
        name="regroup",
    )(bases.reshape(bases.shape[1] // 128, 128))


def prepare_kernel(n, co, t0_ref, w_ref, wq_ref, wk_ref, table_ref, weights_ref, proj_ref):
    for chunk in range(C0 // CHUNK):
        part = t0_ref[chunk * CHUNK : (chunk + 1) * CHUNK, :]
        for pos in range(POOL):
            shifted = part if pos == 0 else pltpu.roll(part, pos, 1)
            first = (chunk * POOL + pos) * CHUNK
            table_ref[first : first + CHUNK, :] = shifted.astype(jnp.bfloat16)
    for tap in range(K1):
        weights_ref[tap * co : (tap + 1) * co, :] = w_ref[:, tap * C0 : (tap + 1) * C0] * 0.5
    for slot in range(n):
        rows = slice(slot * co, (slot + 1) * co)
        proj_ref[slot * SLOT : slot * SLOT + co, :PC] = wq_ref[rows, :]
        proj_ref[slot * SLOT : slot * SLOT + co, PC:] = wk_ref[rows, :]
        proj_ref[slot * SLOT + co : (slot + 1) * SLOT, :] = jnp.zeros(
            (SLOT - co, 2 * PC), jnp.bfloat16
        )


def prepare(n, first_table, conv_weight, query_weight, key_weight):
    co = conv_weight.shape[0]
    return pl.pallas_call(
        functools.partial(prepare_kernel, n, co),
        out_shape=[
            jax.ShapeDtypeStruct((POOL * C0, 128), jnp.bfloat16),
            jax.ShapeDtypeStruct((K1 * co, C0), jnp.bfloat16),
            jax.ShapeDtypeStruct((n * SLOT, 2 * PC), jnp.bfloat16),
        ],
        compiler_params=params(8),
        cost_estimate=pl.CostEstimate(flops=0, bytes_accessed=5 * MIB, transcendentals=0),
        name="prepare",
    )(first_table, conv_weight, query_weight, key_weight)


def stem_kernel(
    n, rows_dev, co, pay_ref, table, weights, grad_ref, p_ref, slope_ref, emb_ref,
    bases, ybuf, sums
):
    rows = n * rows_dev
    blocks = rows // BLOCK
    front = LAG * BLOCK + PAD

    def convolve(block):
        first = pl.multiple_of((block + LAG) * BLOCK, 128)
        conv = None
        for tap in range(K1):
            near = ybuf[tap * co : (tap + 1) * co, pl.ds(first, BLOCK + 2 * PAD)]
            begin = PAD + tap - K1 // 2
            part = near[:, begin : begin + BLOCK]
            conv = part if conv is None else conv + part
        square = conv * conv
        tangent = jnp.tanh(conv * (ROOT + (ROOT * CUBE) * square))
        half = 0.5 * conv
        gelu = half + half * tangent
        to = pl.multiple_of(jnp.maximum(block, 0) * BLOCK, 128)
        slope_ref[:, pl.ds(to, BLOCK)] = (0.5 + 0.5 * tangent) + half * (1.0 - tangent * tangent) * (
            ROOT + (3.0 * ROOT * CUBE) * square
        )
        lane = lax.broadcasted_iota(jnp.int32, (co, 128), 1)
        total = sums[:co, :]
        for part in range(BLOCK // BIN_ROWS):
            mean = jnp.sum(
                gelu[:, part * BIN_ROWS : (part + 1) * BIN_ROWS], axis=1, keepdims=True
            ) * (1.0 / BIN_ROWS)
            total = jnp.where(lane == block * (BLOCK // BIN_ROWS) + part, mean, total)
        sums[:co, :] = total

    def taps(block):
        ybuf[:, pl.ds(pl.multiple_of(front + block * BLOCK, 128), BLOCK)] = jnp.dot(
            weights[...],
            p_ref[:, pl.ds(pl.multiple_of(jnp.maximum(block, 0) * BLOCK, 128), BLOCK)],
            preferred_element_type=jnp.float32,
        )

    me = lax.axis_index("seq")
    bases[:, :PAD] = jnp.full((POOL, PAD), -1.0, jnp.float32)
    bases[:, PAD + rows :] = jnp.full((POOL, PAD), -1.0, jnp.float32)
    half = rows_dev // 2
    for slab in range(n):
        block = pay_ref[jnp.bitwise_xor(me, slab)].astype(jnp.float32)
        first = PAD + slab * rows_dev
        bases[:, first : first + half] = block[:POOL]
        bases[:, first + half : first + 2 * half] = block[POOL:]
    ybuf[:, front + rows :] = jnp.zeros((K1 * co, PAD), jnp.float32)
    p_ref[:, :BLOCK] = jnp.zeros((C0, BLOCK), jnp.bfloat16)
    sums[...] = jnp.zeros(sums.shape, jnp.float32)

    def main(step, carry):
        first = pl.multiple_of(step * BLOCK, 128)
        near = bases[:, pl.ds(first, BLOCK + 2 * PAD)]
        window = jnp.concatenate(
            [near[:, PAD + q : PAD + q + BLOCK] for q in (-1, 0, 1)], axis=0
        )
        onehot = jnp.concatenate(
            [(window == b).astype(jnp.float32) for b in range(4)]
            + [jnp.zeros((128 - 4 * WINDOW, BLOCK), jnp.float32)],
            axis=0,
        ).astype(jnp.bfloat16)
        convolve(step - LAG)
        taps(step - 1)
        for at in range(0, BLOCK, 256):
            for chunk in range(C0 // CHUNK):
                stem = jnp.dot(
                    table[chunk * POOL * CHUNK : (chunk + 1) * POOL * CHUNK, :],
                    onehot[:, at : at + 256],
                    preferred_element_type=jnp.float32,
                )
                most = least = stem[:CHUNK]
                for pos in range(1, POOL):
                    part = stem[pos * CHUNK : (pos + 1) * CHUNK]
                    most = jnp.maximum(most, part)
                    least = jnp.minimum(least, part)
                p_ref[
                    chunk * CHUNK : (chunk + 1) * CHUNK, pl.ds(pl.multiple_of(first + at, 128), 256)
                ] = jnp.maximum(twice_gelu(most), twice_gelu(least)).astype(jnp.bfloat16)
        return carry

    lax.fori_loop(0, blocks, main, 0)
    taps(blocks - 1)
    for last in range(LAG):
        convolve(blocks - LAG + last)

    own_pos, npos = grad_ref.shape
    embed = sums[...].T[:npos, :].astype(jnp.bfloat16).astype(jnp.float32)
    rest = grad_ref[...]
    parts = []
    for _ in range(3):
        part = rest.astype(jnp.bfloat16).astype(jnp.float32)
        parts.append(part)
        rest = rest - part
    grads = jnp.concatenate(
        parts + [jnp.zeros((npos - 3 * own_pos, npos), jnp.float32)], axis=0
    )
    emb_ref[...] = jnp.concatenate(
        [embed[:, :co], grads, jnp.zeros((npos, SLOT - co - npos), jnp.float32)], axis=1
    ).astype(jnp.bfloat16)


def stem_and_conv(n, payload, table, weights, pair_grad):
    co = weights.shape[0] // K1
    rows_dev = payload.shape[2] * 2
    rows = n * rows_dev
    npos = rows // BIN_ROWS
    return pl.pallas_call(
        functools.partial(stem_kernel, n, rows_dev, co),
        out_shape=[
            jax.ShapeDtypeStruct((C0, rows), jnp.bfloat16),
            jax.ShapeDtypeStruct((co, rows), jnp.float32),
            jax.ShapeDtypeStruct((npos, SLOT), jnp.bfloat16),
        ],
        scratch_shapes=[
            pltpu.VMEM((POOL, rows + 2 * PAD), jnp.float32),
            pltpu.VMEM((K1 * co, LAG * BLOCK + rows + 2 * PAD), jnp.float32),
            pltpu.VMEM((128, 128), jnp.float32),
        ],
        compiler_params=params(36),
        name="stem_and_conv",
    )(payload, table, weights, pair_grad)


COLS = C0 // 2
PARTS = ((0, K1 * COLS), (K1 * COLS, K1 * COLS + PC))
WIDE = K1 * COLS + PC
CODED = WIDE + 128


def encode(values, out_ref):
    exponents = []
    for (begin, end), x in zip(PARTS, values):
        top = jnp.maximum(jnp.max(jnp.abs(x), axis=1, keepdims=True), 1e-30)
        exponent = jnp.floor(jnp.log2(32000.0 / top))
        scaled = jnp.floor(x * jnp.exp2(exponent) + 0.5)
        out_ref[:, begin:end] = scaled.astype(jnp.int32).astype(jnp.int16)
        exponents.append(exponent)
    lane = lax.broadcasted_iota(jnp.int32, (out_ref.shape[0], 128), 1)
    packed = jnp.where(lane == 0, exponents[0], exponents[1])
    out_ref[:, WIDE:] = packed.astype(jnp.int32).astype(jnp.int16)


def decode(ref):
    exponents = ref[:, WIDE:].astype(jnp.int32).astype(jnp.float32)
    return [
        ref[:, begin:end].astype(jnp.int32).astype(jnp.float32) * jnp.exp2(-exponents[:, at : at + 1])
        for at, (begin, end) in enumerate(PARTS)
    ]


def build_shifted(half, dconv, shifted):
    held = dconv.shape[1]
    rows = shifted.shape[1]
    shifted[K1 * held :, :] = jnp.zeros((shifted.shape[0] - K1 * held, rows), jnp.bfloat16)
    for first in range(0, rows, BLOCK):
        near = dconv[half, :, first : first + BLOCK + 2 * PAD]
        for tap in range(K1):
            begin = PAD - tap + K1 // 2
            shifted[tap * held : (tap + 1) * held, first : first + BLOCK] = near[
                :, begin : begin + BLOCK
            ]


def gradient(half, part, shifted, qk_ref, pooled_ref, out_ref):
    size = out_ref.shape[0]
    held = -(-size // 16) * 16
    product = lax.dot_general(
        pooled_ref[part * COLS : (part + 1) * COLS, :], shifted[...],
        (((1,), (1,)), ((), ())), preferred_element_type=jnp.float32,
    ).T
    conv = jnp.concatenate(
        [product[tap * held : tap * held + size, :] for tap in range(K1)], axis=1
    )
    proj = qk_ref[half][:, part * PC : (part + 1) * PC]
    if out_ref.dtype == jnp.int16:
        encode((conv, proj), out_ref)
    else:
        out_ref[:, : K1 * COLS] = conv
        out_ref[:, K1 * COLS :] = proj


def first_kernel(
    n, emb_ref, proj_ref, slope_ref, pooled_ref, send_ref, give_ref, stay_ref, qk_ref, dconv_ref
):
    co, rows = slope_ref.shape
    size, held = co // 2, dconv_ref.shape[1]
    npos = rows // BIN_ROWS
    own_pos = npos // n
    scale = PC**-0.5
    me = lax.axis_index("seq")
    both = jnp.dot(
        jnp.concatenate([emb_ref[jnp.bitwise_xor(me, slab)] for slab in range(n)], axis=1),
        proj_ref[...],
        preferred_element_type=jnp.float32,
    )
    query, keys = both[:, :PC], both[:, PC:]
    pieces = []
    for slab in range(n):
        block = emb_ref[jnp.bitwise_xor(me, slab)].astype(jnp.float32)
        total = block[:own_pos]
        for part in range(1, 3):
            total = total + block[part * own_pos : (part + 1) * own_pos]
        pieces.append(total)
    grad = jnp.concatenate(pieces, axis=0)[:, co : co + npos]
    dquery = jnp.dot(grad, keys, precision=HIGH, preferred_element_type=jnp.float32) * scale
    dkeys = (
        lax.dot_general(
            grad, query, (((0,), (0,)), ((), ())), precision=HIGH,
            preferred_element_type=jnp.float32,
        )
        * scale
    )
    cotangent = jnp.concatenate([dquery, dkeys], axis=1)
    own = pl.ds(pl.multiple_of(me * SLOT, SLOT), SLOT)
    dembed = lax.dot_general(
        proj_ref[own, :].astype(jnp.float32), cotangent,
        (((1,), (1,)), ((), ())), precision=HIGH, preferred_element_type=jnp.float32,
    ) * (0.5 / BIN_ROWS)
    qk = lax.dot_general(
        emb_ref[0].astype(jnp.float32), cotangent, (((0,), (0,)), ((), ())),
        precision=HIGH, preferred_element_type=jnp.float32,
    )
    edge = jnp.zeros((held, PAD), jnp.bfloat16)
    for half in range(2):
        channels = slice(half * size, (half + 1) * size)
        qk_ref[half] = qk[channels]
        dconv_ref[half, :, :PAD] = edge
        dconv_ref[half, :, PAD + rows :] = edge
        for pos in range(npos):
            part = slope_ref[channels, pos * BIN_ROWS : (pos + 1) * BIN_ROWS] * dembed[
                channels, pos : pos + 1
            ]
            if held > size:
                part = jnp.concatenate(
                    [part, jnp.zeros((held - size, BIN_ROWS), jnp.float32)], axis=0
                )
            dconv_ref[half, :, PAD + pos * BIN_ROWS : PAD + (pos + 1) * BIN_ROWS] = part.astype(
                jnp.bfloat16
            )
    core = lax.axis_index("dp") % 2
    build_shifted(1 - core, dconv_ref, give_ref)
    gradient(1 - core, 0, give_ref, qk_ref, pooled_ref, send_ref)
    build_shifted(core, dconv_ref, stay_ref)


def middle_kernel(give_ref, stay_ref, qk_ref, pooled_ref, keep_ref, send_ref):
    core = lax.axis_index("dp") % 2
    gradient(core, 0, stay_ref, qk_ref, pooled_ref, keep_ref)
    gradient(1 - core, 1, give_ref, qk_ref, pooled_ref, send_ref)


def last_kernel(stay_ref, qk_ref, pooled_ref, after_ref, keep_ref):
    gradient(lax.axis_index("dp") % 2, 1, stay_ref, qk_ref, pooled_ref, keep_ref)


def first_part(n, embed, proj, slope, pooled):
    co, rows = slope.shape
    size = co // 2
    held = -(-size // 16) * 16
    return pl.pallas_call(
        functools.partial(first_kernel, n),
        out_shape=[
            jax.ShapeDtypeStruct((size, CODED), jnp.int16),
            jax.ShapeDtypeStruct((256, rows), jnp.bfloat16),
            jax.ShapeDtypeStruct((256, rows), jnp.bfloat16),
            jax.ShapeDtypeStruct((2, size, 2 * PC), jnp.float32),
        ],
        scratch_shapes=[pltpu.VMEM((2, held, rows + 2 * PAD), jnp.bfloat16)],
        compiler_params=params(28),
        name="first_part",
    )(embed, proj, slope, pooled)


def gradient_cost(size, rows, count):
    return pl.CostEstimate(
        flops=2 * 256 * COLS * rows * count, bytes_accessed=6 * MIB * count, transcendentals=0
    )


def middle_part(give, stay, qk, pooled):
    size, rows = qk.shape[1], pooled.shape[1]
    return pl.pallas_call(
        middle_kernel,
        out_shape=[
            jax.ShapeDtypeStruct((size, WIDE), jnp.float32),
            jax.ShapeDtypeStruct((size, CODED), jnp.int16),
        ],
        compiler_params=params(28),
        cost_estimate=gradient_cost(size, rows, 2),
        name="middle_part",
    )(give, stay, qk, pooled)


def last_part(stay, qk, pooled, after):
    size, rows = qk.shape[1], pooled.shape[1]
    return pl.pallas_call(
        last_kernel,
        out_shape=jax.ShapeDtypeStruct((size, WIDE), jnp.float32),
        compiler_params=params(28),
        in_specs=[pl.BlockSpec(memory_space=pltpu.VMEM)] * 3 + [pl.BlockSpec(memory_space=pl.ANY)],
        cost_estimate=gradient_cost(size, rows, 1),
        name="last_part",
    )(stay, qk, pooled, after)


def add_kernel(a_ref, b_ref, after_ref, out_ref):
    if a_ref.dtype == jnp.int16:
        a = decode(a_ref)
    else:
        a = [a_ref[:, begin:end] for begin, end in PARTS]
    encode([x + y for x, y in zip(a, decode(b_ref))], out_ref)


def add_half(a, b, after=None):
    return pl.pallas_call(
        add_kernel,
        out_shape=jax.ShapeDtypeStruct(b.shape, jnp.int16),
        in_specs=[pl.BlockSpec(memory_space=pltpu.VMEM)] * 2 + [pl.BlockSpec(memory_space=pl.ANY)],
        compiler_params=params(8),
        name="add_half",
    )(a, b, a if after is None else after)


def join_kernel(*refs):
    conv_ref, query_ref, key_ref = refs[4:]
    size = refs[0].shape[0]
    core = lax.axis_index("dp") % 2
    for part, out_ref in ((0, query_ref), (1, key_ref)):
        for half, ref in ((core, refs[2 * part]), (1 - core, refs[2 * part + 1])):
            rows = pl.ds(pl.multiple_of(half * size, 8), size)
            conv, proj = decode(ref)
            for tap in range(K1):
                first = tap * C0 + part * COLS
                conv_ref[rows, first : first + COLS] = conv[:, tap * COLS : (tap + 1) * COLS]
            out_ref[rows, :] = proj


def join(*halves):
    co = 2 * halves[0].shape[0]
    return pl.pallas_call(
        join_kernel,
        out_shape=[
            jax.ShapeDtypeStruct((co, K1 * C0), jnp.float32),
            jax.ShapeDtypeStruct((co, PC), jnp.float32),
            jax.ShapeDtypeStruct((co, PC), jnp.float32),
        ],
        compiler_params=params(8),
        name="join",
    )(*halves)


def body(bases, stem_table, conv_weight, query_weight, key_weight, pair_grad):
    n = lax.axis_size("seq")
    payload = gather_xor(regroup(bases), "seq")

    first_table = jnp.pad(
        stem_table.transpose(2, 1, 0), ((0, 0), (0, 0), (1, WINDOW - 1 - K0))
    ).reshape(C0, 4 * WINDOW)
    first_table = jnp.pad(first_table, ((0, 0), (0, 128 - 4 * WINDOW))).astype(jnp.float32)
    table, weights, proj = prepare(n, first_table, conv_weight, query_weight, key_weight)

    pooled, slope, embed = stem_and_conv(n, payload, table, weights, pair_grad[0])
    embed_all = gather_xor(embed, "seq")
    send_a, give, stay, qk = first_part(n, embed_all, proj, slope, pooled)
    keep_a, send_b = middle_part(give, stay, qk, pooled)
    mine_a = add_half(keep_a, swap(send_a, "dp", 1))
    mine_b = add_half(last_part(stay, qk, pooled, mine_a), swap(send_b, "dp", 1))
    bit = 2
    while bit < lax.axis_size("dp"):
        other_b = swap(mine_b, "dp", bit)
        mine_a = add_half(mine_a, swap(mine_a, "dp", bit))
        mine_b = add_half(mine_b, other_b, mine_a)
        bit *= 2
    return tuple(join(mine_a, swap(mine_a, "dp", 1), mine_b, swap(mine_b, "dp", 1)))


def solution(mesh):
    return jax.shard_map(
        body,
        mesh=mesh,
        in_specs=(P("dp", "seq"), P(), P("seq", None), P(), P(), P("dp", "seq", None)),
        out_specs=(P("seq", None), P("seq", None), P("seq", None)),
        check_vma=False,
    )
```

```python
import functools

import jax
import jax.numpy as jnp
from jax import lax
from jax.experimental import pallas as pl
from jax.experimental.pallas import tpu as pltpu
from jax.sharding import PartitionSpec as P

C0 = 768
C1 = 768
PC = 128
K0 = 15
K1 = 5
POOL = 8
BIN_ROWS = 256
WINDOW = 24
CHUNK = 16
BLOCK = 256
SHIFT_BLOCK = 512
LAG = 3
PAD = 128
SLOT = 128

ROOT = 0.7978845608028654
CUBE = 0.044715
HIGH = lax.Precision.HIGHEST
MIB = 1024 * 1024


def params(mib):
    return pltpu.CompilerParams(vmem_limit_bytes=mib * MIB)


def swap(x, axis, bit):
    size = lax.axis_size(axis)
    return lax.ppermute(x, axis, [(i, i ^ bit) for i in range(size)])


def gather_xor(x, axis):
    x = x[None]
    bit = 1
    while bit < lax.axis_size(axis):
        x = jnp.concatenate([x, swap(x, axis, bit)], axis=0)
        bit *= 2
    return x


def twice_gelu(v):
    return v + v * jnp.tanh(v * (ROOT + (ROOT * CUBE) * (v * v)))


def regroup_kernel(bases_ref, out_ref):
    lines, width = bases_ref.shape
    per = width // POOL
    rows = lines * per
    line = lax.broadcasted_iota(jnp.int32, (lines, rows), 0)
    column = lax.broadcasted_iota(jnp.int32, (lines, rows), 1)
    spread = lax.dot_general(
        bases_ref[...].astype(jnp.float32).astype(jnp.bfloat16),
        (column // per == line).astype(jnp.float32).astype(jnp.bfloat16),
        (((0,), (0,)), ((), ())),
        preferred_element_type=jnp.float32,
    )
    place = lax.broadcasted_iota(jnp.int32, (width, rows), 0) // POOL
    column = lax.broadcasted_iota(jnp.int32, (width, rows), 1)
    spread = jnp.where(place == column % per, spread, 0.0)
    grouped = spread[:POOL]
    for i in range(1, per):
        grouped = grouped + spread[i * POOL : (i + 1) * POOL]
    out_ref[...] = jnp.concatenate(
        [grouped[:, : rows // 2], grouped[:, rows // 2 :]], axis=0
    ).astype(jnp.bfloat16)


def regroup(bases):
    rows = bases.shape[1] // POOL
    return pl.pallas_call(
        regroup_kernel,
        out_shape=jax.ShapeDtypeStruct((2 * POOL, rows // 2), jnp.bfloat16),
        compiler_params=params(4),
        name="regroup",
    )(bases.reshape(bases.shape[1] // 128, 128))


def prepare_kernel(n, co, t0_ref, w_ref, wq_ref, wk_ref, table_ref, weights_ref, proj_ref):
    for chunk in range(C0 // CHUNK):
        part = t0_ref[chunk * CHUNK : (chunk + 1) * CHUNK, :]
        for pos in range(POOL):
            shifted = part if pos == 0 else pltpu.roll(part, pos, 1)
            first = (chunk * POOL + pos) * CHUNK
            table_ref[first : first + CHUNK, :] = shifted.astype(jnp.bfloat16)
    for tap in range(K1):
        weights_ref[tap * co : (tap + 1) * co, :] = w_ref[:, tap * C0 : (tap + 1) * C0] * 0.5
    for slot in range(n):
        rows = slice(slot * co, (slot + 1) * co)
        proj_ref[slot * SLOT : slot * SLOT + co, :PC] = wq_ref[rows, :]
        proj_ref[slot * SLOT : slot * SLOT + co, PC:] = wk_ref[rows, :]
        proj_ref[slot * SLOT + co : (slot + 1) * SLOT, :] = jnp.zeros(
            (SLOT - co, 2 * PC), jnp.bfloat16
        )


def prepare(n, first_table, conv_weight, query_weight, key_weight):
    co = conv_weight.shape[0]
    return pl.pallas_call(
        functools.partial(prepare_kernel, n, co),
        out_shape=[
            jax.ShapeDtypeStruct((POOL * C0, 128), jnp.bfloat16),
            jax.ShapeDtypeStruct((K1 * co, C0), jnp.bfloat16),
            jax.ShapeDtypeStruct((n * SLOT, 2 * PC), jnp.bfloat16),
        ],
        compiler_params=params(8),
        cost_estimate=pl.CostEstimate(flops=0, bytes_accessed=5 * MIB, transcendentals=0),
        name="prepare",
    )(first_table, conv_weight, query_weight, key_weight)


def stem_kernel(
    n, rows_dev, co, pay_ref, table, weights, grad_ref, p_ref, slope_ref, emb_ref,
    bases, ybuf, sums
):
    rows = n * rows_dev
    blocks = rows // BLOCK
    front = LAG * BLOCK + PAD

    def convolve(block):
        first = pl.multiple_of((block + LAG) * BLOCK, 128)
        conv = None
        for tap in range(K1):
            near = ybuf[tap * co : (tap + 1) * co, pl.ds(first, BLOCK + 2 * PAD)]
            begin = PAD + tap - K1 // 2
            part = near[:, begin : begin + BLOCK]
            conv = part if conv is None else conv + part
        square = conv * conv
        tangent = jnp.tanh(conv * (ROOT + (ROOT * CUBE) * square))
        half = 0.5 * conv
        gelu = half + half * tangent
        to = pl.multiple_of(jnp.maximum(block, 0) * BLOCK, 128)
        slope_ref[:, pl.ds(to, BLOCK)] = (0.5 + 0.5 * tangent) + half * (1.0 - tangent * tangent) * (
            ROOT + (3.0 * ROOT * CUBE) * square
        )
        lane = lax.broadcasted_iota(jnp.int32, (co, 128), 1)
        total = sums[:co, :]
        for part in range(BLOCK // BIN_ROWS):
            mean = jnp.sum(
                gelu[:, part * BIN_ROWS : (part + 1) * BIN_ROWS], axis=1, keepdims=True
            ) * (1.0 / BIN_ROWS)
            total = jnp.where(lane == block * (BLOCK // BIN_ROWS) + part, mean, total)
        sums[:co, :] = total

    def taps(block):
        ybuf[:, pl.ds(pl.multiple_of(front + block * BLOCK, 128), BLOCK)] = jnp.dot(
            weights[...],
            p_ref[:, pl.ds(pl.multiple_of(jnp.maximum(block, 0) * BLOCK, 128), BLOCK)],
            preferred_element_type=jnp.float32,
        )

    me = lax.axis_index("seq")
    bases[:, :PAD] = jnp.full((POOL, PAD), -1.0, jnp.float32)
    bases[:, PAD + rows :] = jnp.full((POOL, PAD), -1.0, jnp.float32)
    half = rows_dev // 2
    for slab in range(n):
        block = pay_ref[jnp.bitwise_xor(me, slab)].astype(jnp.float32)
        first = PAD + slab * rows_dev
        bases[:, first : first + half] = block[:POOL]
        bases[:, first + half : first + 2 * half] = block[POOL:]
    ybuf[:, front + rows :] = jnp.zeros((K1 * co, PAD), jnp.float32)
    p_ref[:, :BLOCK] = jnp.zeros((C0, BLOCK), jnp.bfloat16)
    sums[...] = jnp.zeros(sums.shape, jnp.float32)

    def main(step, carry):
        first = pl.multiple_of(step * BLOCK, 128)
        near = bases[:, pl.ds(first, BLOCK + 2 * PAD)]
        window = jnp.concatenate(
            [near[:, PAD + q : PAD + q + BLOCK] for q in (-1, 0, 1)], axis=0
        )
        onehot = jnp.concatenate(
            [(window == b).astype(jnp.float32) for b in range(4)]
            + [jnp.zeros((128 - 4 * WINDOW, BLOCK), jnp.float32)],
            axis=0,
        ).astype(jnp.bfloat16)
        convolve(step - LAG)
        taps(step - 1)
        for at in range(0, BLOCK, 256):
            for chunk in range(C0 // CHUNK):
                stem = jnp.dot(
                    table[chunk * POOL * CHUNK : (chunk + 1) * POOL * CHUNK, :],
                    onehot[:, at : at + 256],
                    preferred_element_type=jnp.float32,
                )
                most = least = stem[:CHUNK]
                for pos in range(1, POOL):
                    part = stem[pos * CHUNK : (pos + 1) * CHUNK]
                    most = jnp.maximum(most, part)
                    least = jnp.minimum(least, part)
                p_ref[
                    chunk * CHUNK : (chunk + 1) * CHUNK, pl.ds(pl.multiple_of(first + at, 128), 256)
                ] = jnp.maximum(twice_gelu(most), twice_gelu(least)).astype(jnp.bfloat16)
        return carry

    lax.fori_loop(0, blocks, main, 0)
    taps(blocks - 1)
    for last in range(LAG):
        convolve(blocks - LAG + last)

    own_pos, npos = grad_ref.shape
    embed = sums[...].T[:npos, :].astype(jnp.bfloat16).astype(jnp.float32)
    rest = grad_ref[...]
    parts = []
    for _ in range(3):
        part = rest.astype(jnp.bfloat16).astype(jnp.float32)
        parts.append(part)
        rest = rest - part
    grads = jnp.concatenate(
        parts + [jnp.zeros((npos - 3 * own_pos, npos), jnp.float32)], axis=0
    )
    emb_ref[...] = jnp.concatenate(
        [embed[:, :co], grads, jnp.zeros((npos, SLOT - co - npos), jnp.float32)], axis=1
    ).astype(jnp.bfloat16)


def stem_and_conv(n, payload, table, weights, pair_grad):
    co = weights.shape[0] // K1
    rows_dev = payload.shape[2] * 2
    rows = n * rows_dev
    npos = rows // BIN_ROWS
    return pl.pallas_call(
        functools.partial(stem_kernel, n, rows_dev, co),
        out_shape=[
            jax.ShapeDtypeStruct((C0, rows), jnp.bfloat16),
            jax.ShapeDtypeStruct((co, rows), jnp.float32),
            jax.ShapeDtypeStruct((npos, SLOT), jnp.bfloat16),
        ],
        scratch_shapes=[
            pltpu.VMEM((POOL, rows + 2 * PAD), jnp.float32),
            pltpu.VMEM((K1 * co, LAG * BLOCK + rows + 2 * PAD), jnp.float32),
            pltpu.VMEM((128, 128), jnp.float32),
        ],
        compiler_params=params(36),
        name="stem_and_conv",
    )(payload, table, weights, pair_grad)


COLS = C0 // 2
PARTS = ((0, K1 * COLS), (K1 * COLS, K1 * COLS + PC))
WIDE = K1 * COLS + PC
CODED = WIDE + 128


def encode(values, out_ref):
    exponents = []
    for (begin, end), x in zip(PARTS, values):
        top = jnp.maximum(jnp.max(jnp.abs(x), axis=1, keepdims=True), 1e-30)
        exponent = jnp.floor(jnp.log2(32000.0 / top))
        scaled = jnp.floor(x * jnp.exp2(exponent) + 0.5)
        out_ref[:, begin:end] = scaled.astype(jnp.int32).astype(jnp.int16)
        exponents.append(exponent)
    lane = lax.broadcasted_iota(jnp.int32, (out_ref.shape[0], 128), 1)
    packed = jnp.where(lane == 0, exponents[0], exponents[1])
    out_ref[:, WIDE:] = packed.astype(jnp.int32).astype(jnp.int16)


def decode(ref):
    exponents = ref[:, WIDE:].astype(jnp.int32).astype(jnp.float32)
    return [
        ref[:, begin:end].astype(jnp.int32).astype(jnp.float32) * jnp.exp2(-exponents[:, at : at + 1])
        for at, (begin, end) in enumerate(PARTS)
    ]


def build_shifted(half, dconv, shifted):
    held = dconv.shape[1]
    rows = shifted.shape[1]
    shifted[K1 * held :, :] = jnp.zeros((shifted.shape[0] - K1 * held, rows), jnp.bfloat16)
    for first in range(0, rows, SHIFT_BLOCK):
        near = dconv[half, :, first : first + SHIFT_BLOCK + 2 * PAD]
        for tap in range(K1):
            begin = PAD - tap + K1 // 2
            shifted[tap * held : (tap + 1) * held, first : first + SHIFT_BLOCK] = near[
                :, begin : begin + SHIFT_BLOCK
            ]


def gradient(half, part, shifted, qk_ref, pooled_ref, out_ref):
    size = out_ref.shape[0]
    held = -(-size // 16) * 16
    product = lax.dot_general(
        pooled_ref[part * COLS : (part + 1) * COLS, :], shifted[...],
        (((1,), (1,)), ((), ())), preferred_element_type=jnp.float32,
    ).T
    conv = jnp.concatenate(
        [product[tap * held : tap * held + size, :] for tap in range(K1)], axis=1
    )
    proj = qk_ref[half][:, part * PC : (part + 1) * PC]
    if out_ref.dtype == jnp.int16:
        encode((conv, proj), out_ref)
    else:
        out_ref[:, : K1 * COLS] = conv
        out_ref[:, K1 * COLS :] = proj


def first_kernel(
    n, emb_ref, proj_ref, slope_ref, pooled_ref, send_ref, give_ref, stay_ref, qk_ref, dconv_ref
):
    co, rows = slope_ref.shape
    size, held = co // 2, dconv_ref.shape[1]
    npos = rows // BIN_ROWS
    own_pos = npos // n
    scale = PC**-0.5
    me = lax.axis_index("seq")
    both = jnp.dot(
        jnp.concatenate([emb_ref[jnp.bitwise_xor(me, slab)] for slab in range(n)], axis=1),
        proj_ref[...],
        preferred_element_type=jnp.float32,
    )
    query, keys = both[:, :PC], both[:, PC:]
    pieces = []
    for slab in range(n):
        block = emb_ref[jnp.bitwise_xor(me, slab)].astype(jnp.float32)
        total = block[:own_pos]
        for part in range(1, 3):
            total = total + block[part * own_pos : (part + 1) * own_pos]
        pieces.append(total)
    grad = jnp.concatenate(pieces, axis=0)[:, co : co + npos]
    dquery = jnp.dot(grad, keys, precision=HIGH, preferred_element_type=jnp.float32) * scale
    dkeys = (
        lax.dot_general(
            grad, query, (((0,), (0,)), ((), ())), precision=HIGH,
            preferred_element_type=jnp.float32,
        )
        * scale
    )
    cotangent = jnp.concatenate([dquery, dkeys], axis=1)
    own = pl.ds(pl.multiple_of(me * SLOT, SLOT), SLOT)
    dembed = lax.dot_general(
        proj_ref[own, :].astype(jnp.float32), cotangent,
        (((1,), (1,)), ((), ())), precision=HIGH, preferred_element_type=jnp.float32,
    ) * (0.5 / BIN_ROWS)
    qk = lax.dot_general(
        emb_ref[0].astype(jnp.float32), cotangent, (((0,), (0,)), ((), ())),
        precision=HIGH, preferred_element_type=jnp.float32,
    )
    edge = jnp.zeros((held, PAD), jnp.bfloat16)
    for half in range(2):
        channels = slice(half * size, (half + 1) * size)
        qk_ref[half] = qk[channels]
        dconv_ref[half, :, :PAD] = edge
        dconv_ref[half, :, PAD + rows :] = edge
        for pos in range(npos):
            part = slope_ref[channels, pos * BIN_ROWS : (pos + 1) * BIN_ROWS] * dembed[
                channels, pos : pos + 1
            ]
            if held > size:
                part = jnp.concatenate(
                    [part, jnp.zeros((held - size, BIN_ROWS), jnp.float32)], axis=0
                )
            dconv_ref[half, :, PAD + pos * BIN_ROWS : PAD + (pos + 1) * BIN_ROWS] = part.astype(
                jnp.bfloat16
            )
    core = lax.axis_index("dp") % 2
    build_shifted(1 - core, dconv_ref, give_ref)
    gradient(1 - core, 0, give_ref, qk_ref, pooled_ref, send_ref)
    build_shifted(core, dconv_ref, stay_ref)


def middle_kernel(give_ref, stay_ref, qk_ref, pooled_ref, keep_ref, send_ref):
    core = lax.axis_index("dp") % 2
    gradient(core, 0, stay_ref, qk_ref, pooled_ref, keep_ref)
    gradient(1 - core, 1, give_ref, qk_ref, pooled_ref, send_ref)


def last_kernel(stay_ref, qk_ref, pooled_ref, after_ref, keep_ref):
    gradient(lax.axis_index("dp") % 2, 1, stay_ref, qk_ref, pooled_ref, keep_ref)


def first_part(n, embed, proj, slope, pooled):
    co, rows = slope.shape
    size = co // 2
    held = -(-size // 16) * 16
    return pl.pallas_call(
        functools.partial(first_kernel, n),
        out_shape=[
            jax.ShapeDtypeStruct((size, CODED), jnp.int16),
            jax.ShapeDtypeStruct((256, rows), jnp.bfloat16),
            jax.ShapeDtypeStruct((256, rows), jnp.bfloat16),
            jax.ShapeDtypeStruct((2, size, 2 * PC), jnp.float32),
        ],
        scratch_shapes=[pltpu.VMEM((2, held, rows + 2 * PAD), jnp.bfloat16)],
        compiler_params=params(28),
        name="first_part",
    )(embed, proj, slope, pooled)


def gradient_cost(size, rows, count):
    return pl.CostEstimate(
        flops=2 * 256 * COLS * rows * count, bytes_accessed=6 * MIB * count, transcendentals=0
    )


def middle_part(give, stay, qk, pooled):
    size, rows = qk.shape[1], pooled.shape[1]
    return pl.pallas_call(
        middle_kernel,
        out_shape=[
            jax.ShapeDtypeStruct((size, WIDE), jnp.float32),
            jax.ShapeDtypeStruct((size, CODED), jnp.int16),
        ],
        compiler_params=params(28),
        cost_estimate=gradient_cost(size, rows, 2),
        name="middle_part",
    )(give, stay, qk, pooled)


def last_part(stay, qk, pooled, after):
    size, rows = qk.shape[1], pooled.shape[1]
    return pl.pallas_call(
        last_kernel,
        out_shape=jax.ShapeDtypeStruct((size, WIDE), jnp.float32),
        compiler_params=params(28),
        in_specs=[pl.BlockSpec(memory_space=pltpu.VMEM)] * 3 + [pl.BlockSpec(memory_space=pl.ANY)],
        cost_estimate=gradient_cost(size, rows, 1),
        name="last_part",
    )(stay, qk, pooled, after)


def add_kernel(a_ref, b_ref, after_ref, out_ref):
    if a_ref.dtype == jnp.int16:
        a = decode(a_ref)
    else:
        a = [a_ref[:, begin:end] for begin, end in PARTS]
    encode([x + y for x, y in zip(a, decode(b_ref))], out_ref)


def add_half(a, b, after=None):
    return pl.pallas_call(
        add_kernel,
        out_shape=jax.ShapeDtypeStruct(b.shape, jnp.int16),
        in_specs=[pl.BlockSpec(memory_space=pltpu.VMEM)] * 2 + [pl.BlockSpec(memory_space=pl.ANY)],
        compiler_params=params(8),
        name="add_half",
    )(a, b, a if after is None else after)


def join_kernel(*refs):
    conv_ref, query_ref, key_ref = refs[4:]
    size = refs[0].shape[0]
    core = lax.axis_index("dp") % 2
    for part, out_ref in ((0, query_ref), (1, key_ref)):
        for half, ref in ((core, refs[2 * part]), (1 - core, refs[2 * part + 1])):
            rows = pl.ds(pl.multiple_of(half * size, 8), size)
            conv, proj = decode(ref)
            for tap in range(K1):
                first = tap * C0 + part * COLS
                conv_ref[rows, first : first + COLS] = conv[:, tap * COLS : (tap + 1) * COLS]
            out_ref[rows, :] = proj


def join(*halves):
    co = 2 * halves[0].shape[0]
    return pl.pallas_call(
        join_kernel,
        out_shape=[
            jax.ShapeDtypeStruct((co, K1 * C0), jnp.float32),
            jax.ShapeDtypeStruct((co, PC), jnp.float32),
            jax.ShapeDtypeStruct((co, PC), jnp.float32),
        ],
        compiler_params=params(8),
        name="join",
    )(*halves)


def body(bases, stem_table, conv_weight, query_weight, key_weight, pair_grad):
    n = lax.axis_size("seq")
    payload = gather_xor(regroup(bases), "seq")

    first_table = jnp.pad(
        stem_table.transpose(2, 1, 0), ((0, 0), (0, 0), (1, WINDOW - 1 - K0))
    ).reshape(C0, 4 * WINDOW)
    first_table = jnp.pad(first_table, ((0, 0), (0, 128 - 4 * WINDOW))).astype(jnp.float32)
    table, weights, proj = prepare(n, first_table, conv_weight, query_weight, key_weight)

    pooled, slope, embed = stem_and_conv(n, payload, table, weights, pair_grad[0])
    embed_all = gather_xor(embed, "seq")
    send_a, give, stay, qk = first_part(n, embed_all, proj, slope, pooled)
    keep_a, send_b = middle_part(give, stay, qk, pooled)
    mine_a = add_half(keep_a, swap(send_a, "dp", 1))
    mine_b = add_half(last_part(stay, qk, pooled, mine_a), swap(send_b, "dp", 1))
    bit = 2
    while bit < lax.axis_size("dp"):
        other_b = swap(mine_b, "dp", bit)
        mine_a = add_half(mine_a, swap(mine_a, "dp", bit))
        mine_b = add_half(mine_b, other_b, mine_a)
        bit *= 2
    return tuple(join(mine_a, swap(mine_a, "dp", 1), mine_b, swap(mine_b, "dp", 1)))


def solution(mesh):
    return jax.shard_map(
        body,
        mesh=mesh,
        in_specs=(P("dp", "seq"), P(), P("seq", None), P(), P(), P("dp", "seq", None)),
        out_specs=(P("seq", None), P("seq", None), P("seq", None)),
        check_vma=False,
    )
```

```python
import functools

import jax
import jax.numpy as jnp
from jax import lax
from jax.experimental import pallas as pl
from jax.experimental.pallas import tpu as pltpu
from jax.sharding import PartitionSpec as P

C0 = 768
C1 = 768
PC = 128
K0 = 15
K1 = 5
POOL = 8
BIN_ROWS = 256
WINDOW = 24
CHUNK = 16
BLOCK = 512
SHIFT_BLOCK = 512
LAG = 3
PAD = 128
SLOT = 128

ROOT = 0.7978845608028654
CUBE = 0.044715
HIGH = lax.Precision.HIGHEST
MIB = 1024 * 1024


def params(mib):
    return pltpu.CompilerParams(vmem_limit_bytes=mib * MIB)


def swap(x, axis, bit):
    size = lax.axis_size(axis)
    return lax.ppermute(x, axis, [(i, i ^ bit) for i in range(size)])


def gather_xor(x, axis):
    x = x[None]
    bit = 1
    while bit < lax.axis_size(axis):
        x = jnp.concatenate([x, swap(x, axis, bit)], axis=0)
        bit *= 2
    return x


def twice_gelu(v):
    return v + v * jnp.tanh(v * (ROOT + (ROOT * CUBE) * (v * v)))


def regroup_kernel(bases_ref, out_ref):
    lines, width = bases_ref.shape
    per = width // POOL
    rows = lines * per
    line = lax.broadcasted_iota(jnp.int32, (lines, rows), 0)
    column = lax.broadcasted_iota(jnp.int32, (lines, rows), 1)
    spread = lax.dot_general(
        bases_ref[...].astype(jnp.float32).astype(jnp.bfloat16),
        (column // per == line).astype(jnp.float32).astype(jnp.bfloat16),
        (((0,), (0,)), ((), ())),
        preferred_element_type=jnp.float32,
    )
    place = lax.broadcasted_iota(jnp.int32, (width, rows), 0) // POOL
    column = lax.broadcasted_iota(jnp.int32, (width, rows), 1)
    spread = jnp.where(place == column % per, spread, 0.0)
    grouped = spread[:POOL]
    for i in range(1, per):
        grouped = grouped + spread[i * POOL : (i + 1) * POOL]
    out_ref[...] = jnp.concatenate(
        [grouped[:, : rows // 2], grouped[:, rows // 2 :]], axis=0
    ).astype(jnp.bfloat16)


def regroup(bases):
    rows = bases.shape[1] // POOL
    return pl.pallas_call(
        regroup_kernel,
        out_shape=jax.ShapeDtypeStruct((2 * POOL, rows // 2), jnp.bfloat16),
        compiler_params=params(4),
        name="regroup",
    )(bases.reshape(bases.shape[1] // 128, 128))


def prepare_kernel(n, co, t0_ref, w_ref, both_ref, table_ref, weights_ref, proj_ref):
    for chunk in range(C0 // CHUNK):
        part = t0_ref[chunk * CHUNK : (chunk + 1) * CHUNK, :]
        for pos in range(POOL):
            shifted = part if pos == 0 else pltpu.roll(part, pos, 1)
            first = (chunk * POOL + pos) * CHUNK
            table_ref[first : first + CHUNK, :] = shifted.astype(jnp.bfloat16)
    for tap in range(K1):
        weights_ref[tap * co : (tap + 1) * co, :] = w_ref[:, tap * C0 : (tap + 1) * C0]
    for slot in range(n):
        rows = slice(slot * co, (slot + 1) * co)
        proj_ref[slot * SLOT : slot * SLOT + co, :] = both_ref[rows, :]
        proj_ref[slot * SLOT + co : (slot + 1) * SLOT, :] = jnp.zeros(
            (SLOT - co, 2 * PC), jnp.bfloat16
        )


def prepare(n, first_table, conv_weight, both):
    co = conv_weight.shape[0]
    return pl.pallas_call(
        functools.partial(prepare_kernel, n, co),
        out_shape=[
            jax.ShapeDtypeStruct((POOL * C0, 128), jnp.bfloat16),
            jax.ShapeDtypeStruct((K1 * co, C0), jnp.bfloat16),
            jax.ShapeDtypeStruct((n * SLOT, 2 * PC), jnp.bfloat16),
        ],
        compiler_params=params(8),
        cost_estimate=pl.CostEstimate(flops=0, bytes_accessed=5 * MIB, transcendentals=0),
        name="prepare",
    )(first_table, conv_weight, both)


def stem_kernel(
    n, rows_dev, co, pay_ref, table, weights, grad_ref, p_ref, slope_ref, emb_ref,
    bases, ybuf, sums
):
    rows = n * rows_dev
    blocks = rows // BLOCK
    front = LAG * BLOCK + PAD

    def convolve(block):
        first = pl.multiple_of((block + LAG) * BLOCK, 128)
        conv = None
        for tap in range(K1):
            near = ybuf[tap * co : (tap + 1) * co, pl.ds(first, BLOCK + 2 * PAD)]
            begin = PAD + tap - K1 // 2
            part = near[:, begin : begin + BLOCK]
            conv = part if conv is None else conv + part
        square = conv * conv
        tangent = jnp.tanh(conv * (ROOT + (ROOT * CUBE) * square))
        half = 0.5 * conv
        gelu = half + half * tangent
        to = pl.multiple_of(jnp.maximum(block, 0) * BLOCK, 128)
        slope_ref[:, pl.ds(to, BLOCK)] = (0.5 + 0.5 * tangent) + half * (1.0 - tangent * tangent) * (
            ROOT + (3.0 * ROOT * CUBE) * square
        )
        lane = lax.broadcasted_iota(jnp.int32, (co, 128), 1)
        total = sums[:co, :]
        for part in range(BLOCK // BIN_ROWS):
            mean = jnp.sum(
                gelu[:, part * BIN_ROWS : (part + 1) * BIN_ROWS], axis=1, keepdims=True
            ) * (1.0 / BIN_ROWS)
            total = jnp.where(lane == block * (BLOCK // BIN_ROWS) + part, mean, total)
        sums[:co, :] = total

    def taps(block):
        ybuf[:, pl.ds(pl.multiple_of(front + block * BLOCK, 128), BLOCK)] = jnp.dot(
            weights[...],
            p_ref[:, pl.ds(pl.multiple_of(jnp.maximum(block, 0) * BLOCK, 128), BLOCK)],
            preferred_element_type=jnp.float32,
        )

    me = lax.axis_index("seq")
    bases[:, :PAD] = jnp.full((POOL, PAD), -1.0, jnp.float32)
    bases[:, PAD + rows :] = jnp.full((POOL, PAD), -1.0, jnp.float32)
    half = rows_dev // 2
    for slab in range(n):
        block = pay_ref[jnp.bitwise_xor(me, slab)].astype(jnp.float32)
        first = PAD + slab * rows_dev
        bases[:, first : first + half] = block[:POOL]
        bases[:, first + half : first + 2 * half] = block[POOL:]
    ybuf[:, front + rows :] = jnp.zeros((K1 * co, PAD), jnp.float32)
    p_ref[:, :BLOCK] = jnp.zeros((C0, BLOCK), jnp.bfloat16)
    sums[...] = jnp.zeros(sums.shape, jnp.float32)

    def main(step, carry):
        first = pl.multiple_of(step * BLOCK, 128)
        near = bases[:, pl.ds(first, BLOCK + 2 * PAD)]
        window = jnp.concatenate(
            [near[:, PAD + q : PAD + q + BLOCK] for q in (-1, 0, 1)], axis=0
        )
        onehot = jnp.concatenate(
            [(window == b).astype(jnp.float32) for b in range(4)]
            + [jnp.zeros((128 - 4 * WINDOW, BLOCK), jnp.float32)],
            axis=0,
        ).astype(jnp.bfloat16)
        convolve(step - LAG)
        taps(step - 1)
        for at in range(0, BLOCK, 256):
            for chunk in range(C0 // CHUNK):
                stem = jnp.dot(
                    table[chunk * POOL * CHUNK : (chunk + 1) * POOL * CHUNK, :],
                    onehot[:, at : at + 256],
                    preferred_element_type=jnp.float32,
                )
                most = least = stem[:CHUNK]
                for pos in range(1, POOL):
                    part = stem[pos * CHUNK : (pos + 1) * CHUNK]
                    most = jnp.maximum(most, part)
                    least = jnp.minimum(least, part)
                p_ref[
                    chunk * CHUNK : (chunk + 1) * CHUNK, pl.ds(pl.multiple_of(first + at, 128), 256)
                ] = jnp.maximum(twice_gelu(most), twice_gelu(least)).astype(jnp.bfloat16)
        return carry

    lax.fori_loop(0, blocks, main, 0)
    taps(blocks - 1)
    for last in range(LAG):
        convolve(blocks - LAG + last)

    own_pos, npos = grad_ref.shape
    embed = sums[...].T[:npos, :].astype(jnp.bfloat16).astype(jnp.float32)
    rest = grad_ref[...]
    parts = []
    for _ in range(3):
        part = rest.astype(jnp.bfloat16).astype(jnp.float32)
        parts.append(part)
        rest = rest - part
    grads = jnp.concatenate(
        parts + [jnp.zeros((npos - 3 * own_pos, npos), jnp.float32)], axis=0
    )
    emb_ref[...] = jnp.concatenate(
        [embed[:, :co], grads, jnp.zeros((npos, SLOT - co - npos), jnp.float32)], axis=1
    ).astype(jnp.bfloat16)


def stem_and_conv(n, payload, table, weights, pair_grad):
    co = weights.shape[0] // K1
    rows_dev = payload.shape[2] * 2
    rows = n * rows_dev
    npos = rows // BIN_ROWS
    return pl.pallas_call(
        functools.partial(stem_kernel, n, rows_dev, co),
        out_shape=[
            jax.ShapeDtypeStruct((C0, rows), jnp.bfloat16),
            jax.ShapeDtypeStruct((co, rows), jnp.float32),
            jax.ShapeDtypeStruct((npos, SLOT), jnp.bfloat16),
        ],
        scratch_shapes=[
            pltpu.VMEM((POOL, rows + 2 * PAD), jnp.float32),
            pltpu.VMEM((K1 * co, LAG * BLOCK + rows + 2 * PAD), jnp.float32),
            pltpu.VMEM((128, 128), jnp.float32),
        ],
        compiler_params=params(36),
        name="stem_and_conv",
    )(payload, table, weights, pair_grad)


COLS = C0 // 2
PARTS = ((0, K1 * COLS), (K1 * COLS, K1 * COLS + PC))
WIDE = K1 * COLS + PC
CODED = WIDE + 128


def encode(values, out_ref):
    exponents = []
    for (begin, end), x in zip(PARTS, values):
        top = jnp.maximum(jnp.max(jnp.abs(x), axis=1, keepdims=True), 1e-30)
        exponent = jnp.floor(jnp.log2(32000.0 / top))
        scaled = jnp.floor(x * jnp.exp2(exponent) + 0.5)
        out_ref[:, begin:end] = scaled.astype(jnp.int32).astype(jnp.int16)
        exponents.append(exponent)
    lane = lax.broadcasted_iota(jnp.int32, (out_ref.shape[0], 128), 1)
    packed = jnp.where(lane == 0, exponents[0], exponents[1])
    out_ref[:, WIDE:] = packed.astype(jnp.int32).astype(jnp.int16)


def decode(ref):
    exponents = ref[:, WIDE:].astype(jnp.int32).astype(jnp.float32)
    return [
        ref[:, begin:end].astype(jnp.int32).astype(jnp.float32) * jnp.exp2(-exponents[:, at : at + 1])
        for at, (begin, end) in enumerate(PARTS)
    ]


def build_shifted(half, dconv, shifted):
    held = dconv.shape[1]
    rows = shifted.shape[1]
    shifted[K1 * held :, :] = jnp.zeros((shifted.shape[0] - K1 * held, rows), jnp.bfloat16)
    for first in range(0, rows, SHIFT_BLOCK):
        near = dconv[half, :, first : first + SHIFT_BLOCK + 2 * PAD]
        for tap in range(K1):
            begin = PAD - tap + K1 // 2
            shifted[tap * held : (tap + 1) * held, first : first + SHIFT_BLOCK] = near[
                :, begin : begin + SHIFT_BLOCK
            ]


def gradient(half, part, shifted, qk_ref, pooled_ref, out_ref):
    size = out_ref.shape[0]
    held = -(-size // 16) * 16
    product = lax.dot_general(
        pooled_ref[part * COLS : (part + 1) * COLS, :], shifted[...],
        (((1,), (1,)), ((), ())), preferred_element_type=jnp.float32,
    ).T
    conv = jnp.concatenate(
        [product[tap * held : tap * held + size, :] for tap in range(K1)], axis=1
    )
    proj = qk_ref[half][:, part * PC : (part + 1) * PC]
    if out_ref.dtype == jnp.int16:
        encode((conv, proj), out_ref)
    else:
        out_ref[:, : K1 * COLS] = conv
        out_ref[:, K1 * COLS :] = proj


def first_kernel(
    n, emb_ref, proj_ref, slope_ref, pooled_ref, send_ref, give_ref, stay_ref, qk_ref, dconv_ref
):
    co, rows = slope_ref.shape
    size, held = co // 2, dconv_ref.shape[1]
    npos = rows // BIN_ROWS
    own_pos = npos // n
    scale = PC**-0.5
    me = lax.axis_index("seq")
    both = jnp.dot(
        jnp.concatenate([emb_ref[jnp.bitwise_xor(me, slab)] for slab in range(n)], axis=1),
        proj_ref[...],
        preferred_element_type=jnp.float32,
    )
    query, keys = both[:, :PC], both[:, PC:]
    pieces = []
    for slab in range(n):
        block = emb_ref[jnp.bitwise_xor(me, slab)].astype(jnp.float32)
        total = block[:own_pos]
        for part in range(1, 3):
            total = total + block[part * own_pos : (part + 1) * own_pos]
        pieces.append(total)
    grad = jnp.concatenate(pieces, axis=0)[:, co : co + npos]
    dquery = jnp.dot(grad, keys, precision=HIGH, preferred_element_type=jnp.float32) * scale
    dkeys = (
        lax.dot_general(
            grad, query, (((0,), (0,)), ((), ())), precision=HIGH,
            preferred_element_type=jnp.float32,
        )
        * scale
    )
    cotangent = jnp.concatenate([dquery, dkeys], axis=1)
    own = pl.ds(pl.multiple_of(me * SLOT, SLOT), SLOT)
    dembed = lax.dot_general(
        proj_ref[own, :].astype(jnp.float32), cotangent,
        (((1,), (1,)), ((), ())), precision=HIGH, preferred_element_type=jnp.float32,
    ) * (0.5 / BIN_ROWS)
    qk = lax.dot_general(
        emb_ref[0].astype(jnp.float32), cotangent, (((0,), (0,)), ((), ())),
        precision=HIGH, preferred_element_type=jnp.float32,
    )
    edge = jnp.zeros((held, PAD), jnp.bfloat16)
    for half in range(2):
        channels = slice(half * size, (half + 1) * size)
        qk_ref[half] = qk[channels]
        dconv_ref[half, :, :PAD] = edge
        dconv_ref[half, :, PAD + rows :] = edge
        for pos in range(npos):
            part = slope_ref[channels, pos * BIN_ROWS : (pos + 1) * BIN_ROWS] * dembed[
                channels, pos : pos + 1
            ]
            if held > size:
                part = jnp.concatenate(
                    [part, jnp.zeros((held - size, BIN_ROWS), jnp.float32)], axis=0
                )
            dconv_ref[half, :, PAD + pos * BIN_ROWS : PAD + (pos + 1) * BIN_ROWS] = part.astype(
                jnp.bfloat16
            )
    core = lax.axis_index("dp") % 2
    build_shifted(1 - core, dconv_ref, give_ref)
    gradient(1 - core, 0, give_ref, qk_ref, pooled_ref, send_ref)
    build_shifted(core, dconv_ref, stay_ref)


def middle_kernel(give_ref, stay_ref, qk_ref, pooled_ref, keep_ref, send_ref):
    core = lax.axis_index("dp") % 2
    gradient(core, 0, stay_ref, qk_ref, pooled_ref, keep_ref)
    gradient(1 - core, 1, give_ref, qk_ref, pooled_ref, send_ref)


def last_kernel(stay_ref, qk_ref, pooled_ref, after_ref, keep_ref):
    gradient(lax.axis_index("dp") % 2, 1, stay_ref, qk_ref, pooled_ref, keep_ref)


def first_part(n, embed, proj, slope, pooled):
    co, rows = slope.shape
    size = co // 2
    held = -(-size // 16) * 16
    return pl.pallas_call(
        functools.partial(first_kernel, n),
        out_shape=[
            jax.ShapeDtypeStruct((size, CODED), jnp.int16),
            jax.ShapeDtypeStruct((256, rows), jnp.bfloat16),
            jax.ShapeDtypeStruct((256, rows), jnp.bfloat16),
            jax.ShapeDtypeStruct((2, size, 2 * PC), jnp.float32),
        ],
        scratch_shapes=[pltpu.VMEM((2, held, rows + 2 * PAD), jnp.bfloat16)],
        compiler_params=params(28),
        name="first_part",
    )(embed, proj, slope, pooled)


def gradient_cost(size, rows, count):
    return pl.CostEstimate(
        flops=2 * 256 * COLS * rows * count, bytes_accessed=6 * MIB * count, transcendentals=0
    )


def middle_part(give, stay, qk, pooled):
    size, rows = qk.shape[1], pooled.shape[1]
    return pl.pallas_call(
        middle_kernel,
        out_shape=[
            jax.ShapeDtypeStruct((size, WIDE), jnp.float32),
            jax.ShapeDtypeStruct((size, CODED), jnp.int16),
        ],
        compiler_params=params(28),
        cost_estimate=gradient_cost(size, rows, 2),
        name="middle_part",
    )(give, stay, qk, pooled)


def last_part(stay, qk, pooled, after):
    size, rows = qk.shape[1], pooled.shape[1]
    return pl.pallas_call(
        last_kernel,
        out_shape=jax.ShapeDtypeStruct((size, WIDE), jnp.float32),
        compiler_params=params(28),
        in_specs=[pl.BlockSpec(memory_space=pltpu.VMEM)] * 3 + [pl.BlockSpec(memory_space=pl.ANY)],
        cost_estimate=gradient_cost(size, rows, 1),
        name="last_part",
    )(stay, qk, pooled, after)


def add_kernel(a_ref, b_ref, after_ref, out_ref):
    if a_ref.dtype == jnp.int16:
        a = decode(a_ref)
    else:
        a = [a_ref[:, begin:end] for begin, end in PARTS]
    encode([x + y for x, y in zip(a, decode(b_ref))], out_ref)


def add_half(a, b, after=None):
    return pl.pallas_call(
        add_kernel,
        out_shape=jax.ShapeDtypeStruct(b.shape, jnp.int16),
        in_specs=[pl.BlockSpec(memory_space=pltpu.VMEM)] * 2 + [pl.BlockSpec(memory_space=pl.ANY)],
        compiler_params=params(8),
        name="add_half",
    )(a, b, a if after is None else after)


def join_kernel(*refs):
    conv_ref, query_ref, key_ref = refs[4:]
    size = refs[0].shape[0]
    core = lax.axis_index("dp") % 2
    for part, out_ref in ((0, query_ref), (1, key_ref)):
        for half, ref in ((core, refs[2 * part]), (1 - core, refs[2 * part + 1])):
            rows = pl.ds(pl.multiple_of(half * size, 8), size)
            conv, proj = decode(ref)
            for tap in range(K1):
                first = tap * C0 + part * COLS
                conv_ref[rows, first : first + COLS] = conv[:, tap * COLS : (tap + 1) * COLS]
            out_ref[rows, :] = proj


def join(*halves):
    co = 2 * halves[0].shape[0]
    return pl.pallas_call(
        join_kernel,
        out_shape=[
            jax.ShapeDtypeStruct((co, K1 * C0), jnp.float32),
            jax.ShapeDtypeStruct((co, PC), jnp.float32),
            jax.ShapeDtypeStruct((co, PC), jnp.float32),
        ],
        compiler_params=params(8),
        name="join",
    )(*halves)


def body(bases, stem_table, conv_weight, query_weight, key_weight, pair_grad):
    n = lax.axis_size("seq")
    payload = gather_xor(regroup(bases), "seq")

    first_table = jnp.pad(
        stem_table.transpose(2, 1, 0), ((0, 0), (0, 0), (1, WINDOW - 1 - K0))
    ).reshape(C0, 4 * WINDOW)
    first_table = jnp.pad(first_table, ((0, 0), (0, 128 - 4 * WINDOW))).astype(jnp.float32)
    table, weights, proj = prepare(
        n,
        first_table,
        conv_weight * jnp.bfloat16(0.5),
        jnp.concatenate([query_weight, key_weight], axis=1),
    )

    pooled, slope, embed = stem_and_conv(n, payload, table, weights, pair_grad[0])
    embed_all = gather_xor(embed, "seq")
    send_a, give, stay, qk = first_part(n, embed_all, proj, slope, pooled)
    keep_a, send_b = middle_part(give, stay, qk, pooled)
    mine_a = add_half(keep_a, swap(send_a, "dp", 1))
    mine_b = add_half(last_part(stay, qk, pooled, mine_a), swap(send_b, "dp", 1))
    bit = 2
    while bit < lax.axis_size("dp"):
        other_b = swap(mine_b, "dp", bit)
        mine_a = add_half(mine_a, swap(mine_a, "dp", bit))
        mine_b = add_half(mine_b, other_b, mine_a)
        bit *= 2
    return tuple(join(mine_a, swap(mine_a, "dp", 1), mine_b, swap(mine_b, "dp", 1)))


def solution(mesh):
    return jax.shard_map(
        body,
        mesh=mesh,
        in_specs=(P("dp", "seq"), P(), P("seq", None), P(), P(), P("dp", "seq", None)),
        out_specs=(P("seq", None), P("seq", None), P("seq", None)),
        check_vma=False,
    )
```

```python
import functools

import jax
import jax.numpy as jnp
from jax import lax
from jax.experimental import pallas as pl
from jax.experimental.pallas import tpu as pltpu
from jax.sharding import PartitionSpec as P

C0 = 768
C1 = 768
PC = 128
K0 = 15
K1 = 5
POOL = 8
BIN_ROWS = 256
WINDOW = 24
CHUNK = 16
BLOCK = 512
SHIFT_BLOCK = 512
LAG = 3
PAD = 128
SLOT = 128

ROOT = 0.7978845608028654
CUBE = 0.044715
HIGH = lax.Precision.HIGHEST
MIB = 1024 * 1024


def params(mib):
    return pltpu.CompilerParams(vmem_limit_bytes=mib * MIB)


def swap(x, axis, bit):
    size = lax.axis_size(axis)
    return lax.ppermute(x, axis, [(i, i ^ bit) for i in range(size)])


def gather_xor(x, axis):
    x = x[None]
    bit = 1
    while bit < lax.axis_size(axis):
        x = jnp.concatenate([x, swap(x, axis, bit)], axis=0)
        bit *= 2
    return x


def twice_gelu(v):
    return v + v * jnp.tanh(v * (ROOT + (ROOT * CUBE) * (v * v)))


def regroup_kernel(bases_ref, out_ref):
    lines, width = bases_ref.shape
    per = width // POOL
    rows = lines * per
    line = lax.broadcasted_iota(jnp.int32, (lines, rows), 0)
    column = lax.broadcasted_iota(jnp.int32, (lines, rows), 1)
    spread = lax.dot_general(
        bases_ref[...].astype(jnp.float32).astype(jnp.bfloat16),
        (column // per == line).astype(jnp.float32).astype(jnp.bfloat16),
        (((0,), (0,)), ((), ())),
        preferred_element_type=jnp.float32,
    )
    place = lax.broadcasted_iota(jnp.int32, (width, rows), 0) // POOL
    column = lax.broadcasted_iota(jnp.int32, (width, rows), 1)
    spread = jnp.where(place == column % per, spread, 0.0)
    grouped = spread[:POOL]
    for i in range(1, per):
        grouped = grouped + spread[i * POOL : (i + 1) * POOL]
    out_ref[...] = jnp.concatenate(
        [grouped[:, : rows // 2], grouped[:, rows // 2 :]], axis=0
    ).astype(jnp.bfloat16)


def regroup(bases):
    rows = bases.shape[1] // POOL
    return pl.pallas_call(
        regroup_kernel,
        out_shape=jax.ShapeDtypeStruct((2 * POOL, rows // 2), jnp.bfloat16),
        compiler_params=params(4),
        name="regroup",
    )(bases.reshape(bases.shape[1] // 128, 128))


def prepare_kernel(n, co, t0_ref, w_ref, both_ref, table_ref, weights_ref, proj_ref):
    for chunk in range(C0 // CHUNK):
        part = t0_ref[chunk * CHUNK : (chunk + 1) * CHUNK, :]
        for pos in range(POOL):
            shifted = part if pos == 0 else pltpu.roll(part, pos, 1)
            first = (chunk * POOL + pos) * CHUNK
            table_ref[first : first + CHUNK, :] = shifted.astype(jnp.bfloat16)
    for tap in range(K1):
        weights_ref[tap * co : (tap + 1) * co, :] = w_ref[:, tap * C0 : (tap + 1) * C0] * 0.5
    for slot in range(n):
        rows = slice(slot * co, (slot + 1) * co)
        proj_ref[slot * SLOT : slot * SLOT + co, :] = both_ref[rows, :]
        proj_ref[slot * SLOT + co : (slot + 1) * SLOT, :] = jnp.zeros(
            (SLOT - co, 2 * PC), jnp.bfloat16
        )


def prepare(n, first_table, conv_weight, both):
    co = conv_weight.shape[0]
    return pl.pallas_call(
        functools.partial(prepare_kernel, n, co),
        out_shape=[
            jax.ShapeDtypeStruct((POOL * C0, 128), jnp.bfloat16),
            jax.ShapeDtypeStruct((K1 * co, C0), jnp.bfloat16),
            jax.ShapeDtypeStruct((n * SLOT, 2 * PC), jnp.bfloat16),
        ],
        compiler_params=params(8),
        cost_estimate=pl.CostEstimate(flops=0, bytes_accessed=5 * MIB, transcendentals=0),
        name="prepare",
    )(first_table, conv_weight, both)


def stem_kernel(
    n, rows_dev, co, pay_ref, table, weights, grad_ref, p_ref, slope_ref, emb_ref,
    bases, ybuf, sums
):
    rows = n * rows_dev
    blocks = rows // BLOCK
    front = LAG * BLOCK + PAD

    def convolve(block):
        first = pl.multiple_of((block + LAG) * BLOCK, 128)
        conv = None
        for tap in range(K1):
            near = ybuf[tap * co : (tap + 1) * co, pl.ds(first, BLOCK + 2 * PAD)]
            begin = PAD + tap - K1 // 2
            part = near[:, begin : begin + BLOCK]
            conv = part if conv is None else conv + part
        square = conv * conv
        tangent = jnp.tanh(conv * (ROOT + (ROOT * CUBE) * square))
        half = 0.5 * conv
        gelu = half + half * tangent
        to = pl.multiple_of(jnp.maximum(block, 0) * BLOCK, 128)
        slope_ref[:, pl.ds(to, BLOCK)] = (0.5 + 0.5 * tangent) + half * (1.0 - tangent * tangent) * (
            ROOT + (3.0 * ROOT * CUBE) * square
        )
        lane = lax.broadcasted_iota(jnp.int32, (co, 128), 1)
        total = sums[:co, :]
        for part in range(BLOCK // BIN_ROWS):
            mean = jnp.sum(
                gelu[:, part * BIN_ROWS : (part + 1) * BIN_ROWS], axis=1, keepdims=True
            ) * (1.0 / BIN_ROWS)
            total = jnp.where(lane == block * (BLOCK // BIN_ROWS) + part, mean, total)
        sums[:co, :] = total

    def taps(block):
        ybuf[:, pl.ds(pl.multiple_of(front + block * BLOCK, 128), BLOCK)] = jnp.dot(
            weights[...],
            p_ref[:, pl.ds(pl.multiple_of(jnp.maximum(block, 0) * BLOCK, 128), BLOCK)],
            preferred_element_type=jnp.float32,
        )

    me = lax.axis_index("seq")
    bases[:, :PAD] = jnp.full((POOL, PAD), -1.0, jnp.float32)
    bases[:, PAD + rows :] = jnp.full((POOL, PAD), -1.0, jnp.float32)
    half = rows_dev // 2
    for slab in range(n):
        block = pay_ref[jnp.bitwise_xor(me, slab)].astype(jnp.float32)
        first = PAD + slab * rows_dev
        bases[:, first : first + half] = block[:POOL]
        bases[:, first + half : first + 2 * half] = block[POOL:]
    ybuf[:, front + rows :] = jnp.zeros((K1 * co, PAD), jnp.float32)
    p_ref[:, :BLOCK] = jnp.zeros((C0, BLOCK), jnp.bfloat16)
    sums[...] = jnp.zeros(sums.shape, jnp.float32)

    def main(step, carry):
        first = pl.multiple_of(step * BLOCK, 128)
        near = bases[:, pl.ds(first, BLOCK + 2 * PAD)]
        window = jnp.concatenate(
            [near[:, PAD + q : PAD + q + BLOCK] for q in (-1, 0, 1)], axis=0
        )
        onehot = jnp.concatenate(
            [(window == b).astype(jnp.float32) for b in range(4)]
            + [jnp.zeros((128 - 4 * WINDOW, BLOCK), jnp.float32)],
            axis=0,
        ).astype(jnp.bfloat16)
        convolve(step - LAG)
        taps(step - 1)
        for at in range(0, BLOCK, 256):
            for chunk in range(C0 // CHUNK):
                stem = jnp.dot(
                    table[chunk * POOL * CHUNK : (chunk + 1) * POOL * CHUNK, :],
                    onehot[:, at : at + 256],
                    preferred_element_type=jnp.float32,
                )
                most = least = stem[:CHUNK]
                for pos in range(1, POOL):
                    part = stem[pos * CHUNK : (pos + 1) * CHUNK]
                    most = jnp.maximum(most, part)
                    least = jnp.minimum(least, part)
                p_ref[
                    chunk * CHUNK : (chunk + 1) * CHUNK, pl.ds(pl.multiple_of(first + at, 128), 256)
                ] = jnp.maximum(twice_gelu(most), twice_gelu(least)).astype(jnp.bfloat16)
        return carry

    lax.fori_loop(0, blocks, main, 0)
    taps(blocks - 1)
    for last in range(LAG):
        convolve(blocks - LAG + last)

    own_pos, npos = grad_ref.shape
    embed = sums[...].T[:npos, :].astype(jnp.bfloat16).astype(jnp.float32)
    rest = grad_ref[...]
    parts = []
    for _ in range(3):
        part = rest.astype(jnp.bfloat16).astype(jnp.float32)
        parts.append(part)
        rest = rest - part
    grads = jnp.concatenate(
        parts + [jnp.zeros((npos - 3 * own_pos, npos), jnp.float32)], axis=0
    )
    emb_ref[...] = jnp.concatenate(
        [embed[:, :co], grads, jnp.zeros((npos, SLOT - co - npos), jnp.float32)], axis=1
    ).astype(jnp.bfloat16)


def stem_and_conv(n, payload, table, weights, pair_grad):
    co = weights.shape[0] // K1
    rows_dev = payload.shape[2] * 2
    rows = n * rows_dev
    npos = rows // BIN_ROWS
    return pl.pallas_call(
        functools.partial(stem_kernel, n, rows_dev, co),
        out_shape=[
            jax.ShapeDtypeStruct((C0, rows), jnp.bfloat16),
            jax.ShapeDtypeStruct((co, rows), jnp.float32),
            jax.ShapeDtypeStruct((npos, SLOT), jnp.bfloat16),
        ],
        scratch_shapes=[
            pltpu.VMEM((POOL, rows + 2 * PAD), jnp.float32),
            pltpu.VMEM((K1 * co, LAG * BLOCK + rows + 2 * PAD), jnp.float32),
            pltpu.VMEM((128, 128), jnp.float32),
        ],
        compiler_params=params(36),
        name="stem_and_conv",
    )(payload, table, weights, pair_grad)


COLS = C0 // 2
PARTS = ((0, K1 * COLS), (K1 * COLS, K1 * COLS + PC))
WIDE = K1 * COLS + PC
CODED = WIDE + 128


def encode(values, out_ref):
    exponents = []
    for (begin, end), x in zip(PARTS, values):
        top = jnp.maximum(jnp.max(jnp.abs(x), axis=1, keepdims=True), 1e-30)
        exponent = jnp.floor(jnp.log2(32000.0 / top))
        scaled = jnp.floor(x * jnp.exp2(exponent) + 0.5)
        out_ref[:, begin:end] = scaled.astype(jnp.int32).astype(jnp.int16)
        exponents.append(exponent)
    lane = lax.broadcasted_iota(jnp.int32, (out_ref.shape[0], 128), 1)
    packed = jnp.where(lane == 0, exponents[0], exponents[1])
    out_ref[:, WIDE:] = packed.astype(jnp.int32).astype(jnp.int16)


def decode(ref):
    exponents = ref[:, WIDE:].astype(jnp.int32).astype(jnp.float32)
    return [
        ref[:, begin:end].astype(jnp.int32).astype(jnp.float32) * jnp.exp2(-exponents[:, at : at + 1])
        for at, (begin, end) in enumerate(PARTS)
    ]


def build_shifted(half, dconv, shifted):
    held = dconv.shape[1]
    rows = shifted.shape[1]
    shifted[K1 * held :, :] = jnp.zeros((shifted.shape[0] - K1 * held, rows), jnp.bfloat16)
    for first in range(0, rows, SHIFT_BLOCK):
        near = dconv[half, :, first : first + SHIFT_BLOCK + 2 * PAD]
        for tap in range(K1):
            begin = PAD - tap + K1 // 2
            shifted[tap * held : (tap + 1) * held, first : first + SHIFT_BLOCK] = near[
                :, begin : begin + SHIFT_BLOCK
            ]


def gradient(half, part, shifted, qk_ref, pooled_ref, out_ref):
    size = out_ref.shape[0]
    held = -(-size // 16) * 16
    product = lax.dot_general(
        pooled_ref[part * COLS : (part + 1) * COLS, :], shifted[...],
        (((1,), (1,)), ((), ())), preferred_element_type=jnp.float32,
    ).T
    conv = jnp.concatenate(
        [product[tap * held : tap * held + size, :] for tap in range(K1)], axis=1
    )
    proj = qk_ref[half][:, part * PC : (part + 1) * PC]
    if out_ref.dtype == jnp.int16:
        encode((conv, proj), out_ref)
    else:
        out_ref[:, : K1 * COLS] = conv
        out_ref[:, K1 * COLS :] = proj


def first_kernel(
    n, emb_ref, proj_ref, slope_ref, pooled_ref, send_ref, give_ref, stay_ref, qk_ref, dconv_ref
):
    co, rows = slope_ref.shape
    size, held = co // 2, dconv_ref.shape[1]
    npos = rows // BIN_ROWS
    own_pos = npos // n
    scale = PC**-0.5
    me = lax.axis_index("seq")
    both = jnp.dot(
        jnp.concatenate([emb_ref[jnp.bitwise_xor(me, slab)] for slab in range(n)], axis=1),
        proj_ref[...],
        preferred_element_type=jnp.float32,
    )
    query, keys = both[:, :PC], both[:, PC:]
    pieces = []
    for slab in range(n):
        block = emb_ref[jnp.bitwise_xor(me, slab)].astype(jnp.float32)
        total = block[:own_pos]
        for part in range(1, 3):
            total = total + block[part * own_pos : (part + 1) * own_pos]
        pieces.append(total)
    grad = jnp.concatenate(pieces, axis=0)[:, co : co + npos]
    dquery = jnp.dot(grad, keys, precision=HIGH, preferred_element_type=jnp.float32) * scale
    dkeys = (
        lax.dot_general(
            grad, query, (((0,), (0,)), ((), ())), precision=HIGH,
            preferred_element_type=jnp.float32,
        )
        * scale
    )
    cotangent = jnp.concatenate([dquery, dkeys], axis=1)
    own = pl.ds(pl.multiple_of(me * SLOT, SLOT), SLOT)
    dembed = lax.dot_general(
        proj_ref[own, :].astype(jnp.float32), cotangent,
        (((1,), (1,)), ((), ())), precision=HIGH, preferred_element_type=jnp.float32,
    ) * (0.5 / BIN_ROWS)
    qk = lax.dot_general(
        emb_ref[0].astype(jnp.float32), cotangent, (((0,), (0,)), ((), ())),
        precision=HIGH, preferred_element_type=jnp.float32,
    )
    edge = jnp.zeros((held, PAD), jnp.bfloat16)
    for half in range(2):
        channels = slice(half * size, (half + 1) * size)
        qk_ref[half] = qk[channels]
        dconv_ref[half, :, :PAD] = edge
        dconv_ref[half, :, PAD + rows :] = edge
        for pos in range(npos):
            part = slope_ref[channels, pos * BIN_ROWS : (pos + 1) * BIN_ROWS] * dembed[
                channels, pos : pos + 1
            ]
            if held > size:
                part = jnp.concatenate(
                    [part, jnp.zeros((held - size, BIN_ROWS), jnp.float32)], axis=0
                )
            dconv_ref[half, :, PAD + pos * BIN_ROWS : PAD + (pos + 1) * BIN_ROWS] = part.astype(
                jnp.bfloat16
            )
    core = lax.axis_index("dp") % 2
    build_shifted(1 - core, dconv_ref, give_ref)
    gradient(1 - core, 0, give_ref, qk_ref, pooled_ref, send_ref)
    build_shifted(core, dconv_ref, stay_ref)


def middle_kernel(give_ref, stay_ref, qk_ref, pooled_ref, keep_ref, send_ref):
    core = lax.axis_index("dp") % 2
    gradient(core, 0, stay_ref, qk_ref, pooled_ref, keep_ref)
    gradient(1 - core, 1, give_ref, qk_ref, pooled_ref, send_ref)


def last_kernel(stay_ref, qk_ref, pooled_ref, after_ref, keep_ref):
    gradient(lax.axis_index("dp") % 2, 1, stay_ref, qk_ref, pooled_ref, keep_ref)


def first_part(n, embed, proj, slope, pooled):
    co, rows = slope.shape
    size = co // 2
    held = -(-size // 16) * 16
    return pl.pallas_call(
        functools.partial(first_kernel, n),
        out_shape=[
            jax.ShapeDtypeStruct((size, CODED), jnp.int16),
            jax.ShapeDtypeStruct((256, rows), jnp.bfloat16),
            jax.ShapeDtypeStruct((256, rows), jnp.bfloat16),
            jax.ShapeDtypeStruct((2, size, 2 * PC), jnp.float32),
        ],
        scratch_shapes=[pltpu.VMEM((2, held, rows + 2 * PAD), jnp.bfloat16)],
        compiler_params=params(28),
        name="first_part",
    )(embed, proj, slope, pooled)


def gradient_cost(size, rows, count):
    return pl.CostEstimate(
        flops=2 * 256 * COLS * rows * count, bytes_accessed=6 * MIB * count, transcendentals=0
    )


def middle_part(give, stay, qk, pooled):
    size, rows = qk.shape[1], pooled.shape[1]
    return pl.pallas_call(
        middle_kernel,
        out_shape=[
            jax.ShapeDtypeStruct((size, WIDE), jnp.float32),
            jax.ShapeDtypeStruct((size, CODED), jnp.int16),
        ],
        compiler_params=params(28),
        cost_estimate=gradient_cost(size, rows, 2),
        name="middle_part",
    )(give, stay, qk, pooled)


def last_part(stay, qk, pooled, after):
    size, rows = qk.shape[1], pooled.shape[1]
    return pl.pallas_call(
        last_kernel,
        out_shape=jax.ShapeDtypeStruct((size, WIDE), jnp.float32),
        compiler_params=params(28),
        in_specs=[pl.BlockSpec(memory_space=pltpu.VMEM)] * 3 + [pl.BlockSpec(memory_space=pl.ANY)],
        cost_estimate=gradient_cost(size, rows, 1),
        name="last_part",
    )(stay, qk, pooled, after)


def add_kernel(a_ref, b_ref, after_ref, out_ref):
    if a_ref.dtype == jnp.int16:
        a = decode(a_ref)
    else:
        a = [a_ref[:, begin:end] for begin, end in PARTS]
    encode([x + y for x, y in zip(a, decode(b_ref))], out_ref)


def add_half(a, b, after=None):
    return pl.pallas_call(
        add_kernel,
        out_shape=jax.ShapeDtypeStruct(b.shape, jnp.int16),
        in_specs=[pl.BlockSpec(memory_space=pltpu.VMEM)] * 2 + [pl.BlockSpec(memory_space=pl.ANY)],
        compiler_params=params(8),
        name="add_half",
    )(a, b, a if after is None else after)


def join_kernel(*refs):
    conv_ref, query_ref, key_ref = refs[4:]
    size = refs[0].shape[0]
    core = lax.axis_index("dp") % 2
    for part, out_ref in ((0, query_ref), (1, key_ref)):
        for half, ref in ((core, refs[2 * part]), (1 - core, refs[2 * part + 1])):
            rows = pl.ds(pl.multiple_of(half * size, 8), size)
            conv, proj = decode(ref)
            for tap in range(K1):
                first = tap * C0 + part * COLS
                conv_ref[rows, first : first + COLS] = conv[:, tap * COLS : (tap + 1) * COLS]
            out_ref[rows, :] = proj


def join(*halves):
    co = 2 * halves[0].shape[0]
    return pl.pallas_call(
        join_kernel,
        out_shape=[
            jax.ShapeDtypeStruct((co, K1 * C0), jnp.float32),
            jax.ShapeDtypeStruct((co, PC), jnp.float32),
            jax.ShapeDtypeStruct((co, PC), jnp.float32),
        ],
        compiler_params=params(8),
        name="join",
    )(*halves)


def body(bases, stem_table, conv_weight, query_weight, key_weight, pair_grad):
    n = lax.axis_size("seq")
    payload = gather_xor(regroup(bases), "seq")

    first_table = jnp.pad(
        stem_table.transpose(2, 1, 0), ((0, 0), (0, 0), (1, WINDOW - 1 - K0))
    ).reshape(C0, 4 * WINDOW)
    first_table = jnp.pad(first_table, ((0, 0), (0, 128 - 4 * WINDOW))).astype(jnp.float32)
    table, weights, proj = prepare(
        n,
        first_table,
        conv_weight,
        jnp.concatenate([query_weight, key_weight], axis=1),
    )

    pooled, slope, embed = stem_and_conv(n, payload, table, weights, pair_grad[0])
    embed_all = gather_xor(embed, "seq")
    send_a, give, stay, qk = first_part(n, embed_all, proj, slope, pooled)
    keep_a, send_b = middle_part(give, stay, qk, pooled)
    mine_a = add_half(keep_a, swap(send_a, "dp", 1))
    mine_b = add_half(last_part(stay, qk, pooled, mine_a), swap(send_b, "dp", 1))
    bit = 2
    while bit < lax.axis_size("dp"):
        other_b = swap(mine_b, "dp", bit)
        mine_a = add_half(mine_a, swap(mine_a, "dp", bit))
        mine_b = add_half(mine_b, other_b, mine_a)
        bit *= 2
    return tuple(join(mine_a, swap(mine_a, "dp", 1), mine_b, swap(mine_b, "dp", 1)))


def solution(mesh):
    return jax.shard_map(
        body,
        mesh=mesh,
        in_specs=(P("dp", "seq"), P(), P("seq", None), P(), P(), P("dp", "seq", None)),
        out_specs=(P("seq", None), P("seq", None), P("seq", None)),
        check_vma=False,
    )
```
